32 devices in a mesh: rep: 4 (over y, x), ep: 8 (over z, core).
Axes of the slice: x: 2, y: 2, z: 4, core: 2. Of those that a mesh axis runs over, the one named last changes fastest.
Arguments:
- tokens: bfloat16 [8192, 768], P(('rep', 'ep')), may hold values from -6 to 6
- segment_ids: int32 [4, 2048], P('rep', 'ep'), may hold values from 0 to 3, never falling along the last dimension, each value on 1 to 1024 neighbouring positions
- routes: int32 [8192, 2], P(('rep', 'ep')), may hold values from 0 to 7, all different within a row; in each aligned block of 256 rows (0 to 255, 256 to 511, ...) at most 128 rows name the same one
- norm1_gain: bfloat16 [768], P(('rep', 'ep')), may hold values from 0.5 to 1.5
- w_query: bfloat16 [768, 768], P(('rep', 'ep')), may hold values from -0.3125 to 0.3125
- w_key: bfloat16 [768, 768], P(('rep', 'ep')), may hold values from -0.3125 to 0.3125
- w_value: bfloat16 [768, 768], P(('rep', 'ep')), may hold values from -0.21875 to 0.21875
- w_out: bfloat16 [768, 768], P(('rep', 'ep')), may hold values from -1.25 to 1.25
- norm2_gain: bfloat16 [768], P(('rep', 'ep')), may hold values from 0.5 to 1.5
- w_router: bfloat16 [768, 8], P(('rep', 'ep')), may hold values from -0.15625 to 0.15625
- shared_gate: bfloat16 [768, 2048], P(('rep', 'ep')), may hold values from -0.21875 to 0.21875
- shared_up: bfloat16 [768, 2048], P(('rep', 'ep')), may hold values from -0.21875 to 0.21875
- shared_down: bfloat16 [2048, 768], P(('rep', 'ep')), may hold values from -0.1875 to 0.1875
- expert_gate: bfloat16 [8, 768, 2048], P('ep'), may hold values from -0.21875 to 0.21875
- expert_up: bfloat16 [8, 768, 2048], P('ep'), may hold values from -0.21875 to 0.21875
- expert_down: bfloat16 [8, 2048, 768], P('ep'), may hold values from -1.5 to 1.5
- out_grad: bfloat16 [8192, 768], P(('rep', 'ep')), may hold values from -6 to 6
Outputs:
- layer_out: bfloat16 [8192, 768], P(('rep', 'ep'))
- tokens_grad: float32 [8192, 768], P(('rep', 'ep'))
- norm1_gain_grad: float32 [768], P(('rep', 'ep'))
- w_query_grad: float32 [768, 768], P(('rep', 'ep'))
- w_key_grad: float32 [768, 768], P(('rep', 'ep'))
- w_value_grad: float32 [768, 768], P(('rep', 'ep'))
- w_out_grad: float32 [768, 768], P(('rep', 'ep'))
- norm2_gain_grad: float32 [768], P(('rep', 'ep'))
- w_router_grad: float32 [768, 8], P(('rep', 'ep'))
- shared_gate_grad: float32 [768, 2048], P(('rep', 'ep'))
- shared_up_grad: float32 [768, 2048], P(('rep', 'ep'))
- shared_down_grad: float32 [2048, 768], P(('rep', 'ep'))
- expert_gate_grad: float32 [8, 768, 2048], P('ep', None, 'rep')
- expert_up_grad: float32 [8, 768, 2048], P('ep', None, 'rep')
- expert_down_grad: float32 [8, 2048, 768], P('ep', None, 'rep')
The draws below stay inside these ranges and needn't reach their ends.
Inputs may be any that keep to these rules, and one draw needn't show every extreme that they name: `segment_ids`: along each pack of 2048 places the document number never falls; every document has 1 to 1024 places, and one has exactly 1024. `routes`: each token names 2 different experts. Among the 256 tokens of one device no expert is named more than 128 times, and in some device's tokens one expert is named exactly 128 times.
All inputs are finite; a program needn't handle non-finite values.
Results may differ from the reference program's by a relative error of at most 0.03.
Values may be sent and summed in bfloat16 or wider, within the bound.
No kernel may reach another device: no remote copies, remote signals or barrier semaphores. Data moves between devices by JAX's collectives and lax.ppermute only.
A program may use at most 256 MiB of HBM per device.

```python
import math
import jax
import jax.numpy as jnp
import numpy as np
from jax import lax

D = 768
HEADS = 12
HEAD_DIM = 64
FF = 2048
TOPK = 2
BLOCK = 256
TOK_DEV = 256
EXPERTS = 8
ROW_LEN = 2048
SEQ_MAX = 1024
DOCS = 4
CAP = 128
PACKS = 4
TOKENS = 8192
N_REP = 4
N_EP = 8


def raised(values, rng, source, target, parts, factor):
    owner, partner = [(jnp.arange(values.shape[dim]) // (values.shape[dim] // parts)).reshape([-1 if axis == dim else 1 for axis in range(values.ndim)]) for dim in (source, target)]
    chosen = jax.random.permutation(rng, parts)[partner]
    strong = (owner == chosen) | (owner == (partner + parts // 2) % parts)
    return jnp.where(strong, factor * values, values)


def levels(key, dims, shards, smallest, top_value):
    level = 1.0
    for dim, blocks in shards:
        draws = jax.random.uniform(jax.random.fold_in(jax.random.fold_in(key, 6), dim), (blocks,), jnp.float32, smallest / len(shards), top_value / len(shards))
        level = level * jnp.repeat(jnp.exp(draws), dims[dim] // blocks).reshape((-1,) + (1,) * (len(dims) - 1 - dim))
    return level


def length_profile(count, total, limit, slope):
    loads = [(1 << 20) // math.isqrt(standing ** slope) + 1 for standing in range(2, count + 1)]
    rest, given = total - limit - (count - 1), [1] * (count - 1)
    while rest > 0:
        free = [i for i in range(count - 1) if given[i] < limit]
        whole, remaining = sum([loads[i] for i in free]), rest
        for i in free:
            extra = min(limit - given[i], max(1, remaining * loads[i] // whole), rest)
            given[i] = given[i] + extra
            rest = rest - extra
    return np.array([limit] + given)


def uneven_parts(rng, number_of, total, bound, slope):
    if number_of == 2:
        one = jax.random.randint(rng, (), max(1, total - bound), min(bound, total - 1) + 1)
        return jnp.stack([one, total - one])
    lengths = jnp.asarray(length_profile(number_of, total, bound, slope), jnp.int32)
    twos = (number_of - 1) // 2
    donor, taker = lengths[1:1 + 2 * twos:2], lengths[2:2 + 2 * twos:2]
    room = jnp.minimum(donor - 1, bound - taker)
    moved = jax.random.randint(jax.random.fold_in(rng, 1), (twos,), 0, 1 << 20) % (room + 1)
    lengths = lengths.at[1:1 + 2 * twos:2].set(donor - moved).at[2:2 + 2 * twos:2].set(taker + moved)
    return lengths[jax.random.permutation(jax.random.fold_in(rng, 2), number_of)]


def deal_out(key, own, number, rows, count, top, reach, skew):
    order = jax.random.permutation(key, count)
    heavy_load, usual = load_shares(count, rows * top, reach, skew, True), load_shares(count, rows * top, reach, skew, False)
    places = jnp.arange(count)

    def named(sizes, turn):
        used = int((sizes > 0).sum())
        fixed = max(1, used // 4)
        moved = fixed + (places - fixed + turn * (used - fixed)) % max(1, count - fixed)
        return jnp.zeros((count,), jnp.int32).at[order[jnp.where(places < fixed, places, moved)]].set(jnp.asarray(sizes, jnp.int32))

    sizes = jnp.where(number % 4 == 0, named(heavy_load, number // 4), named(usual, number - number // 4 - 1))
    mixed = jax.random.permutation(jax.random.fold_in(own, 3), count)
    source_of, sink = mixed[0:count // 2 * 2:2], mixed[1:count // 2 * 2:2]
    room = jnp.minimum(sizes[source_of] - 1, reach - sizes[sink]) // 2
    room = jnp.where((source_of == order[0]) | (sink == order[0]) | (sizes[sink] == 0), 0, jnp.maximum(room, 0))
    moved = jax.random.randint(jax.random.fold_in(own, 4), (count // 2,), 0, 1 << 20) % (room + 1)
    sizes = sizes.at[source_of].add(-moved).at[sink].add(moved)
    members = jnp.searchsorted(jnp.cumsum(sizes), jnp.arange(rows * top), side="right").astype(jnp.int32)
    grid = members.reshape(top, rows).T
    grid = grid[jax.random.permutation(jax.random.fold_in(own, 1), rows)]
    turn = jax.random.randint(jax.random.fold_in(own, 2), (rows, 1), 0, top)
    return jnp.take_along_axis(grid, (jnp.arange(top)[None, :] + turn) % top, axis=1)


def load_shares(count, total, most, slope, full):
    portions = [(1 << 20) // math.isqrt(grade ** slope) + 1 for grade in range(1, count + 1)]
    largest = most if full else min(most, max(-(-total // count), total * portions[0] // sum(portions)))
    least = 1 if total - largest >= count - 1 else 0
    holding, rest = [largest] + [least] * (count - 1), total - largest - least * (count - 1)
    while rest > 0:
        movable = [i for i in range(1, count) if holding[i] < largest] or [i for i in range(1, count) if holding[i] < most]
        pool, left = sum([portions[i] for i in movable]), rest
        for i in movable:
            more = min(most - holding[i], max(1, left * portions[i] // pool), rest)
            holding[i] = holding[i] + more
            rest = rest - more
    return np.array(holding)


def normal_values(stream_key, dims, deviation, bound, cuts=(), kind=jnp.bfloat16):
    values = deviation * jax.random.normal(stream_key, dims, jnp.float32)
    if cuts:
        values = values * levels(stream_key, dims, cuts, -0.22, 0.18)
    return jnp.clip(values, -bound, bound).astype(kind)


def heavy_noise(rng, shape, spread, limit, cuts, heavy, kind=jnp.bfloat16):
    values = spread * jax.random.normal(rng, shape, jnp.float32)
    if cuts:
        values = values * levels(rng, shape, cuts, -0.22, 0.18)
    return jnp.clip(raised(values, jax.random.fold_in(rng, 3), *heavy), -limit, limit).astype(kind)


def setup_inputs(seed: int = 0) -> dict:
    splits = jax.random.split(jax.random.key(seed), 18)
    tokens = normal_values(splits[0], (TOKENS, D), 1.0, 6.0, ((0, 32),))
    segment_ids = jax.vmap(lambda own: jnp.searchsorted(jnp.cumsum(uneven_parts(own, DOCS, ROW_LEN, SEQ_MAX, 1)), jnp.arange(ROW_LEN), side="right"))(jax.random.split(splits[1], PACKS)).reshape((PACKS, ROW_LEN)).astype(jnp.int32)
    routes_keys = jax.random.split(jax.random.fold_in(splits[2], 1), TOKENS // TOK_DEV)
    routes_turns = jax.random.permutation(jax.random.fold_in(splits[2], 3), TOKENS // TOK_DEV)
    routes = jax.vmap(lambda own, number: deal_out(jax.random.fold_in(splits[2], 2), own, number, TOK_DEV, EXPERTS, TOPK, CAP, 2))(routes_keys, routes_turns).reshape((TOKENS, TOPK))
    norm1_gain = jnp.clip(1.0 + 0.1 * jax.random.normal(splits[3], (D,), jnp.float32), 0.5, 1.5).astype(jnp.bfloat16)
    w_query = normal_values(splits[4], (D, D), (D // 2) ** -0.5, 0.3125, ((0, 32),))
    w_key = normal_values(splits[5], (D, D), (D // 2) ** -0.5, 0.3125, ((0, 32),))
    w_value = normal_values(splits[6], (D, D), D ** -0.5, 0.21875, ((0, 32),))
    w_out = normal_values(splits[7], (D, D), (D // 32) ** -0.5, 1.25, ((0, 32),))
    norm2_gain = jnp.clip(1.0 + 0.1 * jax.random.normal(splits[8], (D,), jnp.float32), 0.5, 1.5).astype(jnp.bfloat16)
    w_router = normal_values(splits[9], (D, EXPERTS), (2 * D) ** -0.5, 0.15625, ((0, 32),))
    shared_gate = normal_values(splits[10], (D, FF), D ** -0.5, 0.21875, ((0, 32),))
    shared_up = normal_values(splits[11], (D, FF), D ** -0.5, 0.21875, ((0, 32),))
    shared_down = normal_values(splits[12], (FF, D), (FF // 2) ** -0.5, 0.1875, ((0, 32),))
    expert_gate = normal_values(splits[13], (EXPERTS, D, FF), D ** -0.5, 0.21875, ((0, 8),))
    expert_up = normal_values(splits[14], (EXPERTS, D, FF), D ** -0.5, 0.21875, ((0, 8),))
    expert_down = normal_values(splits[15], (EXPERTS, FF, D), (FF // 128) ** -0.5, 1.5, ((0, 8),))
    out_grad = heavy_noise(splits[16], (TOKENS, D), 1.0, 6.0, ((0, 32),), (0, 1, 32, 2.75))
    return {"tokens": tokens, "segment_ids": segment_ids, "routes": routes, "norm1_gain": norm1_gain, "w_query": w_query, "w_key": w_key, "w_value": w_value, "w_out": w_out, "norm2_gain": norm2_gain, "w_router": w_router, "shared_gate": shared_gate, "shared_up": shared_up, "shared_down": shared_down, "expert_gate": expert_gate, "expert_up": expert_up, "expert_down": expert_down, "out_grad": out_grad}


@jax.custom_vjp
def low(v):
    return lax.optimization_barrier(v.astype(jnp.bfloat16)).astype(jnp.float32)

@jax.custom_vjp
def low_back(v):
    return v

def low_keep(v):
    return (low(v), None)

def low_pass(kept, grad):
    return (grad,)

def back_keep(v):
    return (v, None)

def back_low(kept, grad):
    return (low(grad),)
low.defvjp(low_keep, low_pass)
low_back.defvjp(back_keep, back_low)
EPSILON = 1e-06
NEG_LARGE = -1e+30
HIGHEST_MODE = lax.Precision.HIGHEST

def precise(former, latter):
    return jnp.dot(former, latter, precision=HIGHEST_MODE, preferred_element_type=jnp.float32)

def rms_scale(values):
    return lax.rsqrt(lax.optimization_barrier(jnp.mean(values * values, axis=1, keepdims=True)) + EPSILON)

def silu_value(values):
    return values * jax.nn.sigmoid(values)

def rotate(values, cosine_table, sine_table):
    halfway = values.shape[-1] // 2
    front_half = values[..., :halfway]
    back_half = values[..., halfway:]
    return jnp.concatenate([front_half * cosine_table - back_half * sine_table, back_half * cosine_table + front_half * sine_table], axis=-1)

def turn_tables(places, head_dim):
    halfway = head_dim // 2
    inverse = jnp.exp(jnp.arange(halfway).astype(jnp.float32) * (-2.0 * math.log(10000.0) / head_dim))
    turned = places.astype(jnp.float32)[:, None] * inverse[None, :]
    return (jnp.cos(turned)[:, None, :], jnp.sin(turned)[:, None, :])

def reference(tokens, segment_ids, routes, norm1_gain, w_query, w_key, w_value, w_out, norm2_gain, w_router, shared_gate, shared_up, shared_down, expert_gate, expert_up, expert_down, out_grad):
    choice_count = TOKENS * TOPK
    expert_room = CAP * N_REP * N_EP
    flat_routes = routes.reshape(choice_count).astype(jnp.int32)
    onehot = (flat_routes[:, None] == jnp.arange(EXPERTS, dtype=jnp.int32)[None, :]).astype(jnp.int32)
    own_rank = lax.optimization_barrier(jnp.sum((jnp.cumsum(onehot, axis=0) - 1) * onehot, axis=1)).astype(jnp.int32)
    slot_of_choice = (flat_routes * expert_room + own_rank).astype(jnp.int32)
    slot_source = jnp.full((EXPERTS * expert_room,), choice_count, jnp.int32).at[slot_of_choice].set(jnp.arange(choice_count, dtype=jnp.int32))
    slot_token_row = jnp.where(slot_source < choice_count, slot_source // TOPK, TOKENS).astype(jnp.int32).reshape(EXPERTS, expert_room)
    places = (jnp.arange(TOKENS, dtype=jnp.int32) % ROW_LEN).astype(jnp.int32)
    cosine_table, sine_table = turn_tables(places, HEAD_DIM)
    route_table = (routes[:, :, None] == jnp.arange(EXPERTS, dtype=jnp.int32)[None, None, :]).astype(jnp.float32)
    segments = segment_ids.reshape(PACKS, ROW_LEN)
    step_rows = math.gcd(ROW_LEN, 512)
    score_scale = HEAD_DIM ** (-0.5)

    def attend_pack(packed):
        pack_queries, pack_keys, pack_values, pack_segments = packed
        key_places = jnp.arange(ROW_LEN, dtype=jnp.int32)

        def attend_block(block_index):
            offset = block_index * step_rows
            block_queries = lax.dynamic_slice_in_dim(pack_queries, offset, step_rows, 0)
            block_segments = lax.dynamic_slice_in_dim(pack_segments, offset, step_rows, 0)
            query_places = offset + jnp.arange(step_rows, dtype=jnp.int32)
            allowed = jnp.logical_and(block_segments[:, None] == pack_segments[None, :], key_places[None, :] // BLOCK <= query_places[:, None] // BLOCK)[None]
            scores = low_back(jnp.einsum('qhd,khd->hqk', block_queries, pack_keys, precision=HIGHEST_MODE) * score_scale)
            scores = jnp.where(allowed, scores, NEG_LARGE)
            shifted = jnp.exp(scores - lax.optimization_barrier(jnp.max(scores, axis=2, keepdims=True)))
            weights = shifted / lax.optimization_barrier(jnp.sum(shifted, axis=2, keepdims=True))
            return jnp.einsum('hqk,khd->qhd', low(weights), pack_values, precision=HIGHEST_MODE)
        blocks = lax.map(jax.checkpoint(attend_block), jnp.arange(ROW_LEN // step_rows, dtype=jnp.int32))
        return blocks.reshape(ROW_LEN, HEADS, HEAD_DIM)

    def forward_pass(layer_inputs, first_norm_gain, query_matrix, key_matrix, value_matrix, output_matrix, second_norm_gain, router_matrix, shared_gate_matrix, shared_up_matrix, shared_down_matrix, expert_gate_matrix, expert_up_matrix, expert_down_matrix):
        normed_one = layer_inputs * rms_scale(layer_inputs)
        hidden_one = low(normed_one * first_norm_gain)
        query_raw = low_back(precise(hidden_one, query_matrix)).reshape(TOKENS, HEADS, HEAD_DIM)
        queries = low(rotate(query_raw, cosine_table, sine_table))
        key_raw = low_back(precise(hidden_one, key_matrix)).reshape(TOKENS, HEADS, HEAD_DIM)
        keys_all = low(rotate(key_raw, cosine_table, sine_table))
        values_all = low(low_back(precise(hidden_one, value_matrix))).reshape(TOKENS, HEADS, HEAD_DIM)
        attended = lax.map(attend_pack, (queries.reshape(PACKS, ROW_LEN, HEADS, HEAD_DIM), keys_all.reshape(PACKS, ROW_LEN, HEADS, HEAD_DIM), values_all.reshape(PACKS, ROW_LEN, HEADS, HEAD_DIM), segments))
        attended_low = low(low_back(attended.reshape(TOKENS, D)))
        middle = layer_inputs + low_back(precise(attended_low, output_matrix))
        normed_two = middle * rms_scale(middle)
        hidden_two = low(normed_two * second_norm_gain)
        logits = low_back(precise(hidden_two, router_matrix))
        shifted = jnp.exp(logits - lax.optimization_barrier(jnp.max(logits, axis=1, keepdims=True)))
        router_probs = shifted / lax.optimization_barrier(jnp.sum(shifted, axis=1, keepdims=True))
        gate_values = lax.optimization_barrier(jnp.sum(router_probs[:, None, :] * route_table, axis=2))
        shared_pre = low_back(precise(hidden_two, shared_gate_matrix))
        shared_lin = low_back(precise(hidden_two, shared_up_matrix))
        shared_hidden = low(silu_value(shared_pre) * shared_lin)
        shared_result = precise(shared_hidden, shared_down_matrix)
        padded_rows = jnp.concatenate([hidden_two, jnp.zeros((1, D), jnp.float32)], axis=0)

        def expert_layer_block(packed):
            gate_weight, up_weight, down_weight, row_index = packed
            routed_rows = low_back(padded_rows[row_index])
            gate_pre = low_back(precise(routed_rows, gate_weight))
            up_pre = low_back(precise(routed_rows, up_weight))
            expert_hidden = low(silu_value(gate_pre) * up_pre)
            return low(low_back(precise(expert_hidden, down_weight)))
        expert_outputs = lax.map(jax.checkpoint(expert_layer_block), (expert_gate_matrix, expert_up_matrix, expert_down_matrix, slot_token_row))
        picked = expert_outputs.reshape(EXPERTS * expert_room, D)[slot_of_choice].reshape(TOKENS, TOPK, D)
        mixture = lax.optimization_barrier(jnp.sum(gate_values[:, :, None] * picked, axis=1))
        return middle + shared_result + mixture
    float_args = (tokens.astype(jnp.float32), norm1_gain.astype(jnp.float32), w_query.astype(jnp.float32), w_key.astype(jnp.float32), w_value.astype(jnp.float32), w_out.astype(jnp.float32), norm2_gain.astype(jnp.float32), w_router.astype(jnp.float32), shared_gate.astype(jnp.float32), shared_up.astype(jnp.float32), shared_down.astype(jnp.float32), expert_gate.astype(jnp.float32), expert_up.astype(jnp.float32), expert_down.astype(jnp.float32))
    result, pullback = jax.vjp(forward_pass, *float_args)
    gradients = pullback(out_grad.astype(jnp.float32))
    return (result.astype(jnp.bfloat16), gradients[0], gradients[1], gradients[2], gradients[3], gradients[4], gradients[5], gradients[6], gradients[7], gradients[8], gradients[9], gradients[10], gradients[11], gradients[12], gradients[13])
```

```python
import functools
import math

import jax
import jax.numpy as jnp
from jax import lax
from jax.experimental import pallas as pl
from jax.experimental.pallas import tpu as pltpu
from jax.sharding import PartitionSpec as P

HEADS = 12
EPSILON = 1e-06
NEG_LARGE = -1e30
BF = jnp.bfloat16
F32 = jnp.float32
VMEM_LIMIT = 58 * 1024 * 1024


def nn(a, b):
    return lax.dot_general(a, b, (((1,), (0,)), ((), ())), preferred_element_type=F32)


def nt(a, b):
    return lax.dot_general(a, b, (((1,), (1,)), ((), ())), preferred_element_type=F32)


def tn(a, b):
    return lax.dot_general(a, b, (((0,), (0,)), ((), ())), preferred_element_type=F32)


def rms_scale(values):
    return lax.rsqrt(jnp.mean(values * values, axis=1, keepdims=True) + EPSILON)


def lanes(shape):
    return lax.broadcasted_iota(jnp.int32, shape, len(shape) - 1)


def turned(x):
    front = lanes(x.shape) % 64 < 32
    return jnp.where(front, -pltpu.roll(x, 96, 1), pltpu.roll(x, 32, 1))


def vmem(n):
    return [pl.BlockSpec(memory_space=pltpu.VMEM)] * n


def params(**kw):
    return pltpu.CompilerParams(vmem_limit_bytes=VMEM_LIMIT, **kw)


def whole(shape):
    return pl.BlockSpec(shape, lambda *_: (0,) * len(shape))


def qkv_kernel(chips, rows, c_ref, *refs):
    own, par = refs[:chips], refs[chips : 2 * chips]
    wq, wk, wv, cos, sin, gain, h1, keys, vals, quer = refs[2 * chips :]
    c = c_ref[0]
    pairs = keys.shape[0]
    scale = 0.125
    for s in range(chips):
        for p, src in ((0, own[s]), (1, par[s])):
            core = c if p == 0 else 1 - c
            slot = 2 * (chips - 1 - s) + core
            x = src[0:rows, :].astype(F32)
            h = (x * rms_scale(x) * gain[...]).astype(BF)
            h1[slot] = h
            co, si = cos[slot], sin[slot]
            k = nn(h, wk[...])
            v = nn(h, wv[...])
            for i in range(pairs):
                kp = k[:, 128 * i : 128 * i + 128]
                keys[i, slot] = (kp * co + turned(kp) * si).astype(BF)
                vals[i, slot] = v[:, 128 * i : 128 * i + 128].astype(BF)
            if s == 0:
                q = nn(h, wq[...])
                for i in range(pairs):
                    qp = q[:, 128 * i : 128 * i + 128]
                    quer[i, core] = ((qp * co + turned(qp) * si) * scale).astype(BF)


def attend_kernel(first, count, rows, q_ref, k_ref, v_ref, sq_ref, sk_ref, o_ref, ol_ref, lse_ref, s_scr):
    low = lanes((rows, 128)) < 64
    for qi in range(2):
        qpair = q_ref[0, qi * rows : (qi + 1) * rows, :]
        sq = sq_ref[qi * rows : (qi + 1) * rows, 0:1]
        outs, lses = [], []
        for hh in range(2):
            keep = low if hh == 0 else jnp.logical_not(low)
            q = jnp.where(keep, qpair, jnp.zeros_like(qpair))
            m = jnp.full((rows, 128), NEG_LARGE, F32)
            for j in range(count):
                at = (first + qi + j) * rows
                s = nt(q, k_ref[0, at : at + rows, :])
                s = jnp.where(sq == sk_ref[0:1, at : at + rows], s, NEG_LARGE)
                s_scr[:, j * rows : (j + 1) * rows] = s
                for g in range(rows // 128):
                    m = jnp.maximum(m, s[:, g * 128 : (g + 1) * 128])
            m = jnp.max(m, axis=1, keepdims=True)
            total = jnp.zeros((rows, 128), F32)
            acc = jnp.zeros((rows, 128), F32)
            for j in range(count):
                at = (first + qi + j) * rows
                e = jnp.exp(s_scr[:, j * rows : (j + 1) * rows] - m)
                for g in range(rows // 128):
                    total = total + e[:, g * 128 : (g + 1) * 128]
                acc = acc + nn(e.astype(BF), v_ref[0, at : at + rows, :])
            total = jnp.sum(total, axis=1, keepdims=True)
            outs.append(acc / total)
            lses.append(m + jnp.log(total))
        o = jnp.where(low, outs[0], outs[1])
        o_ref[0, qi * rows : (qi + 1) * rows, :] = o
        ol_ref[0, qi * rows : (qi + 1) * rows, :] = o.astype(BF)
        both = jnp.where(lanes((rows, 128)) == 0, lses[0], lses[1])
        lse_ref[0, :, qi * rows : (qi + 1) * rows] = both.T[0:8, :]


def mid_kernel(a_ref, w_ref, x_ref, g_ref, mid_ref, h_ref):
    mid = x_ref[...].astype(F32) + nn(a_ref[...], w_ref[...])
    mid_ref[...] = mid
    h_ref[...] = (mid * rms_scale(mid) * g_ref[...]).astype(BF)


def pre_kernel(nblk, rows, *refs):
    og = refs[:nblk]
    p_ref, wd, wsd, dehid, ogx_t, dsh, ogx = refs[nblk:]
    cap = p_ref.shape[1]

    @pl.when(pl.program_id(0) == 0)
    def _():
        for b in range(nblk):
            block = og[b][0:rows, :]
            ogx[b * cap : (b + 1) * cap, :] = nn(p_ref[b], block).astype(BF)
            dsh[b * rows : (b + 1) * rows, :] = nt(block, wsd[...]).astype(BF)
        ogx_t[...] = ogx[...].T

    dehid[...] = nt(ogx[...], wd[...]).astype(BF)


def act(g, u, dh):
    s = jax.nn.sigmoid(g)
    silu = g * s
    hid = (silu * u).astype(BF)
    dg = (dh * u * (s * (1.0 + g * (1.0 - s)))).astype(BF)
    du = (dh * silu).astype(BF)
    return hid, dg, du


def split_nn(a, col):
    wide = jnp.broadcast_to(col, (col.shape[0], 128))
    high = wide.astype(BF)
    return nn(a, high) + nn(a, (wide - high.astype(F32)).astype(BF))


def expert_kernel(nblk, rows, experts, e_ref, *refs):
    g_refs = refs[:nblk]
    (p_ref, pt_ref, wr, wr_t, wsg, wsu, dsh, wg, wu, dehid) = refs[nblk : nblk + 10]
    (x_out, ehid, degate, deup, gate_slot, gate_tok, shid, dsg, dsu, tg, rgrad) = refs[nblk + 10 : nblk + 21]
    x_scr, row_scr, tg_scr, pg_scr, prob_scr, gs_scr = refs[nblk + 21 :]
    cap = p_ref.shape[1]
    step = pl.program_id(0)
    own = lanes((rows, 128)) == e_ref[0]

    @pl.when(step == 0)
    def _():
        row_scr[...] = jnp.zeros_like(row_scr)
        pg_scr[...] = jnp.zeros_like(pg_scr)
        for b in range(nblk):
            block = g_refs[b][...]
            x = nn(p_ref[b], block).astype(BF)
            x_scr[b * cap : (b + 1) * cap, :] = x
            x_out[b * cap : (b + 1) * cap, :] = x
            logits = jnp.where(lanes((rows, 128)) < experts, nn(block, wr[...]), NEG_LARGE)
            shifted = jnp.exp(logits - jnp.max(logits, axis=1, keepdims=True))
            probs = shifted / jnp.sum(shifted, axis=1, keepdims=True)
            prob_scr[b] = probs
            gate = jnp.sum(jnp.where(own, probs, 0.0), axis=1, keepdims=True)
            gate_tok[b] = jnp.broadcast_to(gate, (rows, 128))
            slot = split_nn(p_ref[b], gate)
            gs_scr[b * cap : (b + 1) * cap, :] = slot
            gate_slot[b * cap : (b + 1) * cap, :] = slot
            at = b * rows
            hid, dg, du = act(nn(block, wsg[...]), nn(block, wsu[...]), dsh[at : at + rows, :].astype(F32))
            shid[at : at + rows, :] = hid
            dsg[at : at + rows, :] = dg
            dsu[at : at + rows, :] = du
            tg_scr[at : at + rows, :] = nt(dg, wsg[...]) + nt(du, wsu[...])

    raw = dehid[...].astype(F32)
    hid, dg, du = act(nn(x_scr[...], wg[0]), nn(x_scr[...], wu[0]), raw * gs_scr[:, 0:1])
    ehid[...] = hid
    degate[...] = dg
    deup[...] = du
    row_scr[...] += nt(dg, wg[0]) + nt(du, wu[0])
    pg_scr[...] += jnp.sum(hid.astype(F32) * raw, axis=1, keepdims=True)

    @pl.when(step == pl.num_programs(0) - 1)
    def _():
        total = jnp.zeros_like(rgrad)
        for b in range(nblk):
            at = b * rows
            pg = split_nn(pt_ref[b], pg_scr[b * cap : (b + 1) * cap, 0:1])
            probs = prob_scr[b]
            gate = jnp.sum(jnp.where(own, probs, 0.0), axis=1, keepdims=True)
            lgrad = (pg * probs * (own.astype(F32) - gate)).astype(BF)
            total += tn(lgrad, g_refs[b][...])
            back = nn(pt_ref[b], row_scr[b * cap : (b + 1) * cap, :].astype(BF))
            tg[b] = (tg_scr[at : at + rows, :] + back + nn(lgrad, wr_t[...])).astype(BF)
        rgrad[...] = total


def wgrad_kernel(x_ref, ogx_t, gate_slot, ehid, degate, deup, gu, dn, x_t):
    @pl.when(pl.program_id(0) == 0)
    def _():
        x_t[...] = x_ref[...].T

    gu[0, 0] = nn(x_t[...], degate[...]).astype(BF)
    gu[0, 1] = nn(x_t[...], deup[...]).astype(BF)
    dn[...] = nn(ogx_t[...], (ehid[...].astype(F32) * gate_slot[:, 0:1]).astype(BF)).astype(BF)


def result_kernel(nblk, rows, *refs):
    g_refs, og = refs[:nblk], refs[nblk : 2 * nblk]
    (pt_ref, gate_tok, shid, dsg, dsu, wsd, ehid, wd) = refs[2 * nblk : 2 * nblk + 8]
    mix, sgu, sd, acc = refs[2 * nblk + 8 :]
    cap = pt_ref.shape[2]
    step = pl.program_id(0)

    @pl.when(step == 0)
    def _():
        acc[...] = jnp.zeros_like(acc)
        dg_sum = jnp.zeros((sgu.shape[0], dsg.shape[1]), F32)
        du_sum = jnp.zeros_like(dg_sum)
        sd_sum = jnp.zeros(sd.shape, F32)
        for b in range(nblk):
            at = b * rows
            g_t = g_refs[b][...].T
            dg_sum += nn(g_t, dsg[at : at + rows, :])
            du_sum += nn(g_t, dsu[at : at + rows, :])
            sd_sum += tn(shid[at : at + rows, :], og[b][0:rows, :])
        width = dsg.shape[1]
        sgu[:, :width] = dg_sum.astype(BF)
        sgu[:, width:] = du_sum.astype(BF)
        sd[...] = sd_sum.astype(BF)

    acc[...] += nn(ehid[...], wd[0])

    @pl.when(step == pl.num_programs(0) - 1)
    def _():
        for b in range(nblk):
            at = b * rows
            res = acc[b * cap : (b + 1) * cap, :].astype(BF)
            picked = nn(pt_ref[b], res) * gate_tok[b][:, 0:1]
            mix[b] = (picked + nn(shid[at : at + rows, :], wsd[...])).astype(BF)


def mid_back_kernel(count, *refs):
    pieces = refs[:count]
    mid_ref, g_ref, og_ref, w_ref, mg_ref, ag_ref, da_ref, gg_ref = refs[count:]
    two = pieces[0][...].astype(F32)
    for piece in pieces[1:]:
        two += piece[...].astype(F32)
    mid = mid_ref[...]
    scale = rms_scale(mid)
    mn = mid * scale
    gg_ref[...] = jnp.broadcast_to(jnp.sum(two * mn, axis=0, keepdims=True), gg_ref.shape)
    dn = two * g_ref[...]
    mg = og_ref[...].astype(F32) + scale * (dn - mn * jnp.mean(dn * mn, axis=1, keepdims=True))
    mg_ref[...] = mg
    ag = mg.astype(BF)
    ag_ref[...] = ag
    da = nt(ag, w_ref[...]).astype(BF)
    for i in range(da_ref.shape[0]):
        da_ref[i] = da[:, 128 * i : 128 * i + 128]


def attend_back_kernel(first, count, rows, q_ref, k_ref, v_ref, o_ref, do_ref, lse_ref, sq_ref, sk_ref, cos, sin,
                       h1_ref, wq, wk, wv, gain, grads, og1, gg, h1_t, k_t, dk, dv, og_scr):
    step = pl.program_id(0)
    low = lanes((rows, 128)) < 64
    kv_rows = k_ref.shape[1]
    base = kv_rows - 2 * rows

    @pl.when(step == 0)
    def _():
        h1_t[...] = h1_ref[...].T
        og_scr[...] = jnp.zeros_like(og_scr)

    k_t[...] = k_ref[0].T
    dk[...] = jnp.zeros_like(dk)
    dv[...] = jnp.zeros_like(dv)
    dqs = []
    for qi in range(2):
        at_q = qi * rows
        qpair = q_ref[0, at_q : at_q + rows, :]
        dopair = do_ref[0, at_q : at_q + rows, :]
        prod = dopair.astype(F32) * o_ref[0, at_q : at_q + rows, :]
        d0 = jnp.sum(jnp.where(low, prod, 0.0), axis=1, keepdims=True)
        d1 = jnp.sum(jnp.where(low, 0.0, prod), axis=1, keepdims=True)
        delta = jnp.where(lanes((rows, 128)) == 0, d0, d1).T
        sq = sq_ref[0:1, at_q : at_q + rows]
        halves = []
        for hh in range(2):
            keep = low if hh == 0 else jnp.logical_not(low)
            q = jnp.where(keep, qpair, jnp.zeros_like(qpair))
            do = jnp.where(keep, dopair, jnp.zeros_like(dopair))
            lse_row = lse_ref[0, hh : hh + 1, at_q : at_q + rows]
            delta_row = delta[hh : hh + 1, :]
            dq = jnp.zeros((64, rows), F32)
            for j in range(count):
                at = (first + qi + j) * rows
                same = sk_ref[at : at + rows, 0:1] == sq
                s = nt(k_ref[0, at : at + rows, :], q)
                p = jnp.where(same, jnp.exp(s - lse_row), 0.0)
                dp = nt(v_ref[0, at : at + rows, :], do)
                ds = (p * (dp - delta_row)).astype(BF)
                dv[at : at + rows, :] += nn(p.astype(BF), do)
                dk[at : at + rows, :] += nn(ds, q)
                dq += nn(k_t[64 * hh : 64 * hh + 64, at : at + rows], ds)
            halves.append(dq)
        dq = jnp.concatenate(halves, axis=0).T * 0.125
        at = base + at_q
        dq = dq * cos[at : at + rows, :] - turned(dq) * sin[at : at + rows, :]
        dqs.append(dq.astype(BF))
    dq = jnp.concatenate(dqs, axis=0)
    dkv = dk[...]
    dkb = (dkv * cos[...] - turned(dkv) * sin[...]).astype(BF)
    dvb = dv[...].astype(BF)
    grads[0] = nn(h1_t[:, base:], dq).astype(BF)
    grads[1] = nn(h1_t[...], dkb).astype(BF)
    grads[2] = nn(h1_t[...], dvb).astype(BF)
    og_scr[...] += nt(dkb, wk[...]) + nt(dvb, wv[...])
    og_scr[base:, :] += nt(dq, wq[...])

    @pl.when(step == pl.num_programs(0) - 1)
    def _():
        one = og_scr[...]
        og1[...] = one.astype(BF)
        total = jnp.sum(one * h1_ref[...].astype(F32), axis=0, keepdims=True) / gain[...]
        gg[...] = jnp.broadcast_to(total, gg.shape)


def last_kernel(count, *refs):
    pieces = refs[:count]
    x_ref, g_ref, mg_ref, out = refs[count:]
    one = pieces[0][...].astype(F32)
    for piece in pieces[1:]:
        one += piece[...].astype(F32)
    x = x_ref[...].astype(F32)
    scale = rms_scale(x)
    xn = x * scale
    dn = one * g_ref[...]
    out[...] = mg_ref[...] + scale * (dn - xn * jnp.mean(dn * xn, axis=1, keepdims=True))


def shape(dims, dtype=BF):
    return jax.ShapeDtypeStruct(dims, dtype)


def shards(
    R,
    E,
    tokens,
    segment_ids,
    routes,
    norm1_gain,
    w_query,
    w_key,
    w_value,
    w_out,
    norm2_gain,
    w_router,
    shared_gate,
    shared_up,
    shared_down,
    expert_gate,
    expert_up,
    expert_down,
    out_grad,
):
    Z = E // 2
    T, D = tokens.shape
    FF = shared_gate.shape[1]
    topk = routes.shape[1]
    experts = w_router.shape[1]
    assert expert_gate.shape[0] == 1 and experts == E
    half = D // 2
    pairs = half // 128
    wrow = w_query.shape[0]
    hrow = 2 * wrow
    cap = 2 * T * topk // experts
    slots = E * cap
    fs = FF // E
    drow = shared_down.shape[0]
    longest = E * T // 2
    back = -(-(longest - 1) // T)
    nb = -(-back // 2)
    chips = nb + 1
    kvb = 2 * chips
    first = 2 * nb - back
    count = back + 1
    r = lax.axis_index("rep")
    e = lax.axis_index("ep")
    z, c = e // 2, e % 2
    is0 = c == 0
    c_arr = jnp.reshape(c, (1,)).astype(jnp.int32)
    e_arr = jnp.reshape(e, (1,)).astype(jnp.int32)

    def swap(x):
        return lax.ppermute(x, "ep", [(i, i ^ 1) for i in range(E)])

    def ring(x, s):
        return lax.ppermute(x, "ep", [(i, (i + 2 * s) % E) for i in range(E)])

    def line(x, s):
        return lax.ppermute(x, "ep", [(i, i + 2 * s) for i in range(E) if 0 <= i + 2 * s < E])

    def cross(x, s):
        return lax.ppermute(x, "rep", [(i, i ^ s) for i in range(R)])

    def ordered(mine, other):
        return jnp.where(is0, mine, other), jnp.where(is0, other, mine)

    def put(buf, x, i):
        return lax.dynamic_update_index_in_dim(buf, x, i, 0)

    def chip_pack(mats, extra):
        stacked = jnp.stack(mats).reshape(len(mats) * wrow, D)
        mine, other = ordered(stacked[:, :half], stacked[:, half:])
        ext = jnp.pad(extra.reshape(1, -1), ((0, 0), (0, half - extra.size)))
        got = swap(jnp.concatenate([other, ext], axis=0))
        a, b = ordered(mine, got[:-1])
        ea, eb = ordered(ext, got[-1:])
        rows = jnp.stack([a.reshape(-1, wrow, half), b.reshape(-1, wrow, half)], axis=1).reshape(-1, half)
        rows = jnp.concatenate([rows, ea, eb], axis=0)
        return jnp.pad(rows, ((0, -rows.shape[0] % 16), (0, 0)))

    def gather_z(pack):
        buf = put(jnp.zeros((Z,) + pack.shape, BF), pack, z)
        for s in range(1, Z):
            buf = put(buf, ring(pack, s), (z - s) % Z)
        return buf

    def gather_rep(part):
        buf = put(jnp.zeros((R,) + part.shape, BF), part, r)
        for s in range(1, R):
            buf = put(buf, cross(part, s), r ^ s)
        return buf

    def unpack(full, i):
        return full[:, :, i * hrow : (i + 1) * hrow, :].reshape(D, half)

    pack1 = chip_pack([w_query, w_key, w_value], norm1_gain)
    full1 = gather_rep(gather_z(pack1))
    wq, wk, wv = (unpack(full1, i) for i in range(3))
    gain1 = full1[:, :, 3 * hrow : 3 * hrow + 2, :wrow].reshape(1, D).astype(F32)

    seg_row = jnp.pad(segment_ids.reshape(1, T).astype(BF), ((0, 7), (0, D - T)))
    tok_pack = jnp.concatenate([tokens, seg_row], axis=0)
    own_tok = [tok_pack] + [line(tok_pack, s) for s in range(1, chips)]
    par_tok = [swap(x) for x in own_tok]

    seg_blocks = [None] * kvb
    for s in range(chips):
        valid = z - s >= 0
        a, b = ordered(own_tok[s][T, :T], par_tok[s][T, :T])
        seg_blocks[2 * (nb - s)] = jnp.where(valid, a.astype(F32), -1.0)
        seg_blocks[2 * (nb - s) + 1] = jnp.where(valid, b.astype(F32), -1.0)
    segs = jnp.stack(seg_blocks)
    kv_rows = kvb * T
    seg_flat = segs.reshape(1, kv_rows)
    seg_wide = jnp.broadcast_to(segs.reshape(kv_rows, 1), (kv_rows, 128))

    inverse = jnp.exp(jnp.arange(32).astype(F32) * (-2.0 * math.log(10000.0) / 64))
    inverse = jnp.tile(inverse, 4)
    places = (z - nb) * (2 * T) + jnp.arange(kv_rows, dtype=jnp.int32)
    angle = places.astype(F32)[:, None] * inverse[None, :]
    cos, sin = jnp.cos(angle), jnp.sin(angle)

    h1, keys, vals, quer = pl.pallas_call(
        functools.partial(qkv_kernel, chips, T),
        in_specs=[pl.BlockSpec(memory_space=pltpu.SMEM)] + vmem(2 * chips + 6),
        out_specs=tuple(vmem(4)),
        out_shape=(
            shape((kvb, T, D)),
            shape((pairs, kvb, T, 128)),
            shape((pairs, kvb, T, 128)),
            shape((pairs, 2, T, 128)),
        ),
        compiler_params=params(),
        name="qkv",
    )(c_arr, *own_tok, *par_tok, wq, wk, wv, cos.reshape(kvb, T, 128), sin.reshape(kvb, T, 128), gain1)
    h1 = h1.reshape(kv_rows, D)
    keys = keys.reshape(pairs, kv_rows, 128)
    vals = vals.reshape(pairs, kv_rows, 128)
    quer = quer.reshape(pairs, 2 * T, 128)

    tok_done = own_tok[-1]
    og_pack = jnp.concatenate(
        [out_grad, jnp.pad(routes.reshape(1, topk * T).astype(BF), ((0, 7), (0, D - topk * T)))], axis=0
    )
    og_pack, full1_dep, tok_done = lax.optimization_barrier((og_pack, full1[0, 0, 0], tok_done))

    def gather_ep(x):
        lane = [x] + [ring(x, s) for s in range(1, Z)]
        blocks = []
        for item in lane:
            blocks += [item, swap(item)]
        return blocks

    pack2 = chip_pack([w_out], jnp.concatenate([norm2_gain, w_router.reshape(-1)]))
    full2 = gather_rep(gather_z(pack2))
    wo_half = unpack(full2, 0)
    wo = jnp.concatenate(ordered(wo_half, swap(wo_half)), axis=1)
    ext2 = full2[:, :, hrow : hrow + 2, :].reshape(R * E, half)
    gain2 = ext2[:, :wrow].reshape(1, D).astype(F32)
    router = ext2[:, wrow : wrow + wrow * experts].reshape(D, experts)
    router = jnp.pad(router, ((0, 0), (0, 128 - experts)))
    router_t = router.T

    def by_unit(w):
        return w.reshape(wrow, R, E, drow).transpose(2, 0, 1, 3).reshape(E, wrow, fs)

    gu = jnp.concatenate([by_unit(shared_gate), by_unit(shared_up)], axis=2)
    gu = lax.all_to_all(gu, "ep", split_axis=0, concat_axis=0, tiled=True).reshape(E * wrow, 2 * fs)
    gu = gather_rep(gu).reshape(D, 2 * fs)
    wsg, wsu = gu[:, :fs], gu[:, fs:]
    wsd = gather_rep(shared_down).reshape(fs, D)

    og_blocks = gather_ep(og_pack)
    table = jnp.stack([x[T, : topk * T] for x in og_blocks]).reshape(E, T, topk)
    hit = jnp.any(table == e.astype(F32).astype(BF), axis=2).astype(F32)
    rank = jnp.cumsum(hit, axis=1) - hit
    rank = jnp.where(hit > 0, rank, -1.0)
    slot_ids = jnp.arange(cap).astype(F32)
    pick = (rank[:, None, :] == slot_ids[None, :, None]).astype(BF)
    pick_t = (rank[:, :, None] == slot_ids[None, None, :]).astype(BF)

    one = lambda *dims: pl.BlockSpec((1,) + dims, lambda i: (i, 0, 0))
    att, att_low, lse = pl.pallas_call(
        functools.partial(attend_kernel, first, count, T),
        grid=(pairs,),
        in_specs=[
            one(2 * T, 128),
            one(kv_rows, 128),
            one(kv_rows, 128),
            whole((2 * T, 128)),
            whole((1, kv_rows)),
        ],
        out_specs=(one(2 * T, 128), one(2 * T, 128), one(8, 2 * T)),
        out_shape=(
            shape((pairs, 2 * T, 128), F32),
            shape((pairs, 2 * T, 128)),
            shape((pairs, 8, 2 * T), F32),
        ),
        scratch_shapes=[pltpu.VMEM((T, count * T), F32)],
        compiler_params=params(),
        name="attend",
    )(quer, keys, vals, seg_wide[-2 * T :], seg_flat)

    def joined(mine, other):
        both = jnp.where(is0, jnp.concatenate([mine, other]), jnp.concatenate([other, mine]))
        return both.transpose(1, 0, 2).reshape(T, D)

    att_own, att_other = ordered(att_low[:, :T], att_low[:, T:])
    attended = joined(att_own, swap(att_other))
    mid, h2 = pl.pallas_call(
        mid_kernel,
        in_specs=vmem(4),
        out_specs=tuple(vmem(2)),
        out_shape=(shape((T, D), F32), shape((T, D))),
        compiler_params=params(),
        name="mid",
    )(attended, wo, tokens, gain2)

    ft = min(256, FF // R)
    steps = FF // ft
    per = FF // R // ft
    col = lambda n: pl.BlockSpec((n, ft), lambda i: (0, i))
    wcol = pl.BlockSpec((1, D, ft), lambda i: (0, 0, i))
    wdn = pl.BlockSpec((1, ft, D), lambda i: (0, i, 0))
    dehid, ogx_t, dsh = pl.pallas_call(
        functools.partial(pre_kernel, E, T),
        grid=(steps,),
        in_specs=[whole((T + 8, D))] * E
        + [whole((E, cap, T)), pl.BlockSpec((ft, D), lambda i: (i, 0)), whole((fs, D))],
        out_specs=(col(slots), whole((D, slots)), whole((E * T, fs))),
        out_shape=(shape((slots, FF)), shape((D, slots)), shape((E * T, fs))),
        scratch_shapes=[pltpu.VMEM((slots, D), BF)],
        compiler_params=params(),
        name="pre",
    )(*og_blocks, pick, expert_down.reshape(FF, D), wsd)

    h2_blocks = gather_ep(h2)
    (x_rows, ehid, degate, deup, gate_slot, gate_tok, shid, dsg, dsu, tg, rgrad) = pl.pallas_call(
        functools.partial(expert_kernel, E, T, experts),
        grid=(steps,),
        in_specs=[pl.BlockSpec(memory_space=pltpu.SMEM)]
        + [whole((T, D))] * E
        + [
            whole((E, cap, T)),
            whole((E, T, cap)),
            whole((D, 128)),
            whole((128, D)),
            whole((D, fs)),
            whole((D, fs)),
            whole((E * T, fs)),
            wcol,
            wcol,
            col(slots),
        ],
        out_specs=(
            whole((slots, D)),
            col(slots),
            col(slots),
            col(slots),
            whole((slots, 128)),
            whole((E, T, 128)),
            whole((E * T, fs)),
            whole((E * T, fs)),
            whole((E * T, fs)),
            whole((E, T, D)),
            whole((128, D)),
        ),
        out_shape=(
            shape((slots, D)),
            shape((slots, FF)),
            shape((slots, FF)),
            shape((slots, FF)),
            shape((slots, 128), F32),
            shape((E, T, 128), F32),
            shape((E * T, fs)),
            shape((E * T, fs)),
            shape((E * T, fs)),
            shape((E, T, D)),
            shape((128, D), F32),
        ),
        scratch_shapes=[
            pltpu.VMEM((slots, D), BF),
            pltpu.VMEM((slots, D), F32),
            pltpu.VMEM((E * T, D), F32),
            pltpu.VMEM((slots, 128), F32),
            pltpu.VMEM((E, T, 128), F32),
            pltpu.VMEM((slots, 128), F32),
        ],
        compiler_params=params(),
        name="expert",
    )(e_arr, *h2_blocks, pick, pick_t, router, router_t, wsg, wsu, dsh, expert_gate, expert_up, dehid)

    def scatter_ep(blocks):
        lane = [blocks[2 * s] + swap(blocks[2 * s + 1]) for s in range(Z)]
        return [lane[0]] + [ring(lane[s], -s) for s in range(1, Z)]

    two_parts = scatter_ep(tg)

    gu_grad, dn_grad = pl.pallas_call(
        wgrad_kernel,
        grid=(steps,),
        in_specs=[whole((slots, D)), whole((D, slots)), whole((slots, 128)), col(slots), col(slots), col(slots)],
        out_specs=(
            pl.BlockSpec((1, 2, D, ft), lambda i: (i // per, 0, 0, i % per)),
            col(D),
        ),
        out_shape=(shape((R, 2, D, FF // R)), shape((D, FF))),
        scratch_shapes=[pltpu.VMEM((D, slots), BF)],
        compiler_params=params(),
        name="wgrad",
    )(x_rows, ogx_t, gate_slot, ehid, degate, deup)
    gu_sum = lax.psum_scatter(gu_grad.reshape(-1, FF // R), "rep", scatter_dimension=0, tiled=True)
    gu_sum = gu_sum.reshape(1, 2, D, FF // R)
    dn_sum = lax.psum_scatter(dn_grad, "rep", scatter_dimension=0, tiled=True)

    mix, sgu_grad, sd_grad = pl.pallas_call(
        functools.partial(result_kernel, E, T),
        grid=(steps,),
        in_specs=[whole((T, D))] * E
        + [whole((T + 8, D))] * E
        + [
            whole((E, T, cap)),
            whole((E, T, 128)),
            whole((E * T, fs)),
            whole((E * T, fs)),
            whole((E * T, fs)),
            whole((fs, D)),
            col(slots),
            wdn,
        ],
        out_specs=(whole((E, T, D)), whole((D, 2 * fs)), whole((fs, D))),
        out_shape=(shape((E, T, D)), shape((D, 2 * fs)), shape((fs, D))),
        scratch_shapes=[pltpu.VMEM((slots, D), F32)],
        compiler_params=params(),
        name="result",
    )(*h2_blocks, *og_blocks, pick_t, gate_tok, shid, dsg, dsu, wsd, ehid, expert_down)

    mid_grad, attn_grad, att_grad, gain2_part = pl.pallas_call(
        functools.partial(mid_back_kernel, Z),
        in_specs=vmem(Z + 4),
        out_specs=tuple(vmem(4)),
        out_shape=(shape((T, D), F32), shape((T, D)), shape((2 * pairs, T, 128)), shape((8, D), F32)),
        compiler_params=params(),
        name="mid_back",
    )(*two_parts, mid, gain2, out_grad, wo)

    ag_own, ag_other = ordered(att_grad[:pairs], att_grad[pairs:])
    do_a, do_b = ordered(ag_own, swap(ag_other))
    do = jnp.concatenate([do_a, do_b], axis=1)

    grads, og1, gain1_part = pl.pallas_call(
        functools.partial(attend_back_kernel, first, count, T),
        grid=(pairs,),
        in_specs=[
            one(2 * T, 128),
            one(kv_rows, 128),
            one(kv_rows, 128),
            one(2 * T, 128),
            one(2 * T, 128),
            one(8, 2 * T),
            whole((1, 2 * T)),
            whole((kv_rows, 128)),
            whole((kv_rows, 128)),
            whole((kv_rows, 128)),
            whole((kv_rows, D)),
            pl.BlockSpec((D, 128), lambda i: (0, i)),
            pl.BlockSpec((D, 128), lambda i: (0, i)),
            pl.BlockSpec((D, 128), lambda i: (0, i)),
            whole((1, D)),
        ],
        out_specs=(
            pl.BlockSpec((3, D, 128), lambda i: (0, 0, i)),
            whole((kv_rows, D)),
            whole((8, D)),
        ),
        out_shape=(shape((3, D, half)), shape((kv_rows, D)), shape((8, D), F32)),
        scratch_shapes=[
            pltpu.VMEM((D, kv_rows), BF),
            pltpu.VMEM((128, kv_rows), BF),
            pltpu.VMEM((kv_rows, 128), F32),
            pltpu.VMEM((kv_rows, 128), F32),
            pltpu.VMEM((kv_rows, D), F32),
        ],
        compiler_params=params(),
        name="attend_back",
    )(quer, keys, vals, att, do, lse, seg_flat[:, -2 * T :], seg_wide, cos, sin, h1, wq, wk, wv, gain1)

    og1 = og1.reshape(chips, 2, T, D)
    mine, other = ordered(og1[:, 0], og1[:, 1])
    lane = mine + swap(other)
    one_parts = [lane[nb]] + [line(lane[nb - s], -s) for s in range(1, chips)]
    tokens_grad = pl.pallas_call(
        functools.partial(last_kernel, chips),
        in_specs=vmem(chips + 3),
        out_specs=vmem(1)[0],
        out_shape=shape((T, D), F32),
        compiler_params=params(),
        name="last",
    )(*one_parts, tokens, gain1, mid_grad)

    mix_parts = scatter_ep(mix)
    layer_out = mid
    for part in mix_parts:
        layer_out = layer_out + part.astype(F32)
    layer_out = layer_out.astype(BF)

    def reduce_rep(x):
        total = lax.dynamic_index_in_dim(x, r, 0, keepdims=False).astype(F32)
        for s in range(1, R):
            total += cross(lax.dynamic_index_in_dim(x, r ^ s, 0, keepdims=False), s).astype(F32)
        return total

    def reduce_z(x):
        total = lax.dynamic_index_in_dim(x, z, 0, keepdims=False).astype(F32)
        for s in range(1, Z):
            total += ring(lax.dynamic_index_in_dim(x, (z + s) % Z, 0, keepdims=False), s).astype(F32)
        return total

    wo_part = tn(attended, attn_grad).astype(BF)
    wo_mine, wo_other = ordered(wo_part[:, :half], wo_part[:, half:])
    wo_lane = wo_mine + swap(wo_other)
    n_chip = R * Z
    ext = jnp.concatenate(
        [
            gain1_part[0].reshape(n_chip, hrow),
            gain2_part[0].reshape(n_chip, hrow),
            rgrad[:experts].reshape(experts, n_chip, hrow).transpose(1, 0, 2).reshape(n_chip, experts * hrow),
        ],
        axis=1,
    ).astype(BF)
    ext = jnp.pad(ext, ((0, 0), (0, -ext.shape[1] % half))).reshape(n_chip, -1, half)
    dense = jnp.concatenate([grads, wo_lane[None]]).reshape(4, n_chip, hrow, half).transpose(1, 0, 2, 3)
    dense = jnp.concatenate([dense.reshape(n_chip, 4 * hrow, half), ext], axis=1)
    dense = reduce_rep(dense.reshape((R, Z) + dense.shape[1:])).astype(BF)
    dense = reduce_z(dense)
    mats = dense[: 4 * hrow].reshape(4, 2, wrow, half)
    mats_mine, mats_other = ordered(mats[:, 0], mats[:, 1])
    ext = dense[4 * hrow :]
    got = swap(jnp.concatenate([mats_other.reshape(4 * wrow, half), ext], axis=0).astype(BF)).astype(F32)
    left, right = ordered(mats_mine, got[: 4 * wrow].reshape(4, wrow, half))
    mats = jnp.concatenate([left, right], axis=2)
    ext = (ext + got[4 * wrow :]).reshape(-1)[: (2 + experts) * hrow].reshape(2 + experts, 2, wrow)
    ext = jnp.where(is0, ext[:, 0], ext[:, 1])

    sgu = reduce_rep(sgu_grad.reshape(R, D // R, 2 * fs)).astype(BF)
    sd_sum = reduce_rep(sd_grad.reshape(R, drow, D))
    sgu = lax.all_to_all(sgu.reshape(E, wrow, 2 * fs), "ep", split_axis=0, concat_axis=0, tiled=True)

    def units_back(x):
        return x.astype(F32).reshape(E, wrow, R, drow).transpose(1, 2, 0, 3).reshape(wrow, FF)

    return (
        layer_out,
        tokens_grad,
        ext[0],
        mats[0],
        mats[1],
        mats[2],
        mats[3],
        ext[1],
        ext[2:].T,
        units_back(sgu[:, :, :fs]),
        units_back(sgu[:, :, fs:]),
        sd_sum,
        gu_sum[0, 0][None].astype(F32),
        gu_sum[0, 1][None].astype(F32),
        dn_sum.T[None].astype(F32),
    )


def solution(mesh):
    rows = P(("rep", "ep"), None)
    flat = P(("rep", "ep"))
    expert = P("ep", None, None)
    expert_out = P("ep", None, "rep")
    return jax.shard_map(
        functools.partial(shards, mesh.shape["rep"], mesh.shape["ep"]),
        mesh=mesh,
        in_specs=(rows, P("rep", "ep"), rows, flat, rows, rows, rows, rows, flat)
        + (rows,) * 4
        + (expert,) * 3
        + (rows,),
        out_specs=(rows, rows, flat, rows, rows, rows, rows, flat)
        + (rows,) * 4
        + (expert_out,) * 3,
        check_vma=False,
    )
```

```python
import functools
import math

import jax
import jax.numpy as jnp
from jax import lax
from jax.experimental import pallas as pl
from jax.experimental.pallas import tpu as pltpu
from jax.sharding import PartitionSpec as P

HEADS = 12
EPSILON = 1e-06
NEG_LARGE = -1e30
BF = jnp.bfloat16
F32 = jnp.float32
VMEM_LIMIT = 58 * 1024 * 1024


def nn(a, b):
    return lax.dot_general(a, b, (((1,), (0,)), ((), ())), preferred_element_type=F32)


def nt(a, b):
    return lax.dot_general(a, b, (((1,), (1,)), ((), ())), preferred_element_type=F32)


def tn(a, b):
    return lax.dot_general(a, b, (((0,), (0,)), ((), ())), preferred_element_type=F32)


def rms_scale(values):
    return lax.rsqrt(jnp.mean(values * values, axis=1, keepdims=True) + EPSILON)


def lanes(shape):
    return lax.broadcasted_iota(jnp.int32, shape, len(shape) - 1)


def turned(x):
    front = lanes(x.shape) % 64 < 32
    return jnp.where(front, -pltpu.roll(x, 96, 1), pltpu.roll(x, 32, 1))


def vmem(n):
    return [pl.BlockSpec(memory_space=pltpu.VMEM)] * n


def params(**kw):
    return pltpu.CompilerParams(vmem_limit_bytes=VMEM_LIMIT, **kw)


def cost(micros):
    return pl.CostEstimate(flops=int(micros * 1.1e9), bytes_accessed=int(micros * 1e5), transcendentals=0)


def after(x, *deps):
    return lax.optimization_barrier((x,) + deps)[0]


def whole(shape):
    return pl.BlockSpec(shape, lambda *_: (0,) * len(shape))


def qkv_kernel(chips, rows, c_ref, *refs):
    own, par = refs[:chips], refs[chips : 2 * chips]
    wq, wk, wv, cos, sin, gain, h1, keys, vals, quer = refs[2 * chips :]
    c = c_ref[0]
    pairs = keys.shape[0]
    scale = 0.125
    for s in range(chips):
        for p, src in ((0, own[s]), (1, par[s])):
            core = c if p == 0 else 1 - c
            slot = 2 * (chips - 1 - s) + core
            x = src[0:rows, :].astype(F32)
            h = (x * rms_scale(x) * gain[...]).astype(BF)
            h1[slot] = h
            co, si = cos[slot], sin[slot]
            k = nn(h, wk[...])
            v = nn(h, wv[...])
            for i in range(pairs):
                kp = k[:, 128 * i : 128 * i + 128]
                keys[i, slot] = (kp * co + turned(kp) * si).astype(BF)
                vals[i, slot] = v[:, 128 * i : 128 * i + 128].astype(BF)
            if s == 0:
                q = nn(h, wq[...])
                for i in range(pairs):
                    qp = q[:, 128 * i : 128 * i + 128]
                    quer[i, core] = ((qp * co + turned(qp) * si) * scale).astype(BF)


def attend_kernel(first, count, rows, q_ref, k_ref, v_ref, sq_ref, sk_ref, o_ref, ol_ref, lse_ref, s_scr):
    low = lanes((rows, 128)) < 64
    for qi in range(2):
        qpair = q_ref[0, qi * rows : (qi + 1) * rows, :]
        sq = sq_ref[qi * rows : (qi + 1) * rows, 0:1]
        outs, lses = [], []
        for hh in range(2):
            keep = low if hh == 0 else jnp.logical_not(low)
            q = jnp.where(keep, qpair, jnp.zeros_like(qpair))
            m = jnp.full((rows, 128), NEG_LARGE, F32)
            for j in range(count):
                at = (first + qi + j) * rows
                s = nt(q, k_ref[0, at : at + rows, :])
                s = jnp.where(sq == sk_ref[0:1, at : at + rows], s, NEG_LARGE)
                s_scr[:, j * rows : (j + 1) * rows] = s
                for g in range(rows // 128):
                    m = jnp.maximum(m, s[:, g * 128 : (g + 1) * 128])
            m = jnp.max(m, axis=1, keepdims=True)
            total = jnp.zeros((rows, 128), F32)
            acc = jnp.zeros((rows, 128), F32)
            for j in range(count):
                at = (first + qi + j) * rows
                e = jnp.exp(s_scr[:, j * rows : (j + 1) * rows] - m)
                for g in range(rows // 128):
                    total = total + e[:, g * 128 : (g + 1) * 128]
                acc = acc + nn(e.astype(BF), v_ref[0, at : at + rows, :])
            total = jnp.sum(total, axis=1, keepdims=True)
            outs.append(acc / total)
            lses.append(m + jnp.log(total))
        o = jnp.where(low, outs[0], outs[1])
        o_ref[0, qi * rows : (qi + 1) * rows, :] = o
        ol_ref[0, qi * rows : (qi + 1) * rows, :] = o.astype(BF)
        both = jnp.where(lanes((rows, 128)) == 0, lses[0], lses[1])
        lse_ref[0, :, qi * rows : (qi + 1) * rows] = both.T[0:8, :]


def mid_kernel(a_ref, w_ref, x_ref, g_ref, mid_ref, h_ref):
    mid = x_ref[...].astype(F32) + nn(a_ref[...], w_ref[...])
    mid_ref[...] = mid
    h_ref[...] = (mid * rms_scale(mid) * g_ref[...]).astype(BF)


def pre_kernel(nblk, rows, ix, og, p_ref, wd, dehid, ogx_t, ogx):
    cap = p_ref.shape[1]

    @pl.when(pl.program_id(0) == 0)
    def _():
        for b in range(nblk):
            block = og[ix[b], 0:rows, :]
            ogx[b * cap : (b + 1) * cap, :] = nn(p_ref[ix[b]], block).astype(BF)
        ogx_t[...] = ogx[...].T

    dehid[...] = nt(ogx[...], wd[...]).astype(BF)


def act(g, u, dh):
    s = jax.nn.sigmoid(g)
    silu = g * s
    hid = (silu * u).astype(BF)
    dg = (dh * u * (s * (1.0 + g * (1.0 - s)))).astype(BF)
    du = (dh * silu).astype(BF)
    return hid, dg, du


def split_nn(a, col):
    wide = jnp.broadcast_to(col, (col.shape[0], 128))
    high = wide.astype(BF)
    return nn(a, high) + nn(a, (wide - high.astype(F32)).astype(BF))


def expert_kernel(nblk, rows, experts, e_ref, ix, *refs):
    g_refs = refs[:nblk]
    (p_ref, pt_ref, wr, wr_t, wsg, wsu, wsd, og, wg, wu, dehid) = refs[nblk : nblk + 11]
    (x_out, ehid, degate, deup, gate_slot, gate_tok, shid, dsg, dsu, tg, tg_far, rgrad) = refs[
        nblk + 11 : nblk + 23
    ]
    x_scr, row_scr, tg_scr, pg_scr, prob_scr, gs_scr = refs[nblk + 23 :]
    cap = p_ref.shape[1]
    step = pl.program_id(0)
    own = lanes((rows, 128)) == e_ref[0]

    @pl.when(step == 0)
    def _():
        row_scr[...] = jnp.zeros_like(row_scr)
        pg_scr[...] = jnp.zeros_like(pg_scr)
        for b in range(nblk):
            block = g_refs[b][...]
            x = nn(p_ref[ix[b]], block).astype(BF)
            x_scr[b * cap : (b + 1) * cap, :] = x
            x_out[b * cap : (b + 1) * cap, :] = x
            logits = jnp.where(lanes((rows, 128)) < experts, nn(block, wr[...]), NEG_LARGE)
            shifted = jnp.exp(logits - jnp.max(logits, axis=1, keepdims=True))
            probs = shifted / jnp.sum(shifted, axis=1, keepdims=True)
            prob_scr[b] = probs
            gate = jnp.sum(jnp.where(own, probs, 0.0), axis=1, keepdims=True)
            gate_tok[b] = jnp.broadcast_to(gate, (rows, 128))
            slot = split_nn(p_ref[ix[b]], gate)
            gs_scr[b * cap : (b + 1) * cap, :] = slot
            gate_slot[b * cap : (b + 1) * cap, :] = slot
            at = b * rows
            dsh = nt(og[ix[b], 0:rows, :], wsd[...])
            hid, dg, du = act(nn(block, wsg[...]), nn(block, wsu[...]), dsh)
            shid[at : at + rows, :] = hid
            dsg[at : at + rows, :] = dg
            dsu[at : at + rows, :] = du
            tg_scr[at : at + rows, :] = nt(dg, wsg[...]) + nt(du, wsu[...])

    raw = dehid[...].astype(F32)
    hid, dg, du = act(nn(x_scr[...], wg[0]), nn(x_scr[...], wu[0]), raw * gs_scr[:, 0:1])
    ehid[...] = hid
    degate[...] = dg
    deup[...] = du
    row_scr[...] += nt(dg, wg[0]) + nt(du, wu[0])
    pg_scr[...] += jnp.sum(hid.astype(F32) * raw, axis=1, keepdims=True)

    @pl.when(step == pl.num_programs(0) - 1)
    def _():
        total = jnp.zeros_like(rgrad)
        for b in range(nblk):
            at = b * rows
            pg = split_nn(pt_ref[ix[b]], pg_scr[b * cap : (b + 1) * cap, 0:1])
            probs = prob_scr[b]
            gate = jnp.sum(jnp.where(own, probs, 0.0), axis=1, keepdims=True)
            lgrad = (pg * probs * (own.astype(F32) - gate)).astype(BF)
            total += tn(lgrad, g_refs[b][...])
            back = nn(pt_ref[ix[b]], row_scr[b * cap : (b + 1) * cap, :].astype(BF))
            (tg_far if b % 2 else tg)[b // 2] = (tg_scr[at : at + rows, :] + back + nn(lgrad, wr_t[...])).astype(BF)
        rgrad[...] = total


def wgrad_kernel(per, r_ref, x_ref, degate, deup, gate_near, gate_far, up_near, up_far, x_t):
    step = pl.program_id(0)

    @pl.when(step == 0)
    def _():
        x_t[...] = x_ref[...].T

    @pl.when(step < 2 * per)
    def _():
        gate_near[0] = nn(x_t[...], degate[...]).astype(BF)
        up_near[0] = nn(x_t[...], deup[...]).astype(BF)

    @pl.when(step >= 2 * per)
    def _():
        gate_far[0] = nn(x_t[...], degate[...]).astype(BF)
        up_far[0] = nn(x_t[...], deup[...]).astype(BF)


def wgrad_all_kernel(r_ref, x_ref, degate, deup, gate, up, x_t):
    @pl.when(pl.program_id(0) == 0)
    def _():
        x_t[...] = x_ref[...].T

    gate[0] = nn(x_t[...], degate[...]).astype(BF)
    up[0] = nn(x_t[...], deup[...]).astype(BF)


def down_grad_kernel(ogx_t, gate_slot, ehid, dn):
    dn[...] = nn(ogx_t[...], (ehid[...].astype(F32) * gate_slot[:, 0:1]).astype(BF)).astype(BF)


def result_kernel(nblk, rows, ix, *refs):
    g_refs = refs[:nblk]
    og, pt_ref, gate_tok, shid, dsg, dsu, wsd, ehid, wd, mix, sgu, sd, acc = refs[nblk:]
    cap = pt_ref.shape[2]
    step = pl.program_id(0)

    @pl.when(step == 0)
    def _():
        acc[...] = jnp.zeros_like(acc)
        dg_sum = jnp.zeros((sgu.shape[0], dsg.shape[1]), F32)
        du_sum = jnp.zeros_like(dg_sum)
        sd_sum = jnp.zeros(sd.shape, F32)
        for b in range(nblk):
            at = b * rows
            g_t = g_refs[b][...].T
            dg_sum += nn(g_t, dsg[at : at + rows, :])
            du_sum += nn(g_t, dsu[at : at + rows, :])
            sd_sum += tn(shid[at : at + rows, :], og[ix[b], 0:rows, :])
        width = dsg.shape[1]
        sgu[:, :width] = dg_sum.astype(BF)
        sgu[:, width:] = du_sum.astype(BF)
        sd[...] = sd_sum.astype(BF)

    acc[...] += nn(ehid[...], wd[0])

    @pl.when(step == pl.num_programs(0) - 1)
    def _():
        for b in range(nblk):
            at = b * rows
            res = acc[b * cap : (b + 1) * cap, :].astype(BF)
            picked = nn(pt_ref[ix[b]], res) * gate_tok[b][:, 0:1]
            mix[ix[b]] = (picked + nn(shid[at : at + rows, :], wsd[...])).astype(BF)


def mid_back_kernel(count, *refs):
    pieces = refs[:count]
    mid_ref, g_ref, og_ref, w_ref, mg_ref, ag_ref, da_ref, gg_ref = refs[count:]
    two = pieces[0][...].astype(F32)
    for piece in pieces[1:]:
        two += piece[...].astype(F32)
    mid = mid_ref[...]
    scale = rms_scale(mid)
    mn = mid * scale
    gg_ref[...] = jnp.broadcast_to(jnp.sum(two * mn, axis=0, keepdims=True), gg_ref.shape)
    dn = two * g_ref[...]
    mg = og_ref[...].astype(F32) + scale * (dn - mn * jnp.mean(dn * mn, axis=1, keepdims=True))
    mg_ref[...] = mg
    ag = mg.astype(BF)
    ag_ref[...] = ag
    da = nt(ag, w_ref[...]).astype(BF)
    for i in range(da_ref.shape[0]):
        da_ref[i] = da[:, 128 * i : 128 * i + 128]


def attend_back_kernel(first, count, rows, q_ref, k_ref, v_ref, o_ref, do_ref, lse_ref, sq_ref, sk_ref, cos, sin,
                       h1_ref, wq, wk, wv, gain, c_ref, grads, og_own, og_far, gg, h1_t, k_t, dk, dv, og_scr):
    step = pl.program_id(0)
    low = lanes((rows, 128)) < 64
    kv_rows = k_ref.shape[1]
    base = kv_rows - 2 * rows

    @pl.when(step == 0)
    def _():
        h1_t[...] = h1_ref[...].T
        og_scr[...] = jnp.zeros_like(og_scr)

    k_t[...] = k_ref[0].T
    dk[...] = jnp.zeros_like(dk)
    dv[...] = jnp.zeros_like(dv)
    dqs = []
    for qi in range(2):
        at_q = qi * rows
        qpair = q_ref[0, at_q : at_q + rows, :]
        dopair = do_ref[0, at_q : at_q + rows, :]
        prod = dopair.astype(F32) * o_ref[0, at_q : at_q + rows, :]
        d0 = jnp.sum(jnp.where(low, prod, 0.0), axis=1, keepdims=True)
        d1 = jnp.sum(jnp.where(low, 0.0, prod), axis=1, keepdims=True)
        delta = jnp.where(lanes((rows, 128)) == 0, d0, d1).T
        sq = sq_ref[0:1, at_q : at_q + rows]
        halves = []
        for hh in range(2):
            keep = low if hh == 0 else jnp.logical_not(low)
            q = jnp.where(keep, qpair, jnp.zeros_like(qpair))
            do = jnp.where(keep, dopair, jnp.zeros_like(dopair))
            lse_row = lse_ref[0, hh : hh + 1, at_q : at_q + rows]
            delta_row = delta[hh : hh + 1, :]
            dq = jnp.zeros((64, rows), F32)
            for j in range(count):
                at = (first + qi + j) * rows
                same = sk_ref[at : at + rows, 0:1] == sq
                s = nt(k_ref[0, at : at + rows, :], q)
                p = jnp.where(same, jnp.exp(s - lse_row), 0.0)
                dp = nt(v_ref[0, at : at + rows, :], do)
                ds = (p * (dp - delta_row)).astype(BF)
                dv[at : at + rows, :] += nn(p.astype(BF), do)
                dk[at : at + rows, :] += nn(ds, q)
                dq += nn(k_t[64 * hh : 64 * hh + 64, at : at + rows], ds)
            halves.append(dq)
        dq = jnp.concatenate(halves, axis=0).T * 0.125
        at = base + at_q
        dq = dq * cos[at : at + rows, :] - turned(dq) * sin[at : at + rows, :]
        dqs.append(dq.astype(BF))
    dq = jnp.concatenate(dqs, axis=0)
    dkv = dk[...]
    dkb = (dkv * cos[...] - turned(dkv) * sin[...]).astype(BF)
    dvb = dv[...].astype(BF)
    grads[0] = nn(h1_t[:, base:], dq).astype(BF)
    grads[1] = nn(h1_t[...], dkb).astype(BF)
    grads[2] = nn(h1_t[...], dvb).astype(BF)
    og_scr[...] += nt(dkb, wk[...]) + nt(dvb, wv[...])
    og_scr[base:, :] += nt(dq, wq[...])

    @pl.when(step == pl.num_programs(0) - 1)
    def _():
        one = og_scr[...]
        for slot in range(kv_rows // rows):
            block = one[slot * rows : (slot + 1) * rows, :].astype(BF)

            @pl.when(c_ref[0] == slot % 2)
            def _():
                og_own[slot // 2] = block

            @pl.when(c_ref[0] != slot % 2)
            def _():
                og_far[slot // 2] = block

        total = jnp.sum(one * h1_ref[...].astype(F32), axis=0, keepdims=True) / gain[...]
        gg[...] = jnp.broadcast_to(total, gg.shape)


def last_kernel(count, *refs):
    pieces = refs[:count]
    x_ref, g_ref, mg_ref, out = refs[count:]
    one = pieces[0][...].astype(F32)
    for piece in pieces[1:]:
        one += piece[...].astype(F32)
    x = x_ref[...].astype(F32)
    scale = rms_scale(x)
    xn = x * scale
    dn = one * g_ref[...]
    out[...] = mg_ref[...] + scale * (dn - xn * jnp.mean(dn * xn, axis=1, keepdims=True))


def shape(dims, dtype=BF):
    return jax.ShapeDtypeStruct(dims, dtype)


def shards(
    R,
    E,
    tokens,
    segment_ids,
    routes,
    norm1_gain,
    w_query,
    w_key,
    w_value,
    w_out,
    norm2_gain,
    w_router,
    shared_gate,
    shared_up,
    shared_down,
    expert_gate,
    expert_up,
    expert_down,
    out_grad,
):
    Z = E // 2
    T, D = tokens.shape
    FF = shared_gate.shape[1]
    topk = routes.shape[1]
    experts = w_router.shape[1]
    assert expert_gate.shape[0] == 1 and experts == E
    half = D // 2
    pairs = half // 128
    wrow = w_query.shape[0]
    hrow = 2 * wrow
    cap = 2 * T * topk // experts
    slots = E * cap
    fs = FF // E
    drow = shared_down.shape[0]
    longest = E * T // 2
    back = -(-(longest - 1) // T)
    nb = -(-back // 2)
    chips = nb + 1
    kvb = 2 * chips
    first = 2 * nb - back
    count = back + 1
    r = lax.axis_index("rep")
    e = lax.axis_index("ep")
    z, c = e // 2, e % 2
    is0 = c == 0
    c_arr = jnp.reshape(c, (1,)).astype(jnp.int32)
    e_arr = jnp.reshape(e, (1,)).astype(jnp.int32)

    def swap(x):
        return lax.ppermute(x, "ep", [(i, i ^ 1) for i in range(E)])

    def ring(x, s):
        return lax.ppermute(x, "ep", [(i, (i + 2 * s) % E) for i in range(E)])

    def line(x, s):
        return lax.ppermute(x, "ep", [(i, i + 2 * s) for i in range(E) if 0 <= i + 2 * s < E])

    def cross(x, s):
        return lax.ppermute(x, "rep", [(i, i ^ s) for i in range(R)])

    def ordered(mine, other):
        return jnp.where(is0, mine, other), jnp.where(is0, other, mine)

    def put(buf, x, i):
        return lax.dynamic_update_index_in_dim(buf, x, i, 0)

    def chip_pack(mats, extra):
        stacked = jnp.stack(mats).reshape(len(mats) * wrow, D)
        mine, other = ordered(stacked[:, :half], stacked[:, half:])
        ext = jnp.pad(extra.reshape(1, -1), ((0, 0), (0, half - extra.size)))
        got = swap(jnp.concatenate([other, ext], axis=0))
        a, b = ordered(mine, got[:-1])
        ea, eb = ordered(ext, got[-1:])
        rows = jnp.stack([a.reshape(-1, wrow, half), b.reshape(-1, wrow, half)], axis=1).reshape(-1, half)
        rows = jnp.concatenate([rows, ea, eb], axis=0)
        return jnp.pad(rows, ((0, -rows.shape[0] % 16), (0, 0)))

    def gather_z(pack):
        buf = put(jnp.zeros((Z,) + pack.shape, BF), pack, z)
        for s in range(1, Z):
            buf = put(buf, ring(pack, s), (z - s) % Z)
        return buf

    def gather_rep(part, *deps):
        got = [cross(part, s) for s in range(1, R)]
        if deps:
            got = [after(x, *deps) for x in got]
        buf = put(jnp.zeros((R,) + part.shape, BF), part, r)
        for s in range(1, R):
            buf = put(buf, got[s - 1], r ^ s)
        return buf

    def unpack(full, i):
        return full[:, :, i * hrow : (i + 1) * hrow, :].reshape(D, half)

    pack = chip_pack(
        [w_query, w_key, w_value, w_out], jnp.concatenate([norm1_gain, norm2_gain, w_router.reshape(-1)])
    )
    part = gather_z(pack)
    full = gather_rep(part)
    wq, wk, wv, wo_half = (unpack(full, i) for i in range(4))
    ext = full[:, :, 4 * hrow : 4 * hrow + 2, :].reshape(R * E, half)
    gain1 = ext[:, :wrow].reshape(1, D).astype(F32)
    gain2 = ext[:, wrow : 2 * wrow].reshape(1, D).astype(F32)
    router = ext[:, 2 * wrow : (2 + experts) * wrow].reshape(D, experts)
    router = jnp.pad(router, ((0, 0), (0, 128 - experts)))
    router_t = router.T

    seg_row = jnp.pad(segment_ids.reshape(1, T).astype(BF), ((0, 7), (0, D - T)))
    tok_pack = after(jnp.concatenate([tokens, seg_row], axis=0), pack)
    own_tok = [tok_pack] + [line(tok_pack, s) for s in range(1, chips)]
    par_tok = [swap(x) for x in own_tok]

    seg_blocks = [None] * kvb
    for s in range(chips):
        valid = z - s >= 0
        a, b = ordered(own_tok[s][T, :T], par_tok[s][T, :T])
        seg_blocks[2 * (nb - s)] = jnp.where(valid, a.astype(F32), -1.0)
        seg_blocks[2 * (nb - s) + 1] = jnp.where(valid, b.astype(F32), -1.0)
    segs = jnp.stack(seg_blocks)
    kv_rows = kvb * T
    seg_flat = segs.reshape(1, kv_rows)
    seg_wide = jnp.broadcast_to(segs.reshape(kv_rows, 1), (kv_rows, 128))

    inverse = jnp.exp(jnp.arange(32).astype(F32) * (-2.0 * math.log(10000.0) / 64))
    inverse = jnp.tile(inverse, 4)
    places = after((z - nb) * (2 * T) + jnp.arange(kv_rows, dtype=jnp.int32), pack)
    angle = places.astype(F32)[:, None] * inverse[None, :]
    cos, sin = lax.optimization_barrier((jnp.cos(angle), jnp.sin(angle)))
    cos, sin = cos.reshape(kvb, T, 128), sin.reshape(kvb, T, 128)

    h1, keys, vals, quer = pl.pallas_call(
        functools.partial(qkv_kernel, chips, T),
        in_specs=[pl.BlockSpec(memory_space=pltpu.SMEM)] + vmem(2 * chips + 6),
        out_specs=tuple(vmem(4)),
        out_shape=(
            shape((kvb, T, D)),
            shape((pairs, kvb, T, 128)),
            shape((pairs, kvb, T, 128)),
            shape((pairs, 2, T, 128)),
        ),
        compiler_params=params(),
        name="qkv",
        cost_estimate=cost(8),
    )(c_arr, *own_tok, *par_tok, wq, wk, wv, cos, sin, gain1)
    h1 = h1.reshape(kv_rows, D)
    keys = keys.reshape(pairs, kv_rows, 128)
    vals = vals.reshape(pairs, kv_rows, 128)
    quer = quer.reshape(pairs, 2 * T, 128)

    og_pack = jnp.concatenate(
        [out_grad, jnp.pad(routes.reshape(1, topk * T).astype(BF), ((0, 7), (0, D - topk * T)))], axis=0
    )
    og_all = lax.all_gather(after(og_pack, pack), "ep", axis=0)
    ix_arr = jnp.stack([((z - b // 2) % Z) * 2 + (c ^ (b % 2)) for b in range(E)]).astype(jnp.int32)

    wo = jnp.concatenate(ordered(wo_half, swap(wo_half)), axis=1)

    def by_unit(w):
        return w.reshape(wrow, R, E, drow).transpose(2, 0, 1, 3).reshape(E, wrow, fs)

    gu = jnp.concatenate([by_unit(shared_gate), by_unit(shared_up)], axis=2)
    gu = lax.all_to_all(after(gu, part), "ep", split_axis=0, concat_axis=0, tiled=True).reshape(E * wrow, 2 * fs)
    gu = after(gu, keys)
    wide = D // fs
    shared = jnp.concatenate(
        [gu[:, :fs], gu[:, fs:]] + [shared_down[:, k * fs : (k + 1) * fs] for k in range(wide)], axis=0
    )
    shared_got = [cross(shared, s) for s in range(1, R)]
    one = lambda *dims: pl.BlockSpec((1,) + dims, lambda i: (i, 0, 0))
    att, att_low, lse = pl.pallas_call(
        functools.partial(attend_kernel, first, count, T),
        grid=(pairs,),
        in_specs=[
            one(2 * T, 128),
            one(kv_rows, 128),
            one(kv_rows, 128),
            whole((2 * T, 128)),
            whole((1, kv_rows)),
        ],
        out_specs=(one(2 * T, 128), one(2 * T, 128), one(8, 2 * T)),
        out_shape=(
            shape((pairs, 2 * T, 128), F32),
            shape((pairs, 2 * T, 128)),
            shape((pairs, 8, 2 * T), F32),
        ),
        scratch_shapes=[pltpu.VMEM((T, count * T), F32)],
        compiler_params=params(),
        name="attend",
        cost_estimate=cost(10),
    )(after(quer, wo, shared), keys, vals, seg_wide[-2 * T :], seg_flat)

    def joined(mine, other):
        both = jnp.where(is0, jnp.concatenate([mine, other]), jnp.concatenate([other, mine]))
        return both.transpose(1, 0, 2).reshape(T, D)

    att_own, att_other = ordered(att_low[:, :T], att_low[:, T:])
    attended = joined(att_own, swap(att_other))
    mid, h2 = pl.pallas_call(
        mid_kernel,
        in_specs=vmem(4),
        out_specs=tuple(vmem(2)),
        out_shape=(shape((T, D), F32), shape((T, D))),
        compiler_params=params(),
        name="mid",
        cost_estimate=cost(3),
    )(attended, wo, tokens, gain2)

    shared_got = [after(x, h2) for x in shared_got]
    shared = put(jnp.zeros((R,) + shared.shape, BF), after(shared, h2), r)
    for i in range(1, R):
        shared = put(shared, shared_got[i - 1], r ^ i)
    gr = E * wrow
    wsg = shared[:, :gr].reshape(D, fs)
    wsu = shared[:, gr : 2 * gr].reshape(D, fs)
    wsd = jnp.concatenate(
        [shared[:, 2 * gr + k * drow : 2 * gr + (k + 1) * drow].reshape(fs, fs) for k in range(wide)], axis=1
    )
    h2_lane = [h2] + [ring(h2, s) for s in range(1, Z)]

    def both_cores(lane):
        blocks = []
        for item in lane:
            blocks += [item, swap(item)]
        return blocks

    og_all = after(og_all, h2)
    table = og_all[:, T, : topk * T].reshape(E, T, topk)
    hit = jnp.any(table == e.astype(F32).astype(BF), axis=2).astype(F32)
    rank = jnp.cumsum(hit, axis=1) - hit
    rank = jnp.where(hit > 0, rank, -1.0)
    slot_ids = jnp.arange(cap).astype(F32)
    pick = (rank[:, None, :] == slot_ids[None, :, None]).astype(BF)
    pick_t = (rank[:, :, None] == slot_ids[None, None, :]).astype(BF)

    smem = pl.BlockSpec(memory_space=pltpu.SMEM)
    ft = min(256, FF // R)
    steps = FF // ft
    per = FF // R // ft
    col = lambda n: pl.BlockSpec((n, ft), lambda i: (0, i))
    wcol = pl.BlockSpec((1, D, ft), lambda i: (0, 0, i))
    wdn = pl.BlockSpec((1, ft, D), lambda i: (0, i, 0))
    dehid, ogx_t = pl.pallas_call(
        functools.partial(pre_kernel, E, T),
        grid=(steps,),
        in_specs=[smem, whole((E, T + 8, D))]
        + [whole((E, cap, T)), pl.BlockSpec((ft, D), lambda i: (i, 0))],
        out_specs=(col(slots), whole((D, slots))),
        out_shape=(shape((slots, FF)), shape((D, slots))),
        scratch_shapes=[pltpu.VMEM((slots, D), BF)],
        compiler_params=params(),
        name="pre",
        cost_estimate=cost(12),
    )(ix_arr, og_all, pick, expert_down.reshape(FF, D))

    h2_blocks = both_cores([after(x, dehid) for x in h2_lane])
    (x_rows, ehid, degate, deup, gate_slot, gate_tok, shid, dsg, dsu, tg, tg_far, rgrad) = pl.pallas_call(
        functools.partial(expert_kernel, E, T, experts),
        grid=(steps,),
        in_specs=[smem, smem]
        + [whole((T, D))] * E
        + [
            whole((E, cap, T)),
            whole((E, T, cap)),
            whole((D, 128)),
            whole((128, D)),
            whole((D, fs)),
            whole((D, fs)),
            whole((fs, D)),
            whole((E, T + 8, D)),
            wcol,
            wcol,
            col(slots),
        ],
        out_specs=(
            whole((slots, D)),
            col(slots),
            col(slots),
            col(slots),
            whole((slots, 128)),
            whole((E, T, 128)),
            whole((E * T, fs)),
            whole((E * T, fs)),
            whole((E * T, fs)),
            whole((Z, T, D)),
            whole((Z, T, D)),
            whole((128, D)),
        ),
        out_shape=(
            shape((slots, D)),
            shape((slots, FF)),
            shape((slots, FF)),
            shape((slots, FF)),
            shape((slots, 128), F32),
            shape((E, T, 128), F32),
            shape((E * T, fs)),
            shape((E * T, fs)),
            shape((E * T, fs)),
            shape((Z, T, D)),
            shape((Z, T, D)),
            shape((128, D), F32),
        ),
        scratch_shapes=[
            pltpu.VMEM((slots, D), BF),
            pltpu.VMEM((slots, D), F32),
            pltpu.VMEM((E * T, D), F32),
            pltpu.VMEM((slots, 128), F32),
            pltpu.VMEM((E, T, 128), F32),
            pltpu.VMEM((slots, 128), F32),
        ],
        compiler_params=params(),
        name="expert",
        cost_estimate=cost(38),
    )(e_arr, ix_arr, *h2_blocks, pick, pick_t, router, router_t, wsg, wsu, wsd, og_all, expert_gate, expert_up, dehid)

    def core_sums(mine, other, *deps):
        got = swap(other)
        if deps:
            got = after(got, *deps)
        return [mine[s] + got[s] for s in range(Z)]


    r_arr = jnp.reshape(r, (1,)).astype(jnp.int32)
    wide_rep = FF // R
    square = R == 4
    at0 = lambda n: pl.BlockSpec(n, lambda i, q: (0,) * len(n))
    dn_grad = pl.pallas_call(
        down_grad_kernel,
        grid=(steps,),
        in_specs=[whole((D, slots)), whole((slots, 128)), col(slots)],
        out_specs=col(D),
        out_shape=shape((D, FF)),
        compiler_params=params(),
        name="dgrad",
        cost_estimate=cost(10),
    )(ogx_t, gate_slot, ehid)
    dn_sum = lax.psum_scatter(dn_grad, "rep", scatter_dimension=0, tiled=True)
    lane = core_sums(tg, tg_far, dn_grad)
    two_parts = [lane[0]] + [ring(lane[s], -s) for s in range(1, Z)]

    if square:

        def rel_col(swapped):
            def index(i, q):
                d = i // per
                d = (d % 2) * 2 + d // 2 if swapped else d
                return (0, (d ^ q[0]) * per + i % per)

            return pl.BlockSpec((slots, ft), index)

        early = pl.BlockSpec(
            (1, D, ft),
            lambda i, q: (jnp.minimum(i // per, 1), 0, jnp.where(i < 2 * per, i % per, per - 1)),
        )
        late = pl.BlockSpec(
            (1, D, ft),
            lambda i, q: (jnp.maximum(i // per - 2, 0), 0, jnp.where(i < 2 * per, 0, i % per)),
        )
        gu_in = [rel_col(True), rel_col(False)]
        gu_specs = (early, late, early, late)
        gu_shapes = [(2, D, wide_rep)] * 4
        gu_kernel = functools.partial(wgrad_kernel, per)
    else:
        gu_in = [pl.BlockSpec((slots, ft), lambda i, q: (0, ((i // per) ^ q[0]) * per + i % per))] * 2
        gu_specs = (pl.BlockSpec((1, D, ft), lambda i, q: (i // per, 0, i % per)),) * 2
        gu_shapes = [(R, D, wide_rep)] * 2
        gu_kernel = wgrad_all_kernel
    gu_out = pl.pallas_call(
        gu_kernel,
        grid_spec=pltpu.PrefetchScalarGridSpec(
            num_scalar_prefetch=1,
            grid=(steps,),
            in_specs=[at0((slots, D))] + gu_in,
            out_specs=gu_specs,
            scratch_shapes=[pltpu.VMEM((D, slots), BF)],
        ),
        out_shape=tuple(shape(dims) for dims in gu_shapes),
        compiler_params=params(),
        name="wgrad",
        cost_estimate=cost(13),
    )(r_arr, after(x_rows, *lane), degate, deup)

    def pieces(x):
        return [lax.dynamic_index_in_dim(x, r ^ s, 0, keepdims=False) for s in range(R)]

    def direct(pieces, *deps):
        total = pieces[0].astype(F32)
        for d in range(1, R):
            got = cross(pieces[d], d)
            total += (after(got, *deps) if deps else got).astype(F32)
        return total

    two_parts[2::2] = [after(x, gu_out[0]) for x in two_parts[2::2]]
    near = []
    if square:
        gate_a, up_a = cross(gu_out[1][0], 1), cross(gu_out[3][0], 2)
    mix, sgu_grad, sd_grad = pl.pallas_call(
        functools.partial(result_kernel, E, T),
        grid=(steps,),
        in_specs=[smem]
        + [whole((T, D))] * E
        + [
            whole((E, T + 8, D)),
            whole((E, T, cap)),
            whole((E, T, 128)),
            whole((E * T, fs)),
            whole((E * T, fs)),
            whole((E * T, fs)),
            whole((fs, D)),
            col(slots),
            wdn,
        ],
        out_specs=(whole((E, T, D)), whole((D, 2 * fs)), whole((fs, D))),
        out_shape=(shape((E, T, D)), shape((D, 2 * fs)), shape((fs, D))),
        scratch_shapes=[pltpu.VMEM((slots, D), F32)],
        compiler_params=params(),
        name="result",
        cost_estimate=cost(19),
    )(ix_arr, *h2_blocks, og_all, pick_t, gate_tok, shid, dsg, dsu, wsd, after(ehid, gu_out[0], *two_parts[2::2], *near), expert_down)

    sgrad = jnp.concatenate(
        [sgu_grad[:, :fs].reshape(R, gr, fs), sgu_grad[:, fs:].reshape(R, gr, fs)]
        + [sd_grad[:, k * fs : (k + 1) * fs].reshape(R, drow, fs) for k in range(wide)],
        axis=1,
    )
    two_parts[1::2] = [after(x, mix) for x in two_parts[1::2]]
    if square:
        gate_a, up_a = after(gate_a, mix), after(up_a, mix)
        two_parts[0], gate_a, up_a = lax.optimization_barrier((two_parts[0], gate_a, up_a))
        gate_c, up_c = cross(after(gu_out[1][1], mix), 1), cross(after(gu_out[3][1], mix), 2)

    mix_in = after(mix, two_parts[1], *((gate_a, up_a) if square else ()))
    mix_sum = lax.psum_scatter(mix_in.reshape(E * T, D), "ep", scatter_dimension=0, tiled=True)

    mid_grad, attn_grad, att_grad, gain2_part = pl.pallas_call(
        functools.partial(mid_back_kernel, Z),
        in_specs=vmem(Z + 4),
        out_specs=tuple(vmem(4)),
        out_shape=(shape((T, D), F32), shape((T, D)), shape((2 * pairs, T, 128)), shape((8, D), F32)),
        compiler_params=params(),
        name="mid_back",
        cost_estimate=cost(4),
    )(*two_parts, mid, gain2, out_grad, wo)

    ag_own, ag_other = ordered(att_grad[:pairs], att_grad[pairs:])
    do_a, do_b = ordered(ag_own, swap(ag_other))
    do = jnp.concatenate([do_a, do_b], axis=1)
    wo_part = tn(attended, after(attn_grad, ag_other)).astype(BF)
    wo_mine, wo_other = ordered(wo_part[:, :half], wo_part[:, half:])
    wo_got = swap(wo_other)
    if square:
        gate_mid = gu_out[0][1] + after(gate_c, do)
        up_mid = gu_out[2][1] + after(up_c, do)
        gate_b, up_b = cross(gate_mid, 2), cross(up_mid, 1)
        sg_own, sg_near, sg_a, sg_c = pieces(after(sgrad, do))
        sg_send = jnp.stack([sg_a, sg_c])
        sg_got = cross(sg_send, 2)
        do, gate_mid, up_mid, wo_other, sg_send = lax.optimization_barrier(
            (do, gate_mid, up_mid, wo_other, sg_send)
        )

    cos2, sin2 = cos.reshape(kv_rows, 128), sin.reshape(kv_rows, 128)
    grads, og1, og1_far, gain1_part = pl.pallas_call(
        functools.partial(attend_back_kernel, first, count, T),
        grid=(pairs,),
        in_specs=[
            one(2 * T, 128),
            one(kv_rows, 128),
            one(kv_rows, 128),
            one(2 * T, 128),
            one(2 * T, 128),
            one(8, 2 * T),
            whole((1, 2 * T)),
            whole((kv_rows, 128)),
            whole((kv_rows, 128)),
            whole((kv_rows, 128)),
            whole((kv_rows, D)),
            pl.BlockSpec((D, 128), lambda i: (0, i)),
            pl.BlockSpec((D, 128), lambda i: (0, i)),
            pl.BlockSpec((D, 128), lambda i: (0, i)),
            whole((1, D)),
            smem,
        ],
        out_specs=(
            pl.BlockSpec((3, D, 128), lambda i: (0, 0, i)),
            whole((chips, T, D)),
            whole((chips, T, D)),
            whole((8, D)),
        ),
        out_shape=(shape((3, D, half)), shape((chips, T, D)), shape((chips, T, D)), shape((8, D), F32)),
        scratch_shapes=[
            pltpu.VMEM((D, kv_rows), BF),
            pltpu.VMEM((128, kv_rows), BF),
            pltpu.VMEM((kv_rows, 128), F32),
            pltpu.VMEM((kv_rows, 128), F32),
            pltpu.VMEM((kv_rows, D), F32),
        ],
        compiler_params=params(),
        name="attend_back",
        cost_estimate=cost(30),
    )(quer, keys, vals, att, do, lse, seg_flat[:, -2 * T :], seg_wide, cos2, sin2, h1, wq, wk, wv, gain1, c_arr)

    wo_got = after(wo_got, og1)
    if square:
        gate_b, up_b, sg_got = after(gate_b, og1), after(up_b, og1), after(sg_got, og1)
        og1_far, grads, gate_b, up_b, wo_got, sg_got = lax.optimization_barrier(
            (og1_far, grads, gate_b, up_b, wo_got, sg_got)
        )
    lane = og1 + swap(og1_far)
    one_parts = [lane[nb]] + [line(lane[nb - s], -s) for s in range(1, chips)]
    lane_all = one_parts[1:]

    def reduce_z(x):
        total = lax.dynamic_index_in_dim(x, z, 0, keepdims=False).astype(F32)
        for s in range(1, Z):
            total += ring(lax.dynamic_index_in_dim(x, (z + s) % Z, 0, keepdims=False), s).astype(F32)
        return total

    wo_lane = wo_mine + wo_got
    n_chip = R * Z
    ext = jnp.concatenate(
        [
            gain1_part[0].reshape(n_chip, hrow),
            gain2_part[0].reshape(n_chip, hrow),
            rgrad[:experts].reshape(experts, n_chip, hrow).transpose(1, 0, 2).reshape(n_chip, experts * hrow),
        ],
        axis=1,
    ).astype(BF)
    ext = jnp.pad(ext, ((0, 0), (0, -ext.shape[1] % half))).reshape(n_chip, -1, half)
    dense = jnp.concatenate([grads, wo_lane[None]]).reshape(4, n_chip, hrow, half).transpose(1, 0, 2, 3)
    dense = jnp.concatenate([dense.reshape(n_chip, 4 * hrow, half), ext], axis=1)
    dense = jnp.pad(dense, ((0, 0), (0, -dense.shape[1] % 8), (0, 0)))
    dense_rep = direct(pieces(dense.reshape((R, Z) + dense.shape[1:])), *lane_all).astype(BF)
    dense = reduce_z(dense_rep)
    mats = dense[: 4 * hrow].reshape(4, 2, wrow, half)
    mats_mine, mats_other = ordered(mats[:, 0], mats[:, 1])
    ext = dense[4 * hrow :]
    got = swap(jnp.concatenate([mats_other.reshape(4 * wrow, half), ext], axis=0).astype(BF)).astype(F32)
    left, right = ordered(mats_mine, got[: 4 * wrow].reshape(4, wrow, half))
    mats = jnp.concatenate([left, right], axis=2)
    ext = (ext + got[4 * wrow :]).reshape(-1)[: (2 + experts) * hrow].reshape(2 + experts, 2, wrow)
    ext = jnp.where(is0, ext[:, 0], ext[:, 1])

    if square:
        sg_mid = cross(after(sg_near + sg_got[1], *lane_all), 1)
        sgrad = sg_own.astype(F32) + sg_got[0].astype(F32) + after(sg_mid, dense_rep).astype(F32)
    else:
        sgrad = lax.psum_scatter(sgrad.reshape(-1, fs), "rep", scatter_dimension=0, tiled=True).astype(F32)
    sd_sum = jnp.concatenate(
        [sgrad[2 * gr + k * drow : 2 * gr + (k + 1) * drow] for k in range(wide)], axis=1
    )
    sgu = jnp.concatenate([sgrad[:gr], sgrad[gr : 2 * gr]], axis=1).astype(BF)
    sgu = after(sgu, dense_rep)
    sgu = lax.all_to_all(sgu.reshape(E, wrow, 2 * fs), "ep", split_axis=0, concat_axis=0, tiled=True)

    sgu = after(sgu, dense)

    def units_back(x):
        return x.astype(F32).reshape(E, wrow, R, drow).transpose(1, 2, 0, 3).reshape(wrow, FF)

    sg_sum, su_sum = units_back(sgu[:, :, :fs]), units_back(sgu[:, :, fs:])

    if square:
        gate_sum = gu_out[0][0].astype(F32) + (gate_a.astype(F32) + after(gate_b, dense_rep).astype(F32))
        up_sum = gu_out[2][0].astype(F32) + (up_a.astype(F32) + after(up_b, dense_rep).astype(F32))
    else:
        gate_sum, up_sum = (direct(x, dense_rep) for x in gu_out)
    dn_sum = after(dn_sum, dense_rep).T.astype(F32)
    layer_out = (mid + after(mix_sum, dense_rep).astype(F32)).astype(BF)

    done = [gate_sum, up_sum, dn_sum, layer_out, sd_sum, sg_sum, su_sum]
    one_parts[0], *done = lax.optimization_barrier((one_parts[0], *done))
    gate_sum, up_sum, dn_sum, layer_out, sd_sum, sg_sum, su_sum = done
    tokens_grad = pl.pallas_call(
        functools.partial(last_kernel, chips),
        in_specs=vmem(chips + 3),
        out_specs=vmem(1)[0],
        out_shape=shape((T, D), F32),
        compiler_params=params(),
        name="last",
        cost_estimate=cost(3),
    )(*one_parts, tokens, gain1, mid_grad)

    return (
        layer_out,
        tokens_grad,
        ext[0],
        mats[0],
        mats[1],
        mats[2],
        mats[3],
        ext[1],
        ext[2:].T,
        sg_sum,
        su_sum,
        sd_sum,
        gate_sum[None],
        up_sum[None],
        dn_sum[None],
    )


def solution(mesh):
    rows = P(("rep", "ep"), None)
    flat = P(("rep", "ep"))
    expert = P("ep", None, None)
    expert_out = P("ep", None, "rep")
    return jax.shard_map(
        functools.partial(shards, mesh.shape["rep"], mesh.shape["ep"]),
        mesh=mesh,
        in_specs=(rows, P("rep", "ep"), rows, flat, rows, rows, rows, rows, flat)
        + (rows,) * 4
        + (expert,) * 3
        + (rows,),
        out_specs=(rows, rows, flat, rows, rows, rows, rows, flat)
        + (rows,) * 4
        + (expert_out,) * 3,
        check_vma=False,
    )
```

```python
import functools
import math

import jax
import jax.numpy as jnp
from jax import lax
from jax.experimental import pallas as pl
from jax.experimental.pallas import tpu as pltpu
from jax.sharding import PartitionSpec as P

HEADS = 12
EPSILON = 1e-06
NEG_LARGE = -1e30
BF = jnp.bfloat16
F32 = jnp.float32
VMEM_LIMIT = 58 * 1024 * 1024


def nn(a, b):
    return lax.dot_general(a, b, (((1,), (0,)), ((), ())), preferred_element_type=F32)


def nt(a, b):
    return lax.dot_general(a, b, (((1,), (1,)), ((), ())), preferred_element_type=F32)


def tn(a, b):
    return lax.dot_general(a, b, (((0,), (0,)), ((), ())), preferred_element_type=F32)


def rms_scale(values):
    return lax.rsqrt(jnp.mean(values * values, axis=1, keepdims=True) + EPSILON)


def lanes(shape):
    return lax.broadcasted_iota(jnp.int32, shape, len(shape) - 1)


def turned(x):
    front = lanes(x.shape) % 64 < 32
    return jnp.where(front, -pltpu.roll(x, 96, 1), pltpu.roll(x, 32, 1))


def vmem(n):
    return [pl.BlockSpec(memory_space=pltpu.VMEM)] * n


def params(**kw):
    return pltpu.CompilerParams(vmem_limit_bytes=VMEM_LIMIT, **kw)


def cost(micros):
    return pl.CostEstimate(flops=int(micros * 1.1e9), bytes_accessed=int(micros * 1e5), transcendentals=0)


def after(x, *deps):
    return lax.optimization_barrier((x,) + deps)[0]


def whole(shape):
    return pl.BlockSpec(shape, lambda *_: (0,) * len(shape))


def qkv_kernel(chips, rows, c_ref, *refs):
    own, par = refs[:chips], refs[chips : 2 * chips]
    wq, wk, wv, cos, sin, gain, h1, keys, vals, quer = refs[2 * chips :]
    c = c_ref[0]
    pairs = keys.shape[0]
    scale = 0.125
    for s in range(chips):
        for p, src in ((0, own[s]), (1, par[s])):
            core = c if p == 0 else 1 - c
            slot = 2 * (chips - 1 - s) + core
            x = src[0:rows, :].astype(F32)
            h = (x * rms_scale(x) * gain[...]).astype(BF)
            h1[slot] = h
            co, si = cos[slot], sin[slot]
            k = nn(h, wk[...])
            v = nn(h, wv[...])
            for i in range(pairs):
                kp = k[:, 128 * i : 128 * i + 128]
                keys[i, slot] = (kp * co + turned(kp) * si).astype(BF)
                vals[i, slot] = v[:, 128 * i : 128 * i + 128].astype(BF)
            if s == 0:
                q = nn(h, wq[...])
                for i in range(pairs):
                    qp = q[:, 128 * i : 128 * i + 128]
                    quer[i, core] = ((qp * co + turned(qp) * si) * scale).astype(BF)


def attend_kernel(first, count, rows, q_ref, k_ref, v_ref, sq_ref, sk_ref, o_ref, ol_ref, lse_ref, s_scr):
    low = lanes((rows, 128)) < 64
    for qi in range(2):
        qpair = q_ref[0, qi * rows : (qi + 1) * rows, :]
        sq = sq_ref[qi * rows : (qi + 1) * rows, 0:1]
        outs, lses = [], []
        for hh in range(2):
            keep = low if hh == 0 else jnp.logical_not(low)
            q = jnp.where(keep, qpair, jnp.zeros_like(qpair))
            m = jnp.full((rows, 128), NEG_LARGE, F32)
            for j in range(count):
                at = (first + qi + j) * rows
                s = nt(q, k_ref[0, at : at + rows, :])
                s = jnp.where(sq == sk_ref[0:1, at : at + rows], s, NEG_LARGE)
                s_scr[:, j * rows : (j + 1) * rows] = s
                for g in range(rows // 128):
                    m = jnp.maximum(m, s[:, g * 128 : (g + 1) * 128])
            m = jnp.max(m, axis=1, keepdims=True)
            total = jnp.zeros((rows, 128), F32)
            acc = jnp.zeros((rows, 128), F32)
            for j in range(count):
                at = (first + qi + j) * rows
                e = jnp.exp(s_scr[:, j * rows : (j + 1) * rows] - m)
                for g in range(rows // 128):
                    total = total + e[:, g * 128 : (g + 1) * 128]
                acc = acc + nn(e.astype(BF), v_ref[0, at : at + rows, :])
            total = jnp.sum(total, axis=1, keepdims=True)
            outs.append(acc / total)
            lses.append(m + jnp.log(total))
        o = jnp.where(low, outs[0], outs[1])
        o_ref[0, qi * rows : (qi + 1) * rows, :] = o
        ol_ref[0, qi * rows : (qi + 1) * rows, :] = o.astype(BF)
        both = jnp.where(lanes((rows, 128)) == 0, lses[0], lses[1])
        lse_ref[0, :, qi * rows : (qi + 1) * rows] = both.T[0:8, :]


def mid_kernel(a_ref, w_ref, x_ref, g_ref, mid_ref, h_ref):
    mid = x_ref[...].astype(F32) + nn(a_ref[...], w_ref[...])
    mid_ref[...] = mid
    h_ref[...] = (mid * rms_scale(mid) * g_ref[...]).astype(BF)


def pre_kernel(nblk, rows, ix, og, p_ref, wd, dehid, ogx_t, ogx):
    cap = p_ref.shape[1]

    @pl.when(pl.program_id(0) == 0)
    def _():
        for b in range(nblk):
            block = og[ix[b], 0:rows, :]
            ogx[b * cap : (b + 1) * cap, :] = nn(p_ref[ix[b]], block).astype(BF)
        ogx_t[...] = ogx[...].T

    dehid[...] = nt(ogx[...], wd[...]).astype(BF)


def act(g, u, dh):
    s = 0.5 * jnp.tanh(0.5 * g) + 0.5
    silu = g * s
    hid = (silu * u).astype(BF)
    dg = (dh * u * (s + silu * (1.0 - s))).astype(BF)
    du = (dh * silu).astype(BF)
    return hid, dg, du


def expert_kernel(nblk, rows, experts, e_ref, ix, *refs):
    g_refs = refs[:nblk]
    (p_ref, pt_ref, wr, wr_t, wsg, wsu, wsd, og, wg, wu, dehid) = refs[nblk : nblk + 11]
    (x_out, g_out, ghid, degate, deup, shid, dsg, dsu, tg, tg_far, rgrad) = refs[nblk + 11 : nblk + 22]
    x_scr, row_scr, tg_scr, pg_scr, prob_scr, g_scr = refs[nblk + 22 :]
    cap = p_ref.shape[1]
    slots = nblk * cap
    step = pl.program_id(0)
    per = nblk // pl.num_programs(0)

    @pl.when(step == 0)
    def _():
        row_scr[...] = jnp.zeros_like(row_scr)
        pg_scr[...] = jnp.zeros_like(pg_scr)
        for b in range(nblk):
            block = g_refs[b][...]
            g_scr[b * rows : (b + 1) * rows, :] = block
            x_scr[b * cap : (b + 1) * cap, :] = nn(p_ref[ix[b]], block).astype(BF)
        logits = jnp.where(lanes((slots, 128)) < experts, nn(x_scr[...], wr[...]), NEG_LARGE)
        shifted = jnp.exp(logits - jnp.max(logits, axis=1, keepdims=True))
        prob_scr[...] = shifted / jnp.sum(shifted, axis=1, keepdims=True)

    own = lanes((slots, 128)) == e_ref[0]
    gate = jnp.sum(jnp.where(own, prob_scr[...], 0.0), axis=1, keepdims=True)
    raw = dehid[...].astype(F32)
    hid, dg, du = act(nn(x_scr[...], wg[0]), nn(x_scr[...], wu[0]), raw * gate)
    hid = hid.astype(F32)
    ghid[...] = (hid * gate).astype(BF)
    degate[...] = dg
    deup[...] = du
    row_scr[...] += nt(dg, wg[0]) + nt(du, wu[0])
    pg_scr[...] += jnp.sum(hid * raw, axis=1, keepdims=True)

    for k in range(per):
        b = step * per + k
        at = pl.multiple_of(b * rows, rows)
        block = g_scr[pl.ds(at, rows), :]
        g_out[k * rows : (k + 1) * rows, :] = block
        dsh = nt(og[ix[b], 0:rows, :], wsd[...])
        sh, sg, su = act(nn(block, wsg[...]), nn(block, wsu[...]), dsh)
        here = slice(k * rows, (k + 1) * rows)
        shid[here, :] = sh
        dsg[here, :] = sg
        dsu[here, :] = su
        tg_scr[pl.ds(at, rows), :] = nt(sg, wsg[...]) + nt(su, wsu[...])

    @pl.when(step == pl.num_programs(0) - 1)
    def _():
        x_out[...] = x_scr[...]
        lgrad = (pg_scr[:, 0:1] * prob_scr[...] * (own.astype(F32) - gate)).astype(BF)
        rgrad[...] = tn(lgrad, x_scr[...])
        total = (row_scr[...] + nn(lgrad, wr_t[...])).astype(BF)
        for b in range(nblk):
            back = nn(pt_ref[ix[b]], total[b * cap : (b + 1) * cap, :])
            (tg_far if b % 2 else tg)[b // 2] = (tg_scr[b * rows : (b + 1) * rows, :] + back).astype(BF)


def wgrad_kernel(per, r_ref, x_ref, degate, deup, gate_near, gate_far, up_near, up_far, x_t):
    step = pl.program_id(0)

    @pl.when(step == 0)
    def _():
        x_t[...] = x_ref[...].T

    @pl.when(step < 2 * per)
    def _():
        gate_near[0] = nn(x_t[...], degate[...]).astype(BF)
        up_near[0] = nn(x_t[...], deup[...]).astype(BF)

    @pl.when(step >= 2 * per)
    def _():
        gate_far[0] = nn(x_t[...], degate[...]).astype(BF)
        up_far[0] = nn(x_t[...], deup[...]).astype(BF)


def wgrad_all_kernel(r_ref, x_ref, degate, deup, gate, up, x_t):
    @pl.when(pl.program_id(0) == 0)
    def _():
        x_t[...] = x_ref[...].T

    gate[0] = nn(x_t[...], degate[...]).astype(BF)
    up[0] = nn(x_t[...], deup[...]).astype(BF)


def down_grad_kernel(ogx_t, ghid, dn):
    dn[...] = nn(ogx_t[...], ghid[...]).astype(BF)


def result_kernel(nblk, rows, ix_s, g_ref, og, pt_ref, shid, dsg, dsu, wsd, ghid, wd, mix, sgu, sd, acc, part, sg_acc, sd_acc):
    cap = pt_ref.shape[2]
    step = pl.program_id(0)
    per = nblk // pl.num_programs(0)
    width = dsg.shape[1]

    @pl.when(step == 0)
    def _():
        acc[...] = jnp.zeros_like(acc)
        sg_acc[...] = jnp.zeros_like(sg_acc)
        sd_acc[...] = jnp.zeros_like(sd_acc)

    acc[...] += nn(ghid[...], wd[0])
    sg_acc[:, :width] += tn(g_ref[...], dsg[...])
    sg_acc[:, width:] += tn(g_ref[...], dsu[...])
    for k in range(per):
        b = step * per + k
        here = slice(k * rows, (k + 1) * rows)
        sd_acc[...] += tn(shid[here, :], og[ix_s[b], 0:rows, :])
        part[pl.ds(pl.multiple_of(b * rows, rows), rows), :] = nn(shid[here, :], wsd[...])

    @pl.when(step == pl.num_programs(0) - 1)
    def _():
        sgu[...] = sg_acc[...].astype(BF)
        sd[...] = sd_acc[...].astype(BF)
        res = acc[...].astype(BF)
        for b in range(nblk):
            picked = nn(pt_ref[ix_s[b]], res[b * cap : (b + 1) * cap, :])
            mix[ix_s[b]] = (picked + part[b * rows : (b + 1) * rows, :]).astype(BF)


def mid_back_kernel(count, *refs):
    pieces = refs[:count]
    mid_ref, g_ref, og_ref, w_ref, mg_ref, ag_ref, da_ref, gg_ref = refs[count:]
    two = pieces[0][...].astype(F32)
    for piece in pieces[1:]:
        two += piece[...].astype(F32)
    mid = mid_ref[...]
    scale = rms_scale(mid)
    mn = mid * scale
    gg_ref[...] = jnp.broadcast_to(jnp.sum(two * mn, axis=0, keepdims=True), gg_ref.shape)
    dn = two * g_ref[...]
    mg = og_ref[...].astype(F32) + scale * (dn - mn * jnp.mean(dn * mn, axis=1, keepdims=True))
    mg_ref[...] = mg
    ag = mg.astype(BF)
    ag_ref[...] = ag
    da = nt(ag, w_ref[...]).astype(BF)
    for i in range(da_ref.shape[0]):
        da_ref[i] = da[:, 128 * i : 128 * i + 128]


def attend_back_kernel(first, count, rows, q_ref, k_ref, v_ref, o_ref, do_ref, lse_ref, sq_ref, sk_ref, cos, sin,
                       h1_ref, wq, wk, wv, gain, c_ref, grads, og_own, og_far, gg, h1_t, k_t, dk, dv, og_scr):
    step = pl.program_id(0)
    low = lanes((rows, 128)) < 64
    kv_rows = k_ref.shape[1]
    base = kv_rows - 2 * rows

    @pl.when(step == 0)
    def _():
        h1_t[...] = h1_ref[...].T
        og_scr[...] = jnp.zeros_like(og_scr)

    k_t[...] = k_ref[0].T
    dk[...] = jnp.zeros_like(dk)
    dv[...] = jnp.zeros_like(dv)
    dqs = []
    for qi in range(2):
        at_q = qi * rows
        qpair = q_ref[0, at_q : at_q + rows, :]
        dopair = do_ref[0, at_q : at_q + rows, :]
        prod = dopair.astype(F32) * o_ref[0, at_q : at_q + rows, :]
        d0 = jnp.sum(jnp.where(low, prod, 0.0), axis=1, keepdims=True)
        d1 = jnp.sum(jnp.where(low, 0.0, prod), axis=1, keepdims=True)
        delta = jnp.where(lanes((rows, 128)) == 0, d0, d1).T
        sq = sq_ref[0:1, at_q : at_q + rows]
        halves = []
        for hh in range(2):
            keep = low if hh == 0 else jnp.logical_not(low)
            q = jnp.where(keep, qpair, jnp.zeros_like(qpair))
            do = jnp.where(keep, dopair, jnp.zeros_like(dopair))
            lse_row = lse_ref[0, hh : hh + 1, at_q : at_q + rows]
            delta_row = delta[hh : hh + 1, :]
            dq = jnp.zeros((64, rows), F32)
            for j in range(count):
                at = (first + qi + j) * rows
                same = sk_ref[at : at + rows, 0:1] == sq
                s = nt(k_ref[0, at : at + rows, :], q)
                p = jnp.where(same, jnp.exp(s - lse_row), 0.0)
                dp = nt(v_ref[0, at : at + rows, :], do)
                ds = (p * (dp - delta_row)).astype(BF)
                dv[at : at + rows, :] += nn(p.astype(BF), do)
                dk[at : at + rows, :] += nn(ds, q)
                dq += nn(k_t[64 * hh : 64 * hh + 64, at : at + rows], ds)
            halves.append(dq)
        dq = jnp.concatenate(halves, axis=0).T * 0.125
        at = base + at_q
        dq = dq * cos[at : at + rows, :] - turned(dq) * sin[at : at + rows, :]
        dqs.append(dq.astype(BF))
    dq = jnp.concatenate(dqs, axis=0)
    dkv = dk[...]
    dkb = (dkv * cos[...] - turned(dkv) * sin[...]).astype(BF)
    dvb = dv[...].astype(BF)
    grads[0, 0] = nn(h1_t[:, base:], dq).astype(BF)
    grads[0, 1] = nn(h1_t[...], dkb).astype(BF)
    grads[0, 2] = nn(h1_t[...], dvb).astype(BF)
    og_scr[...] += nt(dkb, wk[...]) + nt(dvb, wv[...])
    og_scr[base:, :] += nt(dq, wq[...])

    @pl.when(step == pl.num_programs(0) - 1)
    def _():
        one = og_scr[...]
        for slot in range(kv_rows // rows):
            block = one[slot * rows : (slot + 1) * rows, :].astype(BF)

            @pl.when(c_ref[0] == slot % 2)
            def _():
                og_own[slot // 2] = block

            @pl.when(c_ref[0] != slot % 2)
            def _():
                og_far[slot // 2] = block

        total = jnp.sum(one * h1_ref[...].astype(F32), axis=0, keepdims=True) / gain[...]
        gg[...] = jnp.broadcast_to(total, gg.shape)


def last_kernel(count, *refs):
    pieces = refs[:count]
    x_ref, g_ref, mg_ref, out = refs[count:]
    one = pieces[0][...].astype(F32)
    for piece in pieces[1:]:
        one += piece[...].astype(F32)
    x = x_ref[...].astype(F32)
    scale = rms_scale(x)
    xn = x * scale
    dn = one * g_ref[...]
    out[...] = mg_ref[...] + scale * (dn - xn * jnp.mean(dn * xn, axis=1, keepdims=True))


def shape(dims, dtype=BF):
    return jax.ShapeDtypeStruct(dims, dtype)


def shards(
    R,
    E,
    tokens,
    segment_ids,
    routes,
    norm1_gain,
    w_query,
    w_key,
    w_value,
    w_out,
    norm2_gain,
    w_router,
    shared_gate,
    shared_up,
    shared_down,
    expert_gate,
    expert_up,
    expert_down,
    out_grad,
):
    Z = E // 2
    T, D = tokens.shape
    FF = shared_gate.shape[1]
    topk = routes.shape[1]
    experts = w_router.shape[1]
    assert expert_gate.shape[0] == 1 and experts == E
    half = D // 2
    pairs = half // 128
    wrow = w_query.shape[0]
    hrow = 2 * wrow
    cap = 2 * T * topk // experts
    slots = E * cap
    fs = FF // E
    drow = shared_down.shape[0]
    longest = E * T // 2
    back = -(-(longest - 1) // T)
    nb = -(-back // 2)
    chips = nb + 1
    kvb = 2 * chips
    first = 2 * nb - back
    count = back + 1
    r = lax.axis_index("rep")
    e = lax.axis_index("ep")
    z, c = e // 2, e % 2
    is0 = c == 0
    c_arr = jnp.reshape(c, (1,)).astype(jnp.int32)
    e_arr = jnp.reshape(e, (1,)).astype(jnp.int32)

    def swap(x):
        return lax.ppermute(x, "ep", [(i, i ^ 1) for i in range(E)])

    def ring(x, s):
        return lax.ppermute(x, "ep", [(i, (i + 2 * s) % E) for i in range(E)])

    def line(x, s):
        return lax.ppermute(x, "ep", [(i, i + 2 * s) for i in range(E) if 0 <= i + 2 * s < E])

    def cross(x, s):
        return lax.ppermute(x, "rep", [(i, i ^ s) for i in range(R)])

    def ordered(mine, other):
        return jnp.where(is0, mine, other), jnp.where(is0, other, mine)

    def put(buf, x, i):
        return lax.dynamic_update_index_in_dim(buf, x, i, 0)

    def chip_pack(mats, extra):
        stacked = jnp.stack(mats).reshape(len(mats) * wrow, D)
        mine, other = ordered(stacked[:, :half], stacked[:, half:])
        ext = jnp.pad(extra.reshape(1, -1), ((0, 0), (0, half - extra.size)))
        got = swap(jnp.concatenate([other, ext], axis=0))
        a, b = ordered(mine, got[:-1])
        ea, eb = ordered(ext, got[-1:])
        rows = jnp.stack([a.reshape(-1, wrow, half), b.reshape(-1, wrow, half)], axis=1).reshape(-1, half)
        rows = jnp.concatenate([rows, ea, eb], axis=0)
        return jnp.pad(rows, ((0, -rows.shape[0] % 16), (0, 0)))

    def gather_z(pack):
        buf = put(jnp.zeros((Z,) + pack.shape, BF), pack, z)
        for s in range(1, Z):
            buf = put(buf, ring(pack, s), (z - s) % Z)
        return buf

    def gather_rep(part, *deps):
        got = [cross(part, s) for s in range(1, R)]
        if deps:
            got = [after(x, *deps) for x in got]
        buf = put(jnp.zeros((R,) + part.shape, BF), part, r)
        for s in range(1, R):
            buf = put(buf, got[s - 1], r ^ s)
        return buf

    def unpack(full, i):
        return full[:, :, i * hrow : (i + 1) * hrow, :].reshape(D, half)

    pack = chip_pack(
        [w_query, w_key, w_value, w_out], jnp.concatenate([norm1_gain, norm2_gain, w_router.reshape(-1)])
    )
    part = gather_z(pack)
    full = gather_rep(part)
    wq, wk, wv, wo_half = (unpack(full, i) for i in range(4))
    ext = full[:, :, 4 * hrow : 4 * hrow + 2, :].reshape(R * E, half)
    gain1 = ext[:, :wrow].reshape(1, D).astype(F32)
    gain2 = ext[:, wrow : 2 * wrow].reshape(1, D).astype(F32)
    router = ext[:, 2 * wrow : (2 + experts) * wrow].reshape(D, experts)
    router = jnp.pad(router, ((0, 0), (0, 128 - experts)))
    router_t = router.T

    seg_row = jnp.pad(segment_ids.reshape(1, T).astype(BF), ((0, 7), (0, D - T)))
    tok_pack = after(jnp.concatenate([tokens, seg_row], axis=0), pack)
    own_tok = [tok_pack] + [line(tok_pack, s) for s in range(1, chips)]
    par_tok = [swap(x) for x in own_tok]

    seg_blocks = [None] * kvb
    for s in range(chips):
        valid = z - s >= 0
        a, b = ordered(own_tok[s][T, :T], par_tok[s][T, :T])
        seg_blocks[2 * (nb - s)] = jnp.where(valid, a.astype(F32), -1.0)
        seg_blocks[2 * (nb - s) + 1] = jnp.where(valid, b.astype(F32), -1.0)
    segs = jnp.stack(seg_blocks)
    kv_rows = kvb * T
    seg_flat = segs.reshape(1, kv_rows)
    seg_wide = jnp.broadcast_to(segs.reshape(kv_rows, 1), (kv_rows, 128))

    inverse = jnp.exp(jnp.arange(32).astype(F32) * (-2.0 * math.log(10000.0) / 64))
    inverse = jnp.tile(inverse, 4)
    places = after((z - nb) * (2 * T) + jnp.arange(kv_rows, dtype=jnp.int32), pack)
    angle = places.astype(F32)[:, None] * inverse[None, :]
    cos, sin = lax.optimization_barrier((jnp.cos(angle), jnp.sin(angle)))
    cos, sin = cos.reshape(kvb, T, 128), sin.reshape(kvb, T, 128)

    h1, keys, vals, quer = pl.pallas_call(
        functools.partial(qkv_kernel, chips, T),
        in_specs=[pl.BlockSpec(memory_space=pltpu.SMEM)] + vmem(2 * chips + 6),
        out_specs=tuple(vmem(4)),
        out_shape=(
            shape((kvb, T, D)),
            shape((pairs, kvb, T, 128)),
            shape((pairs, kvb, T, 128)),
            shape((pairs, 2, T, 128)),
        ),
        compiler_params=params(),
        name="qkv",
        cost_estimate=cost(8),
    )(c_arr, *own_tok, *par_tok, wq, wk, wv, cos, sin, gain1)
    h1 = h1.reshape(kv_rows, D)
    keys = keys.reshape(pairs, kv_rows, 128)
    vals = vals.reshape(pairs, kv_rows, 128)
    quer = quer.reshape(pairs, 2 * T, 128)

    og_pack = jnp.concatenate(
        [out_grad, jnp.pad(routes.reshape(1, topk * T).astype(BF), ((0, 7), (0, D - topk * T)))], axis=0
    )
    og_all = lax.all_gather(after(og_pack, own_tok[-1]), "ep", axis=0)
    ix_arr = jnp.stack([((z - b // 2) % Z) * 2 + (c ^ (b % 2)) for b in range(E)]).astype(jnp.int32)

    wo = jnp.concatenate(ordered(wo_half, swap(wo_half)), axis=1)

    def by_unit(w):
        return w.reshape(wrow, R, E, drow).transpose(2, 0, 1, 3).reshape(E, wrow, fs)

    gu = jnp.concatenate([by_unit(shared_gate), by_unit(shared_up)], axis=2)
    gu = lax.all_to_all(after(gu, part), "ep", split_axis=0, concat_axis=0, tiled=True).reshape(E * wrow, 2 * fs)
    gu = after(gu, keys)
    wide = D // fs
    shared = jnp.concatenate(
        [gu[:, :fs], gu[:, fs:]] + [shared_down[:, k * fs : (k + 1) * fs] for k in range(wide)], axis=0
    )
    shared_got = [cross(shared, s) for s in range(1, R)]
    one = lambda *dims: pl.BlockSpec((1,) + dims, lambda i: (i, 0, 0))
    att, att_low, lse = pl.pallas_call(
        functools.partial(attend_kernel, first, count, T),
        grid=(pairs,),
        in_specs=[
            one(2 * T, 128),
            one(kv_rows, 128),
            one(kv_rows, 128),
            whole((2 * T, 128)),
            whole((1, kv_rows)),
        ],
        out_specs=(one(2 * T, 128), one(2 * T, 128), one(8, 2 * T)),
        out_shape=(
            shape((pairs, 2 * T, 128), F32),
            shape((pairs, 2 * T, 128)),
            shape((pairs, 8, 2 * T), F32),
        ),
        scratch_shapes=[pltpu.VMEM((T, count * T), F32)],
        compiler_params=params(),
        name="attend",
        cost_estimate=cost(10),
    )(after(quer, wo, shared), keys, vals, seg_wide[-2 * T :], seg_flat)

    def joined(mine, other):
        both = jnp.where(is0, jnp.concatenate([mine, other]), jnp.concatenate([other, mine]))
        return both.transpose(1, 0, 2).reshape(T, D)

    att_own, att_other = ordered(att_low[:, :T], att_low[:, T:])
    attended = joined(att_own, swap(att_other))
    mid, h2 = pl.pallas_call(
        mid_kernel,
        in_specs=vmem(4),
        out_specs=tuple(vmem(2)),
        out_shape=(shape((T, D), F32), shape((T, D))),
        compiler_params=params(),
        name="mid",
        cost_estimate=cost(3),
    )(attended, wo, tokens, gain2)

    shared_got = [after(x, h2) for x in shared_got]
    shared = put(jnp.zeros((R,) + shared.shape, BF), after(shared, h2), r)
    for i in range(1, R):
        shared = put(shared, shared_got[i - 1], r ^ i)
    gr = E * wrow
    wsg = shared[:, :gr].reshape(D, fs)
    wsu = shared[:, gr : 2 * gr].reshape(D, fs)
    wsd = jnp.concatenate(
        [shared[:, 2 * gr + k * drow : 2 * gr + (k + 1) * drow].reshape(fs, fs) for k in range(wide)], axis=1
    )
    h2_lane = [h2] + [ring(h2, s) for s in range(1, Z)]

    def both_cores(lane):
        blocks = []
        for item in lane:
            blocks += [item, swap(item)]
        return blocks

    og_all = after(og_all, h2)
    table = og_all[:, T, : topk * T].reshape(E, T, topk)
    hit = jnp.any(table == e.astype(F32).astype(BF), axis=2).astype(F32)
    rank = jnp.cumsum(hit, axis=1) - hit
    rank = jnp.where(hit > 0, rank, -1.0)
    slot_ids = jnp.arange(cap).astype(F32)
    pick = (rank[:, None, :] == slot_ids[None, :, None]).astype(BF)
    pick_t = (rank[:, :, None] == slot_ids[None, None, :]).astype(BF)

    smem = pl.BlockSpec(memory_space=pltpu.SMEM)
    ft = min(256, FF // R)
    steps = FF // ft
    per = FF // R // ft
    col = lambda n: pl.BlockSpec((n, ft), lambda i: (0, i))
    wcol = pl.BlockSpec((1, D, ft), lambda i: (0, 0, i))
    block_of = lambda n: pl.BlockSpec((E // steps * T, n), lambda i: (i, 0))
    wdn = pl.BlockSpec((1, ft, D), lambda i: (0, i, 0))
    dehid, ogx_t = pl.pallas_call(
        functools.partial(pre_kernel, E, T),
        grid=(steps,),
        in_specs=[smem, whole((E, T + 8, D))]
        + [whole((E, cap, T)), pl.BlockSpec((ft, D), lambda i: (i, 0))],
        out_specs=(col(slots), whole((D, slots))),
        out_shape=(shape((slots, FF)), shape((D, slots))),
        scratch_shapes=[pltpu.VMEM((slots, D), BF)],
        compiler_params=params(),
        name="pre",
        cost_estimate=cost(12),
    )(ix_arr, og_all, pick, expert_down.reshape(FF, D))

    h2_blocks = both_cores([after(x, dehid) for x in h2_lane])
    (x_rows, g_rows, ghid, degate, deup, shid, dsg, dsu, tg, tg_far, rgrad) = pl.pallas_call(
        functools.partial(expert_kernel, E, T, experts),
        grid=(steps,),
        in_specs=[smem, smem]
        + [whole((T, D))] * E
        + [
            whole((E, cap, T)),
            whole((E, T, cap)),
            whole((D, 128)),
            whole((128, D)),
            whole((D, fs)),
            whole((D, fs)),
            whole((fs, D)),
            whole((E, T + 8, D)),
            wcol,
            wcol,
            col(slots),
        ],
        out_specs=(
            whole((slots, D)),
            block_of(D),
            col(slots),
            col(slots),
            col(slots),
            block_of(fs),
            block_of(fs),
            block_of(fs),
            whole((Z, T, D)),
            whole((Z, T, D)),
            whole((128, D)),
        ),
        out_shape=(
            shape((slots, D)),
            shape((E * T, D)),
            shape((slots, FF)),
            shape((slots, FF)),
            shape((slots, FF)),
            shape((E * T, fs)),
            shape((E * T, fs)),
            shape((E * T, fs)),
            shape((Z, T, D)),
            shape((Z, T, D)),
            shape((128, D), F32),
        ),
        scratch_shapes=[
            pltpu.VMEM((slots, D), BF),
            pltpu.VMEM((slots, D), F32),
            pltpu.VMEM((E * T, D), F32),
            pltpu.VMEM((slots, 128), F32),
            pltpu.VMEM((slots, 128), F32),
            pltpu.VMEM((E * T, D), BF),
        ],
        compiler_params=params(),
        name="expert",
        cost_estimate=cost(38),
    )(e_arr, ix_arr, *h2_blocks, pick, pick_t, router, router_t, wsg, wsu, wsd, og_all, expert_gate, expert_up, dehid)

    def core_sums(mine, other, *deps):
        got = swap(other)
        if deps:
            got = after(got, *deps)
        return [mine[s] + got[s] for s in range(Z)]


    r_arr = jnp.reshape(r, (1,)).astype(jnp.int32)
    wide_rep = FF // R
    square = R == 4
    at0 = lambda n: pl.BlockSpec(n, lambda i, q: (0,) * len(n))
    dn_grad = pl.pallas_call(
        down_grad_kernel,
        grid=(steps,),
        in_specs=[whole((D, slots)), col(slots)],
        out_specs=col(D),
        out_shape=shape((D, FF)),
        compiler_params=params(),
        name="dgrad",
        cost_estimate=cost(10),
    )(ogx_t, ghid)
    dn_sum = lax.psum_scatter(dn_grad, "rep", scatter_dimension=0, tiled=True)
    lane = core_sums(tg, tg_far, dn_grad)
    two_parts = [lane[0]] + [ring(lane[s], -s) for s in range(1, Z)]

    if square:

        def rel_col(swapped):
            def index(i, q):
                d = i // per
                d = (d % 2) * 2 + d // 2 if swapped else d
                return (0, (d ^ q[0]) * per + i % per)

            return pl.BlockSpec((slots, ft), index)

        early = pl.BlockSpec(
            (1, D, ft),
            lambda i, q: (jnp.minimum(i // per, 1), 0, jnp.where(i < 2 * per, i % per, per - 1)),
        )
        late = pl.BlockSpec(
            (1, D, ft),
            lambda i, q: (jnp.maximum(i // per - 2, 0), 0, jnp.where(i < 2 * per, 0, i % per)),
        )
        gu_in = [rel_col(True), rel_col(False)]
        gu_specs = (early, late, early, late)
        gu_shapes = [(2, D, wide_rep)] * 4
        gu_kernel = functools.partial(wgrad_kernel, per)
    else:
        gu_in = [pl.BlockSpec((slots, ft), lambda i, q: (0, ((i // per) ^ q[0]) * per + i % per))] * 2
        gu_specs = (pl.BlockSpec((1, D, ft), lambda i, q: (i // per, 0, i % per)),) * 2
        gu_shapes = [(R, D, wide_rep)] * 2
        gu_kernel = wgrad_all_kernel
    gu_out = pl.pallas_call(
        gu_kernel,
        grid_spec=pltpu.PrefetchScalarGridSpec(
            num_scalar_prefetch=1,
            grid=(steps,),
            in_specs=[at0((slots, D))] + gu_in,
            out_specs=gu_specs,
            scratch_shapes=[pltpu.VMEM((D, slots), BF)],
        ),
        out_shape=tuple(shape(dims) for dims in gu_shapes),
        compiler_params=params(),
        name="wgrad",
        cost_estimate=cost(13),
    )(r_arr, after(x_rows, *lane), degate, deup)

    def pieces(x):
        return [lax.dynamic_index_in_dim(x, r ^ s, 0, keepdims=False) for s in range(R)]

    def direct(pieces, *deps):
        total = pieces[0].astype(F32)
        for d in range(1, R):
            got = cross(pieces[d], d)
            total += (after(got, *deps) if deps else got).astype(F32)
        return total

    two_parts[2::2] = [after(x, gu_out[0]) for x in two_parts[2::2]]
    near = []
    if square:
        gate_a, up_a = cross(gu_out[1][0], 1), cross(gu_out[3][0], 2)
    mix, sgu_grad, sd_grad = pl.pallas_call(
        functools.partial(result_kernel, E, T),
        grid=(steps,),
        in_specs=[
            smem,
            block_of(D),
            whole((E, T + 8, D)),
            whole((E, T, cap)),
            block_of(fs),
            block_of(fs),
            block_of(fs),
            whole((fs, D)),
            col(slots),
            wdn,
        ],
        out_specs=(whole((E, T, D)), whole((D, 2 * fs)), whole((fs, D))),
        out_shape=(shape((E, T, D)), shape((D, 2 * fs)), shape((fs, D))),
        scratch_shapes=[
            pltpu.VMEM((slots, D), F32),
            pltpu.VMEM((E * T, D), F32),
            pltpu.VMEM((D, 2 * fs), F32),
            pltpu.VMEM((fs, D), F32),
        ],
        compiler_params=params(),
        name="result",
        cost_estimate=cost(14),
    )(ix_arr, g_rows, og_all, pick_t, shid, dsg, dsu, wsd, after(ghid, gu_out[0], *two_parts[2::2], *near), expert_down)

    sgrad = jnp.concatenate(
        [sgu_grad[:, :fs].reshape(R, gr, fs), sgu_grad[:, fs:].reshape(R, gr, fs)]
        + [sd_grad[:, k * fs : (k + 1) * fs].reshape(R, drow, fs) for k in range(wide)],
        axis=1,
    )
    two_parts[1::2] = [after(x, mix) for x in two_parts[1::2]]
    if square:
        gate_a, up_a = after(gate_a, mix), after(up_a, mix)
        two_parts[0], gate_a, up_a = lax.optimization_barrier((two_parts[0], gate_a, up_a))
        gate_c, up_c = cross(after(gu_out[1][1], mix), 1), cross(after(gu_out[3][1], mix), 2)

    mix_in = after(mix, two_parts[1], *((gate_a, up_a) if square else ()))
    mix_sum = lax.psum_scatter(mix_in.reshape(E * T, D), "ep", scatter_dimension=0, tiled=True)

    mid_grad, attn_grad, att_grad, gain2_part = pl.pallas_call(
        functools.partial(mid_back_kernel, Z),
        in_specs=vmem(Z + 4),
        out_specs=tuple(vmem(4)),
        out_shape=(shape((T, D), F32), shape((T, D)), shape((2 * pairs, T, 128)), shape((8, D), F32)),
        compiler_params=params(),
        name="mid_back",
        cost_estimate=cost(4),
    )(*two_parts, mid, gain2, out_grad, wo)

    ag_own, ag_other = ordered(att_grad[:pairs], att_grad[pairs:])
    do_a, do_b = ordered(ag_own, swap(ag_other))
    do = jnp.concatenate([do_a, do_b], axis=1)
    wo_part = tn(attended, after(attn_grad, ag_other)).astype(BF)
    wo_mine, wo_other = ordered(wo_part[:, :half], wo_part[:, half:])
    wo_got = swap(wo_other)
    if square:
        gate_mid = gu_out[0][1] + after(gate_c, do)
        up_mid = gu_out[2][1] + after(up_c, do)
        gate_b, up_b = cross(gate_mid, 2), cross(up_mid, 1)
        sg_own, sg_near, sg_a, sg_c = pieces(after(sgrad, do))
        sg_send = jnp.stack([sg_a, sg_c])
        sg_got = cross(sg_send, 2)
        do, gate_mid, up_mid, wo_other, sg_send = lax.optimization_barrier(
            (do, gate_mid, up_mid, wo_other, sg_send)
        )

    cos2, sin2 = cos.reshape(kv_rows, 128), sin.reshape(kv_rows, 128)
    grads, og1, og1_far, gain1_part = pl.pallas_call(
        functools.partial(attend_back_kernel, first, count, T),
        grid=(pairs,),
        in_specs=[
            one(2 * T, 128),
            one(kv_rows, 128),
            one(kv_rows, 128),
            one(2 * T, 128),
            one(2 * T, 128),
            one(8, 2 * T),
            whole((1, 2 * T)),
            whole((kv_rows, 128)),
            whole((kv_rows, 128)),
            whole((kv_rows, 128)),
            whole((kv_rows, D)),
            pl.BlockSpec((D, 128), lambda i: (0, i)),
            pl.BlockSpec((D, 128), lambda i: (0, i)),
            pl.BlockSpec((D, 128), lambda i: (0, i)),
            whole((1, D)),
            smem,
        ],
        out_specs=(
            pl.BlockSpec((1, 3, D, 128), lambda i: (i, 0, 0, 0)),
            whole((chips, T, D)),
            whole((chips, T, D)),
            whole((8, D)),
        ),
        out_shape=(shape((pairs, 3, D, 128)), shape((chips, T, D)), shape((chips, T, D)), shape((8, D), F32)),
        scratch_shapes=[
            pltpu.VMEM((D, kv_rows), BF),
            pltpu.VMEM((128, kv_rows), BF),
            pltpu.VMEM((kv_rows, 128), F32),
            pltpu.VMEM((kv_rows, 128), F32),
            pltpu.VMEM((kv_rows, D), F32),
        ],
        compiler_params=params(),
        name="attend_back",
        cost_estimate=cost(30),
    )(quer, keys, vals, att, do, lse, seg_flat[:, -2 * T :], seg_wide, cos2, sin2, h1, wq, wk, wv, gain1, c_arr)

    wo_got = after(wo_got, og1)
    if square:
        gate_b, up_b, sg_got = after(gate_b, og1), after(up_b, og1), after(sg_got, og1)
        og1_far, grads, gate_b, up_b, wo_got, sg_got = lax.optimization_barrier(
            (og1_far, grads, gate_b, up_b, wo_got, sg_got)
        )
    far_got = swap(og1_far)
    if square:
        sg_mid = cross(sg_near + sg_got[1], 1)
        sg_mid, far_got = lax.optimization_barrier((sg_mid, far_got))
    lane = og1 + far_got
    one_parts = [lane[nb]] + [line(lane[nb - s], -s) for s in range(1, chips)]

    n_chip = R * Z

    def dense_pack(groups, ext):
        rows = groups.reshape(-1, n_chip, hrow, 128).transpose(1, 0, 2, 3).reshape(n_chip, -1, 128)
        ext = ext.astype(BF)
        ext = jnp.pad(ext, ((0, 0), (0, -ext.shape[1] % 128))).reshape(n_chip, -1, 128)
        rows = jnp.concatenate([rows, ext], axis=1)
        return jnp.pad(rows, ((0, 0), (0, -rows.shape[1] % 8), (0, 0))).reshape(R, Z, -1, 128)

    wo_lane = wo_mine + wo_got
    wo_groups = wo_lane.reshape(D, pairs, 128).transpose(1, 0, 2)
    ext = jnp.concatenate(
        [
            gain1_part[0].reshape(n_chip, hrow),
            gain2_part[0].reshape(n_chip, hrow),
            rgrad[:experts].reshape(experts, n_chip, hrow).transpose(1, 0, 2).reshape(n_chip, experts * hrow),
        ],
        axis=1,
    )

    groups = 4 * pairs
    pack_d = dense_pack(jnp.concatenate([grads.reshape(-1, D, 128), wo_groups]), ext)
    send_d = pieces(pack_d)
    got_d = [after(cross(send_d[s], s), *one_parts[1:]) for s in range(1, R)]
    total_d = send_d[0].astype(F32)
    for x in got_d:
        total_d += x.astype(F32)
    total_d = total_d.astype(BF)
    if square:
        sgrad = sg_own.astype(F32) + sg_got[0].astype(F32) + sg_mid.astype(F32)
    else:
        sgrad = lax.psum_scatter(sgrad.reshape(-1, fs), "rep", scatter_dimension=0, tiled=True).astype(F32)
    sd_sum = jnp.concatenate(
        [sgrad[2 * gr + k * drow : 2 * gr + (k + 1) * drow] for k in range(wide)], axis=1
    )
    sgu = jnp.concatenate([sgrad[:gr], sgrad[gr : 2 * gr]], axis=1).astype(BF)
    sgu = sgu.reshape(Z, hrow, -1, 128).transpose(0, 2, 1, 3).reshape(Z, -1, 128)
    rows_d = total_d.shape[1]
    to_z = jnp.concatenate([total_d, sgu], axis=1)
    z_own = lax.dynamic_index_in_dim(to_z, z, 0, keepdims=False)
    z_got = [ring(lax.dynamic_index_in_dim(to_z, (z + s) % Z, 0, keepdims=False), s) for s in range(1, Z)]

    if square:
        gate_sum = gu_out[0][0].astype(F32) + (gate_a.astype(F32) + after(gate_b, lane).astype(F32))
        up_sum = gu_out[2][0].astype(F32) + (up_a.astype(F32) + after(up_b, lane).astype(F32))
    else:
        gate_sum, up_sum = (direct(x, lane) for x in gu_out)
    dn_sum = after(dn_sum, lane).T.astype(F32)
    layer_out = (mid + after(mix_sum, lane).astype(F32)).astype(BF)
    done = [gate_sum, up_sum, dn_sum, layer_out, sd_sum, to_z]
    one_parts[0], *done = lax.optimization_barrier((one_parts[0], *done))
    gate_sum, up_sum, dn_sum, layer_out, sd_sum, to_z = done
    tokens_grad = pl.pallas_call(
        functools.partial(last_kernel, chips),
        in_specs=vmem(chips + 3),
        out_specs=vmem(1)[0],
        out_shape=shape((T, D), F32),
        compiler_params=params(),
        name="last",
        cost_estimate=cost(3),
    )(*one_parts, tokens, gain1, mid_grad)

    z_got = [after(x, tokens_grad) for x in z_got]
    total = z_own[:rows_d].astype(F32)
    for x in z_got:
        total += x[:rows_d].astype(F32)
    sg_from = put(jnp.zeros((Z,) + sgu.shape[1:], BF), z_own[rows_d:], z)
    for s in range(1, Z):
        sg_from = put(sg_from, z_got[s - 1][rows_d:], (z - s) % Z)
    sg_groups = Z * (2 * fs // 128)
    mats_all, ext_all = total[: groups * hrow], total[groups * hrow :]
    rows_all = jnp.concatenate([mats_all, sg_from.reshape(-1, 128).astype(F32)])
    rows_all = rows_all.reshape(groups + sg_groups, 2, wrow, 128)
    mine, other = ordered(rows_all[:, 0], rows_all[:, 1])
    got = swap(jnp.concatenate([other.reshape(-1, 128), ext_all], axis=0).astype(BF)).astype(F32)
    count_rows = (groups + sg_groups) * wrow
    left, right = ordered(mine, got[:count_rows].reshape(-1, wrow, 128))
    ext_all = ext_all + got[count_rows:]
    ext_all = ext_all.reshape(-1)[: (2 + experts) * hrow].reshape(2 + experts, 2, wrow)
    ext_all = jnp.where(is0, ext_all[:, 0], ext_all[:, 1])

    def joined_mat(indices):
        return jnp.concatenate([left[i] for i in indices] + [right[i] for i in indices], axis=1)

    mats = [joined_mat([3 * p + m for p in range(pairs)]) for m in range(3)]
    mats.append(joined_mat([3 * pairs + p for p in range(pairs)]))

    sg = jnp.stack([left[groups:].reshape(Z, -1, wrow, 128), right[groups:].reshape(Z, -1, wrow, 128)], axis=1)
    sg = sg.reshape(E, 2, fs // 128, wrow, 128)

    def units_back(x):
        x = x.transpose(0, 2, 1, 3).reshape(E, wrow, R, drow)
        return x.transpose(1, 2, 0, 3).reshape(wrow, FF)

    sg_sum, su_sum = units_back(sg[:, 0]), units_back(sg[:, 1])

    return (
        layer_out,
        tokens_grad,
        ext_all[0],
        mats[0],
        mats[1],
        mats[2],
        mats[3],
        ext_all[1],
        ext_all[2:].T,
        sg_sum,
        su_sum,
        sd_sum,
        gate_sum[None],
        up_sum[None],
        dn_sum[None],
    )


def solution(mesh):
    rows = P(("rep", "ep"), None)
    flat = P(("rep", "ep"))
    expert = P("ep", None, None)
    expert_out = P("ep", None, "rep")
    return jax.shard_map(
        functools.partial(shards, mesh.shape["rep"], mesh.shape["ep"]),
        mesh=mesh,
        in_specs=(rows, P("rep", "ep"), rows, flat, rows, rows, rows, rows, flat)
        + (rows,) * 4
        + (expert,) * 3
        + (rows,),
        out_specs=(rows, rows, flat, rows, rows, rows, rows, flat)
        + (rows,) * 4
        + (expert_out,) * 3,
        check_vma=False,
    )
```

```python
import functools
import math

import jax
import jax.numpy as jnp
from jax import lax
from jax.experimental import pallas as pl
from jax.experimental.pallas import tpu as pltpu
from jax.sharding import PartitionSpec as P

HEADS = 12
EPSILON = 1e-06
NEG_LARGE = -1e30
BF = jnp.bfloat16
F32 = jnp.float32
VMEM_LIMIT = 58 * 1024 * 1024


def nn(a, b):
    return lax.dot_general(a, b, (((1,), (0,)), ((), ())), preferred_element_type=F32)


def nt(a, b):
    return lax.dot_general(a, b, (((1,), (1,)), ((), ())), preferred_element_type=F32)


def tn(a, b):
    return lax.dot_general(a, b, (((0,), (0,)), ((), ())), preferred_element_type=F32)


def rms_scale(values):
    return lax.rsqrt(jnp.mean(values * values, axis=1, keepdims=True) + EPSILON)


def lanes(shape):
    return lax.broadcasted_iota(jnp.int32, shape, len(shape) - 1)


def turned(x):
    front = lanes(x.shape) % 64 < 32
    return jnp.where(front, -pltpu.roll(x, 96, 1), pltpu.roll(x, 32, 1))


def vmem(n):
    return [pl.BlockSpec(memory_space=pltpu.VMEM)] * n


def params(**kw):
    return pltpu.CompilerParams(vmem_limit_bytes=VMEM_LIMIT, **kw)


def cost(micros):
    return pl.CostEstimate(flops=int(micros * 1.1e9), bytes_accessed=int(micros * 1e5), transcendentals=0)


def after(x, *deps):
    return lax.optimization_barrier((x,) + deps)[0]


def whole(shape):
    return pl.BlockSpec(shape, lambda *_: (0,) * len(shape))


def qkv_kernel(chips, rows, c_ref, *refs):
    own, par = refs[:chips], refs[chips : 2 * chips]
    wq, wk, wv, cos, sin, gain, h1, keys, vals, quer = refs[2 * chips :]
    c = c_ref[0]
    pairs = keys.shape[0]
    scale = 0.125
    for s in range(chips):
        for p, src in ((0, own[s]), (1, par[s])):
            core = c if p == 0 else 1 - c
            slot = 2 * (chips - 1 - s) + core
            x = src[0:rows, :].astype(F32)
            h = (x * rms_scale(x) * gain[...]).astype(BF)
            h1[slot] = h
            co, si = cos[slot], sin[slot]
            k = nn(h, wk[...])
            v = nn(h, wv[...])
            for i in range(pairs):
                kp = k[:, 128 * i : 128 * i + 128]
                keys[i, slot] = (kp * co + turned(kp) * si).astype(BF)
                vals[i, slot] = v[:, 128 * i : 128 * i + 128].astype(BF)
            if s == 0:
                q = nn(h, wq[...])
                for i in range(pairs):
                    qp = q[:, 128 * i : 128 * i + 128]
                    quer[i, core] = ((qp * co + turned(qp) * si) * scale).astype(BF)


def attend_kernel(first, count, rows, q_ref, k_ref, v_ref, sq_ref, sk_ref, o_ref, ol_ref, lse_ref, s_scr):
    low = lanes((rows, 128)) < 64
    for qi in range(2):
        qpair = q_ref[0, qi * rows : (qi + 1) * rows, :]
        sq = sq_ref[qi * rows : (qi + 1) * rows, 0:1]
        outs, lses = [], []
        for hh in range(2):
            keep = low if hh == 0 else jnp.logical_not(low)
            q = jnp.where(keep, qpair, jnp.zeros_like(qpair))
            m = jnp.full((rows, 128), NEG_LARGE, F32)
            for j in range(count):
                at = (first + qi + j) * rows
                s = nt(q, k_ref[0, at : at + rows, :])
                s = jnp.where(sq == sk_ref[0:1, at : at + rows], s, NEG_LARGE)
                s_scr[:, j * rows : (j + 1) * rows] = s
                for g in range(rows // 128):
                    m = jnp.maximum(m, s[:, g * 128 : (g + 1) * 128])
            m = jnp.max(m, axis=1, keepdims=True)
            total = jnp.zeros((rows, 128), F32)
            acc = jnp.zeros((rows, 128), F32)
            for j in range(count):
                at = (first + qi + j) * rows
                e = jnp.exp(s_scr[:, j * rows : (j + 1) * rows] - m)
                for g in range(rows // 128):
                    total = total + e[:, g * 128 : (g + 1) * 128]
                acc = acc + nn(e.astype(BF), v_ref[0, at : at + rows, :])
            total = jnp.sum(total, axis=1, keepdims=True)
            outs.append(acc / total)
            lses.append(m + jnp.log(total))
        o = jnp.where(low, outs[0], outs[1])
        o_ref[0, qi * rows : (qi + 1) * rows, :] = o
        ol_ref[0, qi * rows : (qi + 1) * rows, :] = o.astype(BF)
        both = jnp.where(lanes((rows, 128)) == 0, lses[0], lses[1])
        lse_ref[0, :, qi * rows : (qi + 1) * rows] = both.T[0:8, :]


def mid_kernel(a_ref, w_ref, x_ref, g_ref, mid_ref, h_ref):
    mid = x_ref[...].astype(F32) + nn(a_ref[...], w_ref[...])
    mid_ref[...] = mid
    h_ref[...] = (mid * rms_scale(mid) * g_ref[...]).astype(BF)


def pre_kernel(nblk, rows, ix, og, p_ref, wd, dehid, ogx_t, ogx):
    cap = p_ref.shape[1]

    @pl.when(pl.program_id(0) == 0)
    def _():
        for b in range(nblk):
            block = og[ix[b], 0:rows, :]
            ogx[b * cap : (b + 1) * cap, :] = nn(p_ref[ix[b]], block).astype(BF)
        ogx_t[...] = ogx[...].T

    dehid[...] = nt(ogx[...], wd[...]).astype(BF)


def act(g, u, dh):
    s = 0.5 * jnp.tanh(0.5 * g) + 0.5
    silu = g * s
    hid = (silu * u).astype(BF)
    dg = (dh * u * (s + silu * (1.0 - s))).astype(BF)
    du = (dh * silu).astype(BF)
    return hid, dg, du


def expert_kernel(nblk, rows, experts, e_ref, ix, *refs):
    g_refs = refs[:nblk]
    (p_ref, pt_ref, wr, wr_t, wsg, wsu, wsd, og, wg, wu, dehid) = refs[nblk : nblk + 11]
    (x_out, g_out, ghid, degate, deup, shid, dsg, dsu, tg, tg_far, rgrad) = refs[nblk + 11 : nblk + 22]
    x_scr, row_scr, tg_scr, pg_scr, prob_scr, g_scr = refs[nblk + 22 :]
    cap = p_ref.shape[1]
    slots = nblk * cap
    step = pl.program_id(0)
    per = nblk // pl.num_programs(0)

    @pl.when(step == 0)
    def _():
        row_scr[...] = jnp.zeros_like(row_scr)
        pg_scr[...] = jnp.zeros_like(pg_scr)
        for b in range(nblk):
            block = g_refs[b][...]
            g_scr[b * rows : (b + 1) * rows, :] = block
            x_scr[b * cap : (b + 1) * cap, :] = nn(p_ref[ix[b]], block).astype(BF)
        logits = jnp.where(lanes((slots, 128)) < experts, nn(x_scr[...], wr[...]), NEG_LARGE)
        shifted = jnp.exp(logits - jnp.max(logits, axis=1, keepdims=True))
        prob_scr[...] = shifted / jnp.sum(shifted, axis=1, keepdims=True)

    own = lanes((slots, 128)) == e_ref[0]
    gate = jnp.sum(jnp.where(own, prob_scr[...], 0.0), axis=1, keepdims=True)
    raw = dehid[...].astype(F32)
    hid, dg, du = act(nn(x_scr[...], wg[0]), nn(x_scr[...], wu[0]), raw * gate)
    hid = hid.astype(F32)
    ghid[...] = (hid * gate).astype(BF)
    degate[...] = dg
    deup[...] = du
    row_scr[...] += nt(dg, wg[0]) + nt(du, wu[0])
    pg_scr[...] += jnp.sum(hid * raw, axis=1, keepdims=True)

    for k in range(per):
        b = step * per + k
        at = pl.multiple_of(b * rows, rows)
        block = g_scr[pl.ds(at, rows), :]
        g_out[k * rows : (k + 1) * rows, :] = block
        dsh = nt(og[ix[b], 0:rows, :], wsd[...])
        sh, sg, su = act(nn(block, wsg[...]), nn(block, wsu[...]), dsh)
        here = slice(k * rows, (k + 1) * rows)
        shid[here, :] = sh
        dsg[here, :] = sg
        dsu[here, :] = su
        tg_scr[pl.ds(at, rows), :] = nt(sg, wsg[...]) + nt(su, wsu[...])

    @pl.when(step == pl.num_programs(0) - 1)
    def _():
        x_out[...] = x_scr[...]
        lgrad = (pg_scr[:, 0:1] * prob_scr[...] * (own.astype(F32) - gate)).astype(BF)
        rgrad[...] = tn(lgrad, x_scr[...])
        total = (row_scr[...] + nn(lgrad, wr_t[...])).astype(BF)
        for b in range(nblk):
            back = nn(pt_ref[ix[b]], total[b * cap : (b + 1) * cap, :])
            (tg_far if b % 2 else tg)[b // 2] = (tg_scr[b * rows : (b + 1) * rows, :] + back).astype(BF)


def wgrad_kernel(per, r_ref, x_ref, degate, deup, gate_near, gate_far, up_near, up_far, x_t):
    step = pl.program_id(0)

    @pl.when(step == 0)
    def _():
        x_t[...] = x_ref[...].T

    @pl.when(step < 2 * per)
    def _():
        gate_near[0] = nn(x_t[...], degate[...]).astype(BF)
        up_near[0] = nn(x_t[...], deup[...]).astype(BF)

    @pl.when(step >= 2 * per)
    def _():
        gate_far[0] = nn(x_t[...], degate[...]).astype(BF)
        up_far[0] = nn(x_t[...], deup[...]).astype(BF)


def wgrad_all_kernel(r_ref, x_ref, degate, deup, gate, up, x_t):
    @pl.when(pl.program_id(0) == 0)
    def _():
        x_t[...] = x_ref[...].T

    gate[0] = nn(x_t[...], degate[...]).astype(BF)
    up[0] = nn(x_t[...], deup[...]).astype(BF)


def down_grad_kernel(ogx_t, ghid, dn):
    dn[...] = nn(ogx_t[...], ghid[...]).astype(BF)


def result_kernel(nblk, rows, ix_s, g_ref, og, pt_ref, shid, dsg, dsu, wsd, ghid, wd, mix, sgu, sd, acc, part, sg_acc, sd_acc):
    cap = pt_ref.shape[2]
    step = pl.program_id(0)
    per = nblk // pl.num_programs(0)
    width = dsg.shape[1]

    @pl.when(step == 0)
    def _():
        acc[...] = jnp.zeros_like(acc)
        sg_acc[...] = jnp.zeros_like(sg_acc)
        sd_acc[...] = jnp.zeros_like(sd_acc)

    acc[...] += nn(ghid[...], wd[0])
    sg_acc[:, :width] += tn(g_ref[...], dsg[...])
    sg_acc[:, width:] += tn(g_ref[...], dsu[...])
    for k in range(per):
        b = step * per + k
        here = slice(k * rows, (k + 1) * rows)
        sd_acc[...] += tn(shid[here, :], og[ix_s[b], 0:rows, :])
        part[pl.ds(pl.multiple_of(b * rows, rows), rows), :] = nn(shid[here, :], wsd[...])

    @pl.when(step == pl.num_programs(0) - 1)
    def _():
        sgu[...] = sg_acc[...].astype(BF)
        sd[...] = sd_acc[...].astype(BF)
        res = acc[...].astype(BF)
        for b in range(nblk):
            picked = nn(pt_ref[ix_s[b]], res[b * cap : (b + 1) * cap, :])
            mix[ix_s[b]] = (picked + part[b * rows : (b + 1) * rows, :]).astype(BF)


def mid_back_kernel(count, *refs):
    pieces = refs[:count]
    mid_ref, g_ref, og_ref, w_ref, mg_ref, ag_ref, da_ref, gg_ref = refs[count:]
    two = pieces[0][...].astype(F32)
    for piece in pieces[1:]:
        two += piece[...].astype(F32)
    mid = mid_ref[...]
    scale = rms_scale(mid)
    mn = mid * scale
    gg_ref[...] = jnp.broadcast_to(jnp.sum(two * mn, axis=0, keepdims=True), gg_ref.shape)
    dn = two * g_ref[...]
    mg = og_ref[...].astype(F32) + scale * (dn - mn * jnp.mean(dn * mn, axis=1, keepdims=True))
    mg_ref[...] = mg
    ag = mg.astype(BF)
    ag_ref[...] = ag
    da = nt(ag, w_ref[...]).astype(BF)
    for i in range(da_ref.shape[0]):
        da_ref[i] = da[:, 128 * i : 128 * i + 128]


def attend_back_kernel(first, count, rows, q_ref, k_ref, v_ref, o_ref, do_ref, lse_ref, sq_ref, sk_ref, cos, sin,
                       h1_ref, wq, wk, wv, gain, c_ref, grads, og_own, og_far, gg, h1_t, k_t, dk, dv, og_scr):
    step = pl.program_id(0)
    low = lanes((rows, 128)) < 64
    kv_rows = k_ref.shape[1]
    base = kv_rows - 2 * rows

    @pl.when(step == 0)
    def _():
        h1_t[...] = h1_ref[...].T
        og_scr[...] = jnp.zeros_like(og_scr)

    k_t[...] = k_ref[0].T
    dk[...] = jnp.zeros_like(dk)
    dv[...] = jnp.zeros_like(dv)
    dqs = []
    for qi in range(2):
        at_q = qi * rows
        qpair = q_ref[0, at_q : at_q + rows, :]
        dopair = do_ref[0, at_q : at_q + rows, :]
        prod = dopair.astype(F32) * o_ref[0, at_q : at_q + rows, :]
        d0 = jnp.sum(jnp.where(low, prod, 0.0), axis=1, keepdims=True)
        d1 = jnp.sum(jnp.where(low, 0.0, prod), axis=1, keepdims=True)
        delta = jnp.where(lanes((rows, 128)) == 0, d0, d1).T
        sq = sq_ref[0:1, at_q : at_q + rows]
        def masked(x):
            zero = jnp.zeros_like(x)
            return jnp.concatenate([jnp.where(low, x, zero), jnp.where(low, zero, x)], axis=0)

        q, do = masked(qpair), masked(dopair)
        lse_row = jnp.concatenate([lse_ref[0, h : h + 1, at_q : at_q + rows] for h in range(2)], axis=1)
        delta_row = jnp.concatenate([delta[h : h + 1, :] for h in range(2)], axis=1)
        sq = jnp.concatenate([sq, sq], axis=1)
        halves = [jnp.zeros((64, rows), F32) for _ in range(2)]
        for j in range(count):
            at = (first + qi + j) * rows
            same = sk_ref[at : at + rows, 0:1] == sq
            s = nt(k_ref[0, at : at + rows, :], q)
            p = jnp.where(same, jnp.exp(s - lse_row), 0.0)
            dp = nt(v_ref[0, at : at + rows, :], do)
            ds = (p * (dp - delta_row)).astype(BF)
            dv[at : at + rows, :] += nn(p.astype(BF), do)
            dk[at : at + rows, :] += nn(ds, q)
            for h in range(2):
                halves[h] += nn(k_t[64 * h : 64 * h + 64, at : at + rows], ds[:, h * rows : (h + 1) * rows])
        dq = jnp.concatenate(halves, axis=0).T * 0.125
        at = base + at_q
        dq = dq * cos[at : at + rows, :] - turned(dq) * sin[at : at + rows, :]
        dqs.append(dq.astype(BF))
    dq = jnp.concatenate(dqs, axis=0)
    dkv = dk[...]
    dkb = (dkv * cos[...] - turned(dkv) * sin[...]).astype(BF)
    dvb = dv[...].astype(BF)
    grads[0, 0] = nn(h1_t[:, base:], dq).astype(BF)
    grads[0, 1] = nn(h1_t[...], dkb).astype(BF)
    grads[0, 2] = nn(h1_t[...], dvb).astype(BF)
    og_scr[...] += nt(dkb, wk[...]) + nt(dvb, wv[...])
    og_scr[base:, :] += nt(dq, wq[...])

    @pl.when(step == pl.num_programs(0) - 1)
    def _():
        one = og_scr[...]
        for slot in range(kv_rows // rows):
            block = one[slot * rows : (slot + 1) * rows, :].astype(BF)

            @pl.when(c_ref[0] == slot % 2)
            def _():
                og_own[slot // 2] = block

            @pl.when(c_ref[0] != slot % 2)
            def _():
                og_far[slot // 2] = block

        total = jnp.sum(one * h1_ref[...].astype(F32), axis=0, keepdims=True) / gain[...]
        gg[...] = jnp.broadcast_to(total, gg.shape)


def last_kernel(count, *refs):
    pieces = refs[:count]
    x_ref, g_ref, mg_ref, out = refs[count:]
    one = pieces[0][...].astype(F32)
    for piece in pieces[1:]:
        one += piece[...].astype(F32)
    x = x_ref[...].astype(F32)
    scale = rms_scale(x)
    xn = x * scale
    dn = one * g_ref[...]
    out[...] = mg_ref[...] + scale * (dn - xn * jnp.mean(dn * xn, axis=1, keepdims=True))


def shape(dims, dtype=BF):
    return jax.ShapeDtypeStruct(dims, dtype)


def shards(
    R,
    E,
    tokens,
    segment_ids,
    routes,
    norm1_gain,
    w_query,
    w_key,
    w_value,
    w_out,
    norm2_gain,
    w_router,
    shared_gate,
    shared_up,
    shared_down,
    expert_gate,
    expert_up,
    expert_down,
    out_grad,
):
    Z = E // 2
    T, D = tokens.shape
    FF = shared_gate.shape[1]
    topk = routes.shape[1]
    experts = w_router.shape[1]
    assert expert_gate.shape[0] == 1 and experts == E
    half = D // 2
    pairs = half // 128
    wrow = w_query.shape[0]
    hrow = 2 * wrow
    cap = 2 * T * topk // experts
    slots = E * cap
    fs = FF // E
    drow = shared_down.shape[0]
    longest = E * T // 2
    back = -(-(longest - 1) // T)
    nb = -(-back // 2)
    chips = nb + 1
    kvb = 2 * chips
    first = 2 * nb - back
    count = back + 1
    r = lax.axis_index("rep")
    e = lax.axis_index("ep")
    z, c = e // 2, e % 2
    is0 = c == 0
    c_arr = jnp.reshape(c, (1,)).astype(jnp.int32)
    e_arr = jnp.reshape(e, (1,)).astype(jnp.int32)

    def swap(x):
        return lax.ppermute(x, "ep", [(i, i ^ 1) for i in range(E)])

    def ring(x, s):
        return lax.ppermute(x, "ep", [(i, (i + 2 * s) % E) for i in range(E)])

    def line(x, s):
        return lax.ppermute(x, "ep", [(i, i + 2 * s) for i in range(E) if 0 <= i + 2 * s < E])

    def cross(x, s):
        return lax.ppermute(x, "rep", [(i, i ^ s) for i in range(R)])

    def ordered(mine, other):
        return jnp.where(is0, mine, other), jnp.where(is0, other, mine)

    def put(buf, x, i):
        return lax.dynamic_update_index_in_dim(buf, x, i, 0)

    def chip_pack(mats, extra):
        stacked = jnp.stack(mats).reshape(len(mats) * wrow, D)
        mine, other = ordered(stacked[:, :half], stacked[:, half:])
        ext = jnp.pad(extra.reshape(1, -1), ((0, 0), (0, half - extra.size)))
        got = swap(jnp.concatenate([other, ext], axis=0))
        a, b = ordered(mine, got[:-1])
        ea, eb = ordered(ext, got[-1:])
        rows = jnp.stack([a.reshape(-1, wrow, half), b.reshape(-1, wrow, half)], axis=1).reshape(-1, half)
        rows = jnp.concatenate([rows, ea, eb], axis=0)
        return jnp.pad(rows, ((0, -rows.shape[0] % 16), (0, 0)))

    def gather_z(pack):
        buf = put(jnp.zeros((Z,) + pack.shape, BF), pack, z)
        for s in range(1, Z):
            buf = put(buf, ring(pack, s), (z - s) % Z)
        return buf

    def gather_rep(part, *deps):
        got = [cross(part, s) for s in range(1, R)]
        if deps:
            got = [after(x, *deps) for x in got]
        buf = put(jnp.zeros((R,) + part.shape, BF), part, r)
        for s in range(1, R):
            buf = put(buf, got[s - 1], r ^ s)
        return buf

    def unpack(full, i):
        return full[:, :, i * hrow : (i + 1) * hrow, :].reshape(D, half)

    pack = chip_pack(
        [w_query, w_key, w_value, w_out], jnp.concatenate([norm1_gain, norm2_gain, w_router.reshape(-1)])
    )
    part = gather_z(pack)
    full = gather_rep(part)
    wq, wk, wv, wo_half = (unpack(full, i) for i in range(4))
    ext = full[:, :, 4 * hrow : 4 * hrow + 2, :].reshape(R * E, half)
    gain1 = ext[:, :wrow].reshape(1, D).astype(F32)
    gain2 = ext[:, wrow : 2 * wrow].reshape(1, D).astype(F32)
    router = ext[:, 2 * wrow : (2 + experts) * wrow].reshape(D, experts)
    router = jnp.pad(router, ((0, 0), (0, 128 - experts)))
    router_t = router.T

    seg_row = jnp.pad(segment_ids.reshape(1, T).astype(BF), ((0, 7), (0, D - T)))
    tok_pack = after(jnp.concatenate([tokens, seg_row], axis=0), pack)
    own_tok = [tok_pack] + [line(tok_pack, s) for s in range(1, chips)]
    par_tok = [swap(x) for x in own_tok]

    seg_blocks = [None] * kvb
    for s in range(chips):
        valid = z - s >= 0
        a, b = ordered(own_tok[s][T, :T], par_tok[s][T, :T])
        seg_blocks[2 * (nb - s)] = jnp.where(valid, a.astype(F32), -1.0)
        seg_blocks[2 * (nb - s) + 1] = jnp.where(valid, b.astype(F32), -1.0)
    segs = jnp.stack(seg_blocks)
    kv_rows = kvb * T
    seg_flat = segs.reshape(1, kv_rows)
    seg_wide = jnp.broadcast_to(segs.reshape(kv_rows, 1), (kv_rows, 128))

    inverse = jnp.exp(jnp.arange(32).astype(F32) * (-2.0 * math.log(10000.0) / 64))
    inverse = jnp.tile(inverse, 4)
    places = after((z - nb) * (2 * T) + jnp.arange(kv_rows, dtype=jnp.int32), pack)
    angle = places.astype(F32)[:, None] * inverse[None, :]
    cos, sin = lax.optimization_barrier((jnp.cos(angle), jnp.sin(angle)))
    cos, sin = cos.reshape(kvb, T, 128), sin.reshape(kvb, T, 128)

    h1, keys, vals, quer = pl.pallas_call(
        functools.partial(qkv_kernel, chips, T),
        in_specs=[pl.BlockSpec(memory_space=pltpu.SMEM)] + vmem(2 * chips + 6),
        out_specs=tuple(vmem(4)),
        out_shape=(
            shape((kvb, T, D)),
            shape((pairs, kvb, T, 128)),
            shape((pairs, kvb, T, 128)),
            shape((pairs, 2, T, 128)),
        ),
        compiler_params=params(),
        name="qkv",
        cost_estimate=cost(8),
    )(c_arr, *own_tok, *par_tok, wq, wk, wv, cos, sin, gain1)
    h1 = h1.reshape(kv_rows, D)
    keys = keys.reshape(pairs, kv_rows, 128)
    vals = vals.reshape(pairs, kv_rows, 128)
    quer = quer.reshape(pairs, 2 * T, 128)

    og_pack = jnp.concatenate(
        [out_grad, jnp.pad(routes.reshape(1, topk * T).astype(BF), ((0, 7), (0, D - topk * T)))], axis=0
    )
    og_all = lax.all_gather(after(og_pack, own_tok[-1]), "ep", axis=0)
    ix_arr = jnp.stack([((z - b // 2) % Z) * 2 + (c ^ (b % 2)) for b in range(E)]).astype(jnp.int32)

    wo = jnp.concatenate(ordered(wo_half, swap(wo_half)), axis=1)

    def by_unit(w):
        return w.reshape(wrow, R, E, drow).transpose(2, 0, 1, 3).reshape(E, wrow, fs)

    gu = jnp.concatenate([by_unit(shared_gate), by_unit(shared_up)], axis=2)
    gu = lax.all_to_all(after(gu, part), "ep", split_axis=0, concat_axis=0, tiled=True).reshape(E * wrow, 2 * fs)
    gu = after(gu, keys)
    wide = D // fs
    shared = jnp.concatenate(
        [gu[:, :fs], gu[:, fs:]] + [shared_down[:, k * fs : (k + 1) * fs] for k in range(wide)], axis=0
    )
    shared_got = [cross(shared, s) for s in range(1, R)]
    one = lambda *dims: pl.BlockSpec((1,) + dims, lambda i: (i, 0, 0))
    att, att_low, lse = pl.pallas_call(
        functools.partial(attend_kernel, first, count, T),
        grid=(pairs,),
        in_specs=[
            one(2 * T, 128),
            one(kv_rows, 128),
            one(kv_rows, 128),
            whole((2 * T, 128)),
            whole((1, kv_rows)),
        ],
        out_specs=(one(2 * T, 128), one(2 * T, 128), one(8, 2 * T)),
        out_shape=(
            shape((pairs, 2 * T, 128), F32),
            shape((pairs, 2 * T, 128)),
            shape((pairs, 8, 2 * T), F32),
        ),
        scratch_shapes=[pltpu.VMEM((T, count * T), F32)],
        compiler_params=params(),
        name="attend",
        cost_estimate=cost(10),
    )(after(quer, wo, shared), keys, vals, seg_wide[-2 * T :], seg_flat)

    def joined(mine, other):
        both = jnp.where(is0, jnp.concatenate([mine, other]), jnp.concatenate([other, mine]))
        return both.transpose(1, 0, 2).reshape(T, D)

    att_own, att_other = ordered(att_low[:, :T], att_low[:, T:])
    attended = joined(att_own, swap(att_other))
    mid, h2 = pl.pallas_call(
        mid_kernel,
        in_specs=vmem(4),
        out_specs=tuple(vmem(2)),
        out_shape=(shape((T, D), F32), shape((T, D))),
        compiler_params=params(),
        name="mid",
        cost_estimate=cost(3),
    )(attended, wo, tokens, gain2)

    shared_got = [after(x, h2) for x in shared_got]
    shared = put(jnp.zeros((R,) + shared.shape, BF), after(shared, h2), r)
    for i in range(1, R):
        shared = put(shared, shared_got[i - 1], r ^ i)
    gr = E * wrow
    wsg = shared[:, :gr].reshape(D, fs)
    wsu = shared[:, gr : 2 * gr].reshape(D, fs)
    wsd = jnp.concatenate(
        [shared[:, 2 * gr + k * drow : 2 * gr + (k + 1) * drow].reshape(fs, fs) for k in range(wide)], axis=1
    )
    h2_lane = [h2] + [ring(h2, s) for s in range(1, Z)]

    def both_cores(lane):
        blocks = []
        for item in lane:
            blocks += [item, swap(item)]
        return blocks

    og_all = after(og_all, h2)
    table = og_all[:, T, : topk * T].reshape(E, T, topk)
    hit = jnp.any(table == e.astype(F32).astype(BF), axis=2).astype(F32)
    rank = jnp.cumsum(hit, axis=1) - hit
    rank = jnp.where(hit > 0, rank, -1.0)
    slot_ids = jnp.arange(cap).astype(F32)
    pick = (rank[:, None, :] == slot_ids[None, :, None]).astype(BF)
    pick_t = (rank[:, :, None] == slot_ids[None, None, :]).astype(BF)

    smem = pl.BlockSpec(memory_space=pltpu.SMEM)
    ft = min(512, FF // R)
    steps = FF // ft
    per = FF // R // ft
    col = lambda n: pl.BlockSpec((n, ft), lambda i: (0, i))
    wcol = pl.BlockSpec((1, D, ft), lambda i: (0, 0, i))
    block_of = lambda n: pl.BlockSpec((E // steps * T, n), lambda i: (i, 0))
    wdn = pl.BlockSpec((1, ft, D), lambda i: (0, i, 0))
    dehid, ogx_t = pl.pallas_call(
        functools.partial(pre_kernel, E, T),
        grid=(steps,),
        in_specs=[smem, whole((E, T + 8, D))]
        + [whole((E, cap, T)), pl.BlockSpec((ft, D), lambda i: (i, 0))],
        out_specs=(col(slots), whole((D, slots))),
        out_shape=(shape((slots, FF)), shape((D, slots))),
        scratch_shapes=[pltpu.VMEM((slots, D), BF)],
        compiler_params=params(),
        name="pre",
        cost_estimate=cost(12),
    )(ix_arr, og_all, pick, expert_down.reshape(FF, D))

    h2_blocks = both_cores([after(x, dehid) for x in h2_lane])
    (x_rows, g_rows, ghid, degate, deup, shid, dsg, dsu, tg, tg_far, rgrad) = pl.pallas_call(
        functools.partial(expert_kernel, E, T, experts),
        grid=(steps,),
        in_specs=[smem, smem]
        + [whole((T, D))] * E
        + [
            whole((E, cap, T)),
            whole((E, T, cap)),
            whole((D, 128)),
            whole((128, D)),
            whole((D, fs)),
            whole((D, fs)),
            whole((fs, D)),
            whole((E, T + 8, D)),
            wcol,
            wcol,
            col(slots),
        ],
        out_specs=(
            whole((slots, D)),
            block_of(D),
            col(slots),
            col(slots),
            col(slots),
            block_of(fs),
            block_of(fs),
            block_of(fs),
            whole((Z, T, D)),
            whole((Z, T, D)),
            whole((128, D)),
        ),
        out_shape=(
            shape((slots, D)),
            shape((E * T, D)),
            shape((slots, FF)),
            shape((slots, FF)),
            shape((slots, FF)),
            shape((E * T, fs)),
            shape((E * T, fs)),
            shape((E * T, fs)),
            shape((Z, T, D)),
            shape((Z, T, D)),
            shape((128, D), F32),
        ),
        scratch_shapes=[
            pltpu.VMEM((slots, D), BF),
            pltpu.VMEM((slots, D), F32),
            pltpu.VMEM((E * T, D), F32),
            pltpu.VMEM((slots, 128), F32),
            pltpu.VMEM((slots, 128), F32),
            pltpu.VMEM((E * T, D), BF),
        ],
        compiler_params=params(),
        name="expert",
        cost_estimate=cost(38),
    )(e_arr, ix_arr, *h2_blocks, pick, pick_t, router, router_t, wsg, wsu, wsd, og_all, expert_gate, expert_up, dehid)

    def core_sums(mine, other, *deps):
        got = swap(other)
        if deps:
            got = after(got, *deps)
        return [mine[s] + got[s] for s in range(Z)]


    r_arr = jnp.reshape(r, (1,)).astype(jnp.int32)
    wide_rep = FF // R
    square = R == 4
    at0 = lambda n: pl.BlockSpec(n, lambda i, q: (0,) * len(n))
    dn_grad = pl.pallas_call(
        down_grad_kernel,
        grid=(steps,),
        in_specs=[whole((D, slots)), col(slots)],
        out_specs=col(D),
        out_shape=shape((D, FF)),
        compiler_params=params(),
        name="dgrad",
        cost_estimate=cost(10),
    )(ogx_t, ghid)
    dn_sum = lax.psum_scatter(dn_grad, "rep", scatter_dimension=0, tiled=True)
    lane = core_sums(tg, tg_far, dn_grad)
    two_parts = [lane[0]] + [ring(lane[s], -s) for s in range(1, Z)]

    if square:

        def rel_col(swapped):
            def index(i, q):
                d = i // per
                d = (d % 2) * 2 + d // 2 if swapped else d
                return (0, (d ^ q[0]) * per + i % per)

            return pl.BlockSpec((slots, ft), index)

        early = pl.BlockSpec(
            (1, D, ft),
            lambda i, q: (jnp.minimum(i // per, 1), 0, jnp.where(i < 2 * per, i % per, per - 1)),
        )
        late = pl.BlockSpec(
            (1, D, ft),
            lambda i, q: (jnp.maximum(i // per - 2, 0), 0, jnp.where(i < 2 * per, 0, i % per)),
        )
        gu_in = [rel_col(True), rel_col(False)]
        gu_specs = (early, late, early, late)
        gu_shapes = [(2, D, wide_rep)] * 4
        gu_kernel = functools.partial(wgrad_kernel, per)
    else:
        gu_in = [pl.BlockSpec((slots, ft), lambda i, q: (0, ((i // per) ^ q[0]) * per + i % per))] * 2
        gu_specs = (pl.BlockSpec((1, D, ft), lambda i, q: (i // per, 0, i % per)),) * 2
        gu_shapes = [(R, D, wide_rep)] * 2
        gu_kernel = wgrad_all_kernel
    gu_out = pl.pallas_call(
        gu_kernel,
        grid_spec=pltpu.PrefetchScalarGridSpec(
            num_scalar_prefetch=1,
            grid=(steps,),
            in_specs=[at0((slots, D))] + gu_in,
            out_specs=gu_specs,
            scratch_shapes=[pltpu.VMEM((D, slots), BF)],
        ),
        out_shape=tuple(shape(dims) for dims in gu_shapes),
        compiler_params=params(),
        name="wgrad",
        cost_estimate=cost(13),
    )(r_arr, after(x_rows, *lane), degate, deup)

    def pieces(x):
        return [lax.dynamic_index_in_dim(x, r ^ s, 0, keepdims=False) for s in range(R)]

    def direct(pieces, *deps):
        total = pieces[0].astype(F32)
        for d in range(1, R):
            got = cross(pieces[d], d)
            total += (after(got, *deps) if deps else got).astype(F32)
        return total

    two_parts[1] = after(two_parts[1], gu_out[0])
    near = []
    if square:
        gate_a, up_a = cross(gu_out[1][0], 1), cross(gu_out[3][0], 2)
    mix, sgu_grad, sd_grad = pl.pallas_call(
        functools.partial(result_kernel, E, T),
        grid=(steps,),
        in_specs=[
            smem,
            block_of(D),
            whole((E, T + 8, D)),
            whole((E, T, cap)),
            block_of(fs),
            block_of(fs),
            block_of(fs),
            whole((fs, D)),
            col(slots),
            wdn,
        ],
        out_specs=(whole((E, T, D)), whole((D, 2 * fs)), whole((fs, D))),
        out_shape=(shape((E, T, D)), shape((D, 2 * fs)), shape((fs, D))),
        scratch_shapes=[
            pltpu.VMEM((slots, D), F32),
            pltpu.VMEM((E * T, D), F32),
            pltpu.VMEM((D, 2 * fs), F32),
            pltpu.VMEM((fs, D), F32),
        ],
        compiler_params=params(),
        name="result",
        cost_estimate=cost(14),
    )(ix_arr, g_rows, og_all, pick_t, shid, dsg, dsu, wsd, after(ghid, gu_out[0], two_parts[1], *near), expert_down)

    sgrad = jnp.concatenate(
        [sgu_grad[:, :fs].reshape(R, gr, fs), sgu_grad[:, fs:].reshape(R, gr, fs)]
        + [sd_grad[:, k * fs : (k + 1) * fs].reshape(R, drow, fs) for k in range(wide)],
        axis=1,
    )
    two_parts[2:] = [after(x, mix) for x in two_parts[2:]]
    if square:
        gate_a, up_a = after(gate_a, mix), after(up_a, mix)
        two_parts[0], gate_a, up_a = lax.optimization_barrier((two_parts[0], gate_a, up_a))
        gate_c, up_c = cross(after(gu_out[1][1], mix), 1), cross(after(gu_out[3][1], mix), 2)

    mix_in = after(mix, two_parts[2], *((gate_a, up_a) if square else ()))
    mix_sum = lax.psum_scatter(mix_in.reshape(E * T, D), "ep", scatter_dimension=0, tiled=True)

    mid_grad, attn_grad, att_grad, gain2_part = pl.pallas_call(
        functools.partial(mid_back_kernel, Z),
        in_specs=vmem(Z + 4),
        out_specs=tuple(vmem(4)),
        out_shape=(shape((T, D), F32), shape((T, D)), shape((2 * pairs, T, 128)), shape((8, D), F32)),
        compiler_params=params(),
        name="mid_back",
        cost_estimate=cost(4),
    )(*two_parts, mid, gain2, out_grad, wo)

    ag_own, ag_other = ordered(att_grad[:pairs], att_grad[pairs:])
    do_a, do_b = ordered(ag_own, swap(ag_other))
    do = jnp.concatenate([do_a, do_b], axis=1)
    wo_part = tn(attended, after(attn_grad, ag_other)).astype(BF)
    wo_mine, wo_other = ordered(wo_part[:, :half], wo_part[:, half:])
    wo_got = swap(wo_other)
    if square:
        gate_mid = gu_out[0][1] + after(gate_c, do)
        up_mid = gu_out[2][1] + after(up_c, do)
        gate_b, up_b = cross(gate_mid, 2), cross(up_mid, 1)
        sg_own, sg_near, sg_a, sg_c = pieces(after(sgrad, do))
        sg_send = jnp.stack([sg_a, sg_c])
        sg_got = cross(sg_send, 2)
        do, gate_mid, up_mid, wo_other, sg_send = lax.optimization_barrier(
            (do, gate_mid, up_mid, wo_other, sg_send)
        )

    cos2, sin2 = cos.reshape(kv_rows, 128), sin.reshape(kv_rows, 128)
    grads, og1, og1_far, gain1_part = pl.pallas_call(
        functools.partial(attend_back_kernel, first, count, T),
        grid=(pairs,),
        in_specs=[
            one(2 * T, 128),
            one(kv_rows, 128),
            one(kv_rows, 128),
            one(2 * T, 128),
            one(2 * T, 128),
            one(8, 2 * T),
            whole((1, 2 * T)),
            whole((kv_rows, 128)),
            whole((kv_rows, 128)),
            whole((kv_rows, 128)),
            whole((kv_rows, D)),
            pl.BlockSpec((D, 128), lambda i: (0, i)),
            pl.BlockSpec((D, 128), lambda i: (0, i)),
            pl.BlockSpec((D, 128), lambda i: (0, i)),
            whole((1, D)),
            smem,
        ],
        out_specs=(
            pl.BlockSpec((1, 3, D, 128), lambda i: (i, 0, 0, 0)),
            whole((chips, T, D)),
            whole((chips, T, D)),
            whole((8, D)),
        ),
        out_shape=(shape((pairs, 3, D, 128)), shape((chips, T, D)), shape((chips, T, D)), shape((8, D), F32)),
        scratch_shapes=[
            pltpu.VMEM((D, kv_rows), BF),
            pltpu.VMEM((128, kv_rows), BF),
            pltpu.VMEM((kv_rows, 128), F32),
            pltpu.VMEM((kv_rows, 128), F32),
            pltpu.VMEM((kv_rows, D), F32),
        ],
        compiler_params=params(),
        name="attend_back",
        cost_estimate=cost(30),
    )(quer, keys, vals, att, do, lse, seg_flat[:, -2 * T :], seg_wide, cos2, sin2, h1, wq, wk, wv, gain1, c_arr)

    wo_got = after(wo_got, og1)
    if square:
        gate_b, up_b, sg_got = after(gate_b, og1), after(up_b, og1), after(sg_got, og1)
        og1_far, grads, gate_b, up_b, wo_got, sg_got = lax.optimization_barrier(
            (og1_far, grads, gate_b, up_b, wo_got, sg_got)
        )
    far_got = swap(og1_far)
    if square:
        sg_mid = cross(sg_near + sg_got[1], 1)
        sg_mid, far_got = lax.optimization_barrier((sg_mid, far_got))
    lane = og1 + far_got
    one_moved = lane[0]
    for i in range(1, nb):
        one_moved = lane[i] + line(one_moved, -1)
    one_parts = [lane[nb], line(one_moved, -1)]

    n_chip = R * Z

    def dense_pack(groups, ext):
        rows = groups.reshape(-1, n_chip, hrow, 128).transpose(1, 0, 2, 3).reshape(n_chip, -1, 128)
        ext = ext.astype(BF)
        ext = jnp.pad(ext, ((0, 0), (0, -ext.shape[1] % 128))).reshape(n_chip, -1, 128)
        rows = jnp.concatenate([rows, ext], axis=1)
        return jnp.pad(rows, ((0, 0), (0, -rows.shape[1] % 8), (0, 0))).reshape(R, Z, -1, 128)

    wo_lane = wo_mine + wo_got
    wo_groups = wo_lane.reshape(D, pairs, 128).transpose(1, 0, 2)
    ext = jnp.concatenate(
        [
            gain1_part[0].reshape(n_chip, hrow),
            gain2_part[0].reshape(n_chip, hrow),
            rgrad[:experts].reshape(experts, n_chip, hrow).transpose(1, 0, 2).reshape(n_chip, experts * hrow),
        ],
        axis=1,
    )

    groups = 4 * pairs
    pack_d = dense_pack(jnp.concatenate([grads.reshape(-1, D, 128), wo_groups]), ext)
    send_d = pieces(pack_d)
    got_d = [after(cross(send_d[s], s), *one_parts[1:]) for s in range(1, R)]
    total_d = send_d[0].astype(F32)
    for x in got_d:
        total_d += x.astype(F32)
    total_d = total_d.astype(BF)
    if square:
        sgrad = sg_own.astype(F32) + sg_got[0].astype(F32) + sg_mid.astype(F32)
    else:
        sgrad = lax.psum_scatter(sgrad.reshape(-1, fs), "rep", scatter_dimension=0, tiled=True).astype(F32)
    sd_sum = jnp.concatenate(
        [sgrad[2 * gr + k * drow : 2 * gr + (k + 1) * drow] for k in range(wide)], axis=1
    )
    sgu = jnp.concatenate([sgrad[:gr], sgrad[gr : 2 * gr]], axis=1).astype(BF)
    sgu = sgu.reshape(Z, hrow, -1, 128).transpose(0, 2, 1, 3).reshape(Z, -1, 128)
    rows_d = total_d.shape[1]
    to_z = jnp.concatenate([total_d, sgu], axis=1)
    z_own = lax.dynamic_index_in_dim(to_z, z, 0, keepdims=False)
    z_got = [ring(lax.dynamic_index_in_dim(to_z, (z + s) % Z, 0, keepdims=False), s) for s in range(1, Z)]

    if square:
        gate_sum = gu_out[0][0].astype(F32) + (gate_a.astype(F32) + after(gate_b, lane).astype(F32))
        up_sum = gu_out[2][0].astype(F32) + (up_a.astype(F32) + after(up_b, lane).astype(F32))
    else:
        gate_sum, up_sum = (direct(x, lane) for x in gu_out)
    dn_sum = after(dn_sum, lane).T.astype(F32)
    layer_out = (mid + after(mix_sum, lane).astype(F32)).astype(BF)
    done = [gate_sum, up_sum, dn_sum, layer_out, sd_sum, to_z]
    one_parts[0], *done = lax.optimization_barrier((one_parts[0], *done))
    gate_sum, up_sum, dn_sum, layer_out, sd_sum, to_z = done
    tokens_grad = pl.pallas_call(
        functools.partial(last_kernel, 2),
        in_specs=vmem(5),
        out_specs=vmem(1)[0],
        out_shape=shape((T, D), F32),
        compiler_params=params(),
        name="last",
        cost_estimate=cost(3),
    )(*one_parts, tokens, gain1, mid_grad)

    z_got = [after(x, tokens_grad) for x in z_got]
    total = z_own[:rows_d].astype(F32)
    for x in z_got:
        total += x[:rows_d].astype(F32)
    sg_from = put(jnp.zeros((Z,) + sgu.shape[1:], BF), z_own[rows_d:], z)
    for s in range(1, Z):
        sg_from = put(sg_from, z_got[s - 1][rows_d:], (z - s) % Z)
    sg_groups = Z * (2 * fs // 128)
    mats_all, ext_all = total[: groups * hrow], total[groups * hrow :]
    rows_all = jnp.concatenate([mats_all, sg_from.reshape(-1, 128).astype(F32)])
    rows_all = rows_all.reshape(groups + sg_groups, 2, wrow, 128)
    mine, other = ordered(rows_all[:, 0], rows_all[:, 1])
    got = swap(jnp.concatenate([other.reshape(-1, 128), ext_all], axis=0).astype(BF)).astype(F32)
    count_rows = (groups + sg_groups) * wrow
    left, right = ordered(mine, got[:count_rows].reshape(-1, wrow, 128))
    ext_all = ext_all + got[count_rows:]
    ext_all = ext_all.reshape(-1)[: (2 + experts) * hrow].reshape(2 + experts, 2, wrow)
    ext_all = jnp.where(is0, ext_all[:, 0], ext_all[:, 1])

    def joined_mat(indices):
        return jnp.concatenate([left[i] for i in indices] + [right[i] for i in indices], axis=1)

    mats = [joined_mat([3 * p + m for p in range(pairs)]) for m in range(3)]
    mats.append(joined_mat([3 * pairs + p for p in range(pairs)]))

    sg = jnp.stack([left[groups:].reshape(Z, -1, wrow, 128), right[groups:].reshape(Z, -1, wrow, 128)], axis=1)
    sg = sg.reshape(E, 2, fs // 128, wrow, 128)

    def units_back(x):
        x = x.transpose(0, 2, 1, 3).reshape(E, wrow, R, drow)
        return x.transpose(1, 2, 0, 3).reshape(wrow, FF)

    sg_sum, su_sum = units_back(sg[:, 0]), units_back(sg[:, 1])

    return (
        layer_out,
        tokens_grad,
        ext_all[0],
        mats[0],
        mats[1],
        mats[2],
        mats[3],
        ext_all[1],
        ext_all[2:].T,
        sg_sum,
        su_sum,
        sd_sum,
        gate_sum[None],
        up_sum[None],
        dn_sum[None],
    )


def solution(mesh):
    rows = P(("rep", "ep"), None)
    flat = P(("rep", "ep"))
    expert = P("ep", None, None)
    expert_out = P("ep", None, "rep")
    return jax.shard_map(
        functools.partial(shards, mesh.shape["rep"], mesh.shape["ep"]),
        mesh=mesh,
        in_specs=(rows, P("rep", "ep"), rows, flat, rows, rows, rows, rows, flat)
        + (rows,) * 4
        + (expert,) * 3
        + (rows,),
        out_specs=(rows, rows, flat, rows, rows, rows, rows, flat)
        + (rows,) * 4
        + (expert_out,) * 3,
        check_vma=False,
    )
```

```python
import functools
import math

import jax
import jax.numpy as jnp
from jax import lax
from jax.experimental import pallas as pl
from jax.experimental.pallas import tpu as pltpu
from jax.sharding import PartitionSpec as P

HEADS = 12
EPSILON = 1e-06
NEG_LARGE = -1e30
BF = jnp.bfloat16
F32 = jnp.float32
VMEM_LIMIT = 58 * 1024 * 1024


def nn(a, b):
    return lax.dot_general(a, b, (((1,), (0,)), ((), ())), preferred_element_type=F32)


def nt(a, b):
    return lax.dot_general(a, b, (((1,), (1,)), ((), ())), preferred_element_type=F32)


def tn(a, b):
    return lax.dot_general(a, b, (((0,), (0,)), ((), ())), preferred_element_type=F32)


def rms_scale(values):
    return lax.rsqrt(jnp.mean(values * values, axis=1, keepdims=True) + EPSILON)


def lanes(shape):
    return lax.broadcasted_iota(jnp.int32, shape, len(shape) - 1)


def turned(x):
    front = lanes(x.shape) % 64 < 32
    return jnp.where(front, -pltpu.roll(x, 96, 1), pltpu.roll(x, 32, 1))


def vmem(n):
    return [pl.BlockSpec(memory_space=pltpu.VMEM)] * n


def params(**kw):
    return pltpu.CompilerParams(vmem_limit_bytes=VMEM_LIMIT, **kw)


def cost(micros):
    return pl.CostEstimate(flops=int(micros * 1.1e9), bytes_accessed=int(micros * 1e5), transcendentals=0)


def after(x, *deps):
    return lax.optimization_barrier((x,) + deps)[0]


def whole(shape):
    return pl.BlockSpec(shape, lambda *_: (0,) * len(shape))


def qkv_kernel(chips, rows, c_ref, *refs):
    own, par = refs[:chips], refs[chips : 2 * chips]
    wq, wk, wv, cos, sin, gain, h1, keys, vals, quer = refs[2 * chips :]
    c = c_ref[0]
    pairs = keys.shape[0]
    scale = 0.125
    for s in range(chips):
        for p, src in ((0, own[s]), (1, par[s])):
            core = c if p == 0 else 1 - c
            slot = 2 * (chips - 1 - s) + core
            x = src[0:rows, :].astype(F32)
            h = (x * rms_scale(x) * gain[...]).astype(BF)
            h1[slot] = h
            co, si = cos[slot], sin[slot]
            k = nn(h, wk[...])
            v = nn(h, wv[...])
            for i in range(pairs):
                kp = k[:, 128 * i : 128 * i + 128]
                keys[i, slot] = (kp * co + turned(kp) * si).astype(BF)
                vals[i, slot] = v[:, 128 * i : 128 * i + 128].astype(BF)
            if s == 0:
                q = nn(h, wq[...])
                for i in range(pairs):
                    qp = q[:, 128 * i : 128 * i + 128]
                    quer[i, core] = ((qp * co + turned(qp) * si) * scale).astype(BF)


def attend_kernel(first, count, rows, q_ref, k_ref, v_ref, sq_ref, sk_ref, o_ref, ol_ref, lse_ref, s_scr):
    low = lanes((rows, 128)) < 64
    for qi in range(2):
        qpair = q_ref[0, qi * rows : (qi + 1) * rows, :]
        sq = sq_ref[qi * rows : (qi + 1) * rows, 0:1]
        outs, lses = [], []
        for hh in range(2):
            keep = low if hh == 0 else jnp.logical_not(low)
            q = jnp.where(keep, qpair, jnp.zeros_like(qpair))
            m = jnp.full((rows, 128), NEG_LARGE, F32)
            for j in range(count):
                at = (first + qi + j) * rows
                s = nt(q, k_ref[0, at : at + rows, :])
                s = jnp.where(sq == sk_ref[0:1, at : at + rows], s, NEG_LARGE)
                s_scr[:, j * rows : (j + 1) * rows] = s
                for g in range(rows // 128):
                    m = jnp.maximum(m, s[:, g * 128 : (g + 1) * 128])
            m = jnp.max(m, axis=1, keepdims=True)
            total = jnp.zeros((rows, 128), F32)
            acc = jnp.zeros((rows, 128), F32)
            for j in range(count):
                at = (first + qi + j) * rows
                e = jnp.exp(s_scr[:, j * rows : (j + 1) * rows] - m)
                for g in range(rows // 128):
                    total = total + e[:, g * 128 : (g + 1) * 128]
                acc = acc + nn(e.astype(BF), v_ref[0, at : at + rows, :])
            total = jnp.sum(total, axis=1, keepdims=True)
            outs.append(acc / total)
            lses.append(m + jnp.log(total))
        o = jnp.where(low, outs[0], outs[1])
        o_ref[0, qi * rows : (qi + 1) * rows, :] = o
        ol_ref[0, qi * rows : (qi + 1) * rows, :] = o.astype(BF)
        both = jnp.where(lanes((rows, 128)) == 0, lses[0], lses[1])
        lse_ref[0, :, qi * rows : (qi + 1) * rows] = both.T[0:8, :]


def mid_kernel(a_ref, w_ref, x_ref, g_ref, mid_ref, h_ref):
    mid = x_ref[...].astype(F32) + nn(a_ref[...], w_ref[...])
    mid_ref[...] = mid
    h_ref[...] = (mid * rms_scale(mid) * g_ref[...]).astype(BF)


def pre_kernel(nblk, rows, ix, og, p_ref, wd, dehid, ogx_t, ogx):
    cap = p_ref.shape[1]

    @pl.when(pl.program_id(0) == 0)
    def _():
        for b in range(nblk):
            block = og[ix[b], 0:rows, :]
            ogx[b * cap : (b + 1) * cap, :] = nn(p_ref[ix[b]], block).astype(BF)
        ogx_t[...] = ogx[...].T

    dehid[...] = nt(ogx[...], wd[...]).astype(BF)


def act(g, u, dh):
    s = 0.5 * jnp.tanh(0.5 * g) + 0.5
    silu = g * s
    hid = (silu * u).astype(BF)
    dg = (dh * u * (s + silu * (1.0 - s))).astype(BF)
    du = (dh * silu).astype(BF)
    return hid, dg, du


def expert_kernel(nblk, rows, experts, e_ref, ix, *refs):
    g_refs = refs[:nblk]
    (p_ref, pt_ref, wr, wr_t, wsg, wsu, wsd, og, wg, wu, dehid) = refs[nblk : nblk + 11]
    (x_out, g_out, ghid, degate, deup, shid, dsg, dsu, tg, tg_far, rgrad) = refs[nblk + 11 : nblk + 22]
    x_scr, row_scr, tg_scr, pg_scr, prob_scr, g_scr = refs[nblk + 22 :]
    cap = p_ref.shape[1]
    slots = nblk * cap
    step = pl.program_id(0)
    per = nblk // pl.num_programs(0)

    @pl.when(step == 0)
    def _():
        row_scr[...] = jnp.zeros_like(row_scr)
        pg_scr[...] = jnp.zeros_like(pg_scr)
        for b in range(nblk):
            block = g_refs[b][...]
            g_scr[b * rows : (b + 1) * rows, :] = block
            x_scr[b * cap : (b + 1) * cap, :] = nn(p_ref[ix[b]], block).astype(BF)
        logits = jnp.where(lanes((slots, 128)) < experts, nn(x_scr[...], wr[...]), NEG_LARGE)
        shifted = jnp.exp(logits - jnp.max(logits, axis=1, keepdims=True))
        prob_scr[...] = shifted / jnp.sum(shifted, axis=1, keepdims=True)

    own = lanes((slots, 128)) == e_ref[0]
    gate = jnp.sum(jnp.where(own, prob_scr[...], 0.0), axis=1, keepdims=True)
    raw = dehid[...].astype(F32)
    hid, dg, du = act(nn(x_scr[...], wg[0]), nn(x_scr[...], wu[0]), raw * gate)
    hid = hid.astype(F32)
    ghid[...] = (hid * gate).astype(BF)
    degate[...] = dg
    deup[...] = du
    row_scr[...] += nt(dg, wg[0]) + nt(du, wu[0])
    pg_scr[...] += jnp.sum(hid * raw, axis=1, keepdims=True)

    for k in range(per):
        b = step * per + k
        at = pl.multiple_of(b * rows, rows)
        block = g_scr[pl.ds(at, rows), :]
        g_out[k * rows : (k + 1) * rows, :] = block
        dsh = nt(og[ix[b], 0:rows, :], wsd[...])
        sh, sg, su = act(nn(block, wsg[...]), nn(block, wsu[...]), dsh)
        here = slice(k * rows, (k + 1) * rows)
        shid[here, :] = sh
        dsg[here, :] = sg
        dsu[here, :] = su
        tg_scr[pl.ds(at, rows), :] = nt(sg, wsg[...]) + nt(su, wsu[...])

    @pl.when(step == pl.num_programs(0) - 1)
    def _():
        x_out[...] = x_scr[...]
        lgrad = (pg_scr[:, 0:1] * prob_scr[...] * (own.astype(F32) - gate)).astype(BF)
        rgrad[...] = tn(lgrad, x_scr[...])
        total = (row_scr[...] + nn(lgrad, wr_t[...])).astype(BF)
        for b in range(nblk):
            back = nn(pt_ref[ix[b]], total[b * cap : (b + 1) * cap, :])
            (tg_far if b % 2 else tg)[b // 2] = (tg_scr[b * rows : (b + 1) * rows, :] + back).astype(BF)


def wgrad_kernel(per, r_ref, x_ref, degate, deup, gate_near, gate_far, up_near, up_far, x_t):
    step = pl.program_id(0)

    @pl.when(step == 0)
    def _():
        x_t[...] = x_ref[...].T

    @pl.when(step < 2 * per)
    def _():
        gate_near[0] = nn(x_t[...], degate[...]).astype(BF)
        up_near[0] = nn(x_t[...], deup[...]).astype(BF)

    @pl.when(step >= 2 * per)
    def _():
        gate_far[0] = nn(x_t[...], degate[...]).astype(BF)
        up_far[0] = nn(x_t[...], deup[...]).astype(BF)


def wgrad_all_kernel(r_ref, x_ref, degate, deup, gate, up, x_t):
    @pl.when(pl.program_id(0) == 0)
    def _():
        x_t[...] = x_ref[...].T

    gate[0] = nn(x_t[...], degate[...]).astype(BF)
    up[0] = nn(x_t[...], deup[...]).astype(BF)


def down_grad_kernel(ogx_t, ghid, dn):
    dn[...] = nn(ogx_t[...], ghid[...]).astype(BF)


def result_kernel(nblk, rows, ix_s, g_ref, og, pt_ref, shid, dsg, dsu, wsd, ghid, wd, mix, sgu, sd, acc, part, sg_acc, sd_acc):
    cap = pt_ref.shape[2]
    step = pl.program_id(0)
    per = nblk // pl.num_programs(0)
    width = dsg.shape[1]

    @pl.when(step == 0)
    def _():
        acc[...] = jnp.zeros_like(acc)
        sg_acc[...] = jnp.zeros_like(sg_acc)
        sd_acc[...] = jnp.zeros_like(sd_acc)

    acc[...] += nn(ghid[...], wd[0])
    sg_acc[:, :width] += tn(g_ref[...], dsg[...])
    sg_acc[:, width:] += tn(g_ref[...], dsu[...])
    for k in range(per):
        b = step * per + k
        here = slice(k * rows, (k + 1) * rows)
        sd_acc[...] += tn(shid[here, :], og[ix_s[b], 0:rows, :])
        part[pl.ds(pl.multiple_of(b * rows, rows), rows), :] = nn(shid[here, :], wsd[...])

    @pl.when(step == pl.num_programs(0) - 1)
    def _():
        sgu[...] = sg_acc[...].astype(BF)
        sd[...] = sd_acc[...].astype(BF)
        res = acc[...].astype(BF)
        for b in range(nblk):
            picked = nn(pt_ref[ix_s[b]], res[b * cap : (b + 1) * cap, :])
            mix[ix_s[b]] = (picked + part[b * rows : (b + 1) * rows, :]).astype(BF)


def mid_back_kernel(count, *refs):
    pieces = refs[:count]
    mid_ref, g_ref, og_ref, w_ref, mg_ref, ag_ref, da_ref, gg_ref = refs[count:]
    two = pieces[0][...].astype(F32)
    for piece in pieces[1:]:
        two += piece[...].astype(F32)
    mid = mid_ref[...]
    scale = rms_scale(mid)
    mn = mid * scale
    gg_ref[...] = jnp.broadcast_to(jnp.sum(two * mn, axis=0, keepdims=True), gg_ref.shape)
    dn = two * g_ref[...]
    mg = og_ref[...].astype(F32) + scale * (dn - mn * jnp.mean(dn * mn, axis=1, keepdims=True))
    mg_ref[...] = mg
    ag = mg.astype(BF)
    ag_ref[...] = ag
    da = nt(ag, w_ref[...]).astype(BF)
    for i in range(da_ref.shape[0]):
        da_ref[i] = da[:, 128 * i : 128 * i + 128]


def attend_back_kernel(first, count, rows, q_ref, k_ref, v_ref, o_ref, do_ref, lse_ref, sq_ref, sk_ref, cos, sin,
                       h1_ref, wq, wk, wv, gain, c_ref, grads, og_own, og_far, gg, h1_t, k_t, dk, dv, og_scr):
    step = pl.program_id(0)
    low = lanes((rows, 128)) < 64
    kv_rows = k_ref.shape[1]
    base = kv_rows - 2 * rows

    @pl.when(step == 0)
    def _():
        h1_t[...] = h1_ref[...].T
        og_scr[...] = jnp.zeros_like(og_scr)

    k_t[...] = k_ref[0].T
    dk[...] = jnp.zeros_like(dk)
    dv[...] = jnp.zeros_like(dv)
    dqs = []
    for qi in range(2):
        at_q = qi * rows
        qpair = q_ref[0, at_q : at_q + rows, :]
        dopair = do_ref[0, at_q : at_q + rows, :]
        prod = dopair.astype(F32) * o_ref[0, at_q : at_q + rows, :]
        d0 = jnp.sum(jnp.where(low, prod, 0.0), axis=1, keepdims=True)
        d1 = jnp.sum(jnp.where(low, 0.0, prod), axis=1, keepdims=True)
        delta = jnp.where(lanes((rows, 128)) == 0, d0, d1).T
        sq = sq_ref[0:1, at_q : at_q + rows]
        def masked(x):
            zero = jnp.zeros_like(x)
            return jnp.concatenate([jnp.where(low, x, zero), jnp.where(low, zero, x)], axis=0)

        q, do = masked(qpair), masked(dopair)
        lse_row = jnp.concatenate([lse_ref[0, h : h + 1, at_q : at_q + rows] for h in range(2)], axis=1)
        delta_row = jnp.concatenate([delta[h : h + 1, :] for h in range(2)], axis=1)
        sq = jnp.concatenate([sq, sq], axis=1)
        halves = [jnp.zeros((64, rows), F32) for _ in range(2)]
        for j in range(count):
            at = (first + qi + j) * rows
            same = sk_ref[at : at + rows, 0:1] == sq
            s = nt(k_ref[0, at : at + rows, :], q)
            p = jnp.where(same, jnp.exp(s - lse_row), 0.0)
            dp = nt(v_ref[0, at : at + rows, :], do)
            ds = (p * (dp - delta_row)).astype(BF)
            dv[at : at + rows, :] += nn(p.astype(BF), do)
            dk[at : at + rows, :] += nn(ds, q)
            for h in range(2):
                halves[h] += nn(k_t[64 * h : 64 * h + 64, at : at + rows], ds[:, h * rows : (h + 1) * rows])
        dq = jnp.concatenate(halves, axis=0).T * 0.125
        at = base + at_q
        dq = dq * cos[at : at + rows, :] - turned(dq) * sin[at : at + rows, :]
        dqs.append(dq.astype(BF))
    dq = jnp.concatenate(dqs, axis=0)
    dkv = dk[...]
    dkb = (dkv * cos[...] - turned(dkv) * sin[...]).astype(BF)
    dvb = dv[...].astype(BF)
    grads[0, 0] = nn(h1_t[:, base:], dq).astype(BF)
    grads[0, 1] = nn(h1_t[...], dkb).astype(BF)
    grads[0, 2] = nn(h1_t[...], dvb).astype(BF)
    og_scr[...] += nt(dkb, wk[...]) + nt(dvb, wv[...])
    og_scr[base:, :] += nt(dq, wq[...])

    @pl.when(step == pl.num_programs(0) - 1)
    def _():
        one = og_scr[...]
        for slot in range(kv_rows // rows):
            block = one[slot * rows : (slot + 1) * rows, :].astype(BF)

            @pl.when(c_ref[0] == slot % 2)
            def _():
                og_own[slot // 2] = block

            @pl.when(c_ref[0] != slot % 2)
            def _():
                og_far[slot // 2] = block

        total = jnp.sum(one * h1_ref[...].astype(F32), axis=0, keepdims=True) / gain[...]
        gg[...] = jnp.broadcast_to(total, gg.shape)


def last_kernel(count, *refs):
    pieces = refs[:count]
    x_ref, g_ref, mg_ref, out = refs[count:]
    one = pieces[0][...].astype(F32)
    for piece in pieces[1:]:
        one += piece[...].astype(F32)
    x = x_ref[...].astype(F32)
    scale = rms_scale(x)
    xn = x * scale
    dn = one * g_ref[...]
    out[...] = mg_ref[...] + scale * (dn - xn * jnp.mean(dn * xn, axis=1, keepdims=True))


def shape(dims, dtype=BF):
    return jax.ShapeDtypeStruct(dims, dtype)


def shards(
    R,
    E,
    tokens,
    segment_ids,
    routes,
    norm1_gain,
    w_query,
    w_key,
    w_value,
    w_out,
    norm2_gain,
    w_router,
    shared_gate,
    shared_up,
    shared_down,
    expert_gate,
    expert_up,
    expert_down,
    out_grad,
):
    Z = E // 2
    T, D = tokens.shape
    FF = shared_gate.shape[1]
    topk = routes.shape[1]
    experts = w_router.shape[1]
    assert expert_gate.shape[0] == 1 and experts == E
    half = D // 2
    pairs = half // 128
    wrow = w_query.shape[0]
    hrow = 2 * wrow
    cap = 2 * T * topk // experts
    slots = E * cap
    fs = FF // E
    drow = shared_down.shape[0]
    longest = E * T // 2
    back = -(-(longest - 1) // T)
    nb = -(-back // 2)
    chips = nb + 1
    kvb = 2 * chips
    first = 2 * nb - back
    count = back + 1
    r = lax.axis_index("rep")
    e = lax.axis_index("ep")
    z, c = e // 2, e % 2
    is0 = c == 0
    c_arr = jnp.reshape(c, (1,)).astype(jnp.int32)
    e_arr = jnp.reshape(e, (1,)).astype(jnp.int32)

    def swap(x):
        return lax.ppermute(x, "ep", [(i, i ^ 1) for i in range(E)])

    def ring(x, s):
        return lax.ppermute(x, "ep", [(i, (i + 2 * s) % E) for i in range(E)])

    def line(x, s):
        return lax.ppermute(x, "ep", [(i, i + 2 * s) for i in range(E) if 0 <= i + 2 * s < E])

    def cross(x, s):
        return lax.ppermute(x, "rep", [(i, i ^ s) for i in range(R)])

    def ordered(mine, other):
        return jnp.where(is0, mine, other), jnp.where(is0, other, mine)

    def put(buf, x, i):
        return lax.dynamic_update_index_in_dim(buf, x, i, 0)

    def chip_pack(mats, extra):
        stacked = jnp.stack(mats).reshape(len(mats) * wrow, D)
        mine, other = ordered(stacked[:, :half], stacked[:, half:])
        ext = jnp.pad(extra.reshape(1, -1), ((0, 0), (0, half - extra.size)))
        got = swap(jnp.concatenate([other, ext], axis=0))
        a, b = ordered(mine, got[:-1])
        ea, eb = ordered(ext, got[-1:])
        rows = jnp.stack([a.reshape(-1, wrow, half), b.reshape(-1, wrow, half)], axis=1).reshape(-1, half)
        rows = jnp.concatenate([rows, ea, eb], axis=0)
        return jnp.pad(rows, ((0, -rows.shape[0] % 16), (0, 0)))

    def gather_z(pack):
        buf = put(jnp.zeros((Z,) + pack.shape, BF), pack, z)
        for s in range(1, Z):
            buf = put(buf, ring(pack, s), (z - s) % Z)
        return buf

    def gather_rep(part, *deps):
        got = [cross(part, s) for s in range(1, R)]
        if deps:
            got = [after(x, *deps) for x in got]
        buf = put(jnp.zeros((R,) + part.shape, BF), part, r)
        for s in range(1, R):
            buf = put(buf, got[s - 1], r ^ s)
        return buf

    def unpack(full, i):
        return full[:, :, i * hrow : (i + 1) * hrow, :].reshape(D, half)

    pack = chip_pack(
        [w_query, w_key, w_value, w_out], jnp.concatenate([norm1_gain, norm2_gain, w_router.reshape(-1)])
    )
    part = gather_z(pack)
    full = gather_rep(part)
    wq, wk, wv, wo_half = (unpack(full, i) for i in range(4))
    ext = full[:, :, 4 * hrow : 4 * hrow + 2, :].reshape(R * E, half)
    gain1 = ext[:, :wrow].reshape(1, D).astype(F32)
    gain2 = ext[:, wrow : 2 * wrow].reshape(1, D).astype(F32)
    router = ext[:, 2 * wrow : (2 + experts) * wrow].reshape(D, experts)
    router = jnp.pad(router, ((0, 0), (0, 128 - experts)))
    router_t = router.T

    seg_row = jnp.pad(segment_ids.reshape(1, T).astype(BF), ((0, 7), (0, D - T)))
    tok_pack = after(jnp.concatenate([tokens, seg_row], axis=0), pack)
    own_tok = [tok_pack] + [line(tok_pack, s) for s in range(1, chips)]
    par_tok = [swap(x) for x in own_tok]

    seg_blocks = [None] * kvb
    for s in range(chips):
        valid = z - s >= 0
        a, b = ordered(own_tok[s][T, :T], par_tok[s][T, :T])
        seg_blocks[2 * (nb - s)] = jnp.where(valid, a.astype(F32), -1.0)
        seg_blocks[2 * (nb - s) + 1] = jnp.where(valid, b.astype(F32), -1.0)
    segs = jnp.stack(seg_blocks)
    kv_rows = kvb * T
    seg_flat = segs.reshape(1, kv_rows)
    seg_wide = jnp.broadcast_to(segs.reshape(kv_rows, 1), (kv_rows, 128))

    inverse = jnp.exp(jnp.arange(32).astype(F32) * (-2.0 * math.log(10000.0) / 64))
    inverse = jnp.tile(inverse, 4)
    places = after((z - nb) * (2 * T) + jnp.arange(kv_rows, dtype=jnp.int32), pack)
    angle = places.astype(F32)[:, None] * inverse[None, :]
    cos, sin = lax.optimization_barrier((jnp.cos(angle), jnp.sin(angle)))
    cos, sin = cos.reshape(kvb, T, 128), sin.reshape(kvb, T, 128)

    h1, keys, vals, quer = pl.pallas_call(
        functools.partial(qkv_kernel, chips, T),
        in_specs=[pl.BlockSpec(memory_space=pltpu.SMEM)] + vmem(2 * chips + 6),
        out_specs=tuple(vmem(4)),
        out_shape=(
            shape((kvb, T, D)),
            shape((pairs, kvb, T, 128)),
            shape((pairs, kvb, T, 128)),
            shape((pairs, 2, T, 128)),
        ),
        compiler_params=params(),
        name="qkv",
        cost_estimate=cost(8),
    )(c_arr, *own_tok, *par_tok, wq, wk, wv, cos, sin, gain1)
    h1 = h1.reshape(kv_rows, D)
    keys = keys.reshape(pairs, kv_rows, 128)
    vals = vals.reshape(pairs, kv_rows, 128)
    quer = quer.reshape(pairs, 2 * T, 128)

    og_pack = jnp.concatenate(
        [out_grad, jnp.pad(routes.reshape(1, topk * T).astype(BF), ((0, 7), (0, D - topk * T)))], axis=0
    )
    og_all = lax.all_gather(after(og_pack, own_tok[-1]), "ep", axis=0)
    ix_arr = jnp.stack([((z - b // 2) % Z) * 2 + (c ^ (b % 2)) for b in range(E)]).astype(jnp.int32)

    wo = jnp.concatenate(ordered(wo_half, swap(wo_half)), axis=1)

    def by_unit(w):
        return w.reshape(wrow, R, E, drow).transpose(2, 0, 1, 3).reshape(E, wrow, fs)

    gu = jnp.concatenate([by_unit(shared_gate), by_unit(shared_up)], axis=2)
    gu = lax.all_to_all(after(gu, part), "ep", split_axis=0, concat_axis=0, tiled=True).reshape(E * wrow, 2 * fs)
    gu = after(gu, keys)
    wide = D // fs
    shared = jnp.concatenate(
        [gu[:, :fs], gu[:, fs:]] + [shared_down[:, k * fs : (k + 1) * fs] for k in range(wide)], axis=0
    )
    one = lambda *dims: pl.BlockSpec((1,) + dims, lambda i: (i, 0, 0))
    att, att_low, lse = pl.pallas_call(
        functools.partial(attend_kernel, first, count, T),
        grid=(pairs,),
        in_specs=[
            one(2 * T, 128),
            one(kv_rows, 128),
            one(kv_rows, 128),
            whole((2 * T, 128)),
            whole((1, kv_rows)),
        ],
        out_specs=(one(2 * T, 128), one(2 * T, 128), one(8, 2 * T)),
        out_shape=(
            shape((pairs, 2 * T, 128), F32),
            shape((pairs, 2 * T, 128)),
            shape((pairs, 8, 2 * T), F32),
        ),
        scratch_shapes=[pltpu.VMEM((T, count * T), F32)],
        compiler_params=params(),
        name="attend",
        cost_estimate=cost(10),
    )(after(quer, wo, shared), keys, vals, seg_wide[-2 * T :], seg_flat)

    def joined(mine, other):
        both = jnp.where(is0, jnp.concatenate([mine, other]), jnp.concatenate([other, mine]))
        return both.transpose(1, 0, 2).reshape(T, D)

    att_own, att_other = ordered(att_low[:, :T], att_low[:, T:])
    attended = joined(att_own, swap(att_other))
    mid, h2 = pl.pallas_call(
        mid_kernel,
        in_specs=vmem(4),
        out_specs=tuple(vmem(2)),
        out_shape=(shape((T, D), F32), shape((T, D))),
        compiler_params=params(),
        name="mid",
        cost_estimate=cost(3),
    )(attended, wo, tokens, gain2)

    h2_lane = [h2] + [None] * (Z - 1)
    h2_lane[1] = ring(h2, 1)
    for s in range(Z - 1, Z // 2, -1):
        h2_lane[s] = ring(h2 if s == Z - 1 else h2_lane[s + 1], -1)

    def both_cores(lane):
        blocks = []
        for item in lane:
            blocks += [item, swap(item)]
        return blocks

    og_all = after(og_all, h2)
    table = og_all[:, T, : topk * T].reshape(E, T, topk)
    hit = jnp.any(table == e.astype(F32).astype(BF), axis=2).astype(F32)
    rank = jnp.cumsum(hit, axis=1) - hit
    rank = jnp.where(hit > 0, rank, -1.0)
    slot_ids = jnp.arange(cap).astype(F32)
    pick = (rank[:, None, :] == slot_ids[None, :, None]).astype(BF)
    pick_t = (rank[:, :, None] == slot_ids[None, None, :]).astype(BF)

    smem = pl.BlockSpec(memory_space=pltpu.SMEM)
    ft = min(512, FF // R)
    steps = FF // ft
    per = FF // R // ft
    col = lambda n: pl.BlockSpec((n, ft), lambda i: (0, i))
    wcol = pl.BlockSpec((1, D, ft), lambda i: (0, 0, i))
    block_of = lambda n: pl.BlockSpec((E // steps * T, n), lambda i: (i, 0))
    wdn = pl.BlockSpec((1, ft, D), lambda i: (0, i, 0))
    dehid, ogx_t = pl.pallas_call(
        functools.partial(pre_kernel, E, T),
        grid=(steps,),
        in_specs=[smem, whole((E, T + 8, D))]
        + [whole((E, cap, T)), pl.BlockSpec((ft, D), lambda i: (i, 0))],
        out_specs=(col(slots), whole((D, slots))),
        out_shape=(shape((slots, FF)), shape((D, slots))),
        scratch_shapes=[pltpu.VMEM((slots, D), BF)],
        compiler_params=params(),
        name="pre",
        cost_estimate=cost(12),
    )(ix_arr, og_all, pick, expert_down.reshape(FF, D))

    shared_part = after(shared, pick)
    shared_got = [cross(shared_part, s) for s in range(1, R)]
    shared = put(jnp.zeros((R,) + shared.shape, BF), after(shared_part, dehid), r)
    for i in range(1, R):
        shared = put(shared, after(shared_got[i - 1], dehid), r ^ i)
    gr = E * wrow
    wsg = shared[:, :gr].reshape(D, fs)
    wsu = shared[:, gr : 2 * gr].reshape(D, fs)
    wsd = jnp.concatenate(
        [shared[:, 2 * gr + k * drow : 2 * gr + (k + 1) * drow].reshape(fs, fs) for k in range(wide)], axis=1
    )
    h2_lane[1] = after(h2_lane[1], dehid)
    for s in range(2, Z // 2 + 1):
        h2_lane[s] = ring(h2_lane[s - 1], 1)
    h2_blocks = both_cores([h2_lane[s] if 0 < s <= Z // 2 else after(h2_lane[s], dehid) for s in range(Z)])
    (x_rows, g_rows, ghid, degate, deup, shid, dsg, dsu, tg, tg_far, rgrad) = pl.pallas_call(
        functools.partial(expert_kernel, E, T, experts),
        grid=(steps,),
        in_specs=[smem, smem]
        + [whole((T, D))] * E
        + [
            whole((E, cap, T)),
            whole((E, T, cap)),
            whole((D, 128)),
            whole((128, D)),
            whole((D, fs)),
            whole((D, fs)),
            whole((fs, D)),
            whole((E, T + 8, D)),
            wcol,
            wcol,
            col(slots),
        ],
        out_specs=(
            whole((slots, D)),
            block_of(D),
            col(slots),
            col(slots),
            col(slots),
            block_of(fs),
            block_of(fs),
            block_of(fs),
            whole((Z, T, D)),
            whole((Z, T, D)),
            whole((128, D)),
        ),
        out_shape=(
            shape((slots, D)),
            shape((E * T, D)),
            shape((slots, FF)),
            shape((slots, FF)),
            shape((slots, FF)),
            shape((E * T, fs)),
            shape((E * T, fs)),
            shape((E * T, fs)),
            shape((Z, T, D)),
            shape((Z, T, D)),
            shape((128, D), F32),
        ),
        scratch_shapes=[
            pltpu.VMEM((slots, D), BF),
            pltpu.VMEM((slots, D), F32),
            pltpu.VMEM((E * T, D), F32),
            pltpu.VMEM((slots, 128), F32),
            pltpu.VMEM((slots, 128), F32),
            pltpu.VMEM((E * T, D), BF),
        ],
        compiler_params=params(),
        name="expert",
        cost_estimate=cost(38),
    )(e_arr, ix_arr, *h2_blocks, pick, pick_t, router, router_t, wsg, wsu, wsd, og_all, expert_gate, expert_up, dehid)

    def core_sums(mine, other, *deps):
        got = swap(other)
        if deps:
            got = after(got, *deps)
        return [mine[s] + got[s] for s in range(Z)]


    r_arr = jnp.reshape(r, (1,)).astype(jnp.int32)
    wide_rep = FF // R
    square = R == 4
    at0 = lambda n: pl.BlockSpec(n, lambda i, q: (0,) * len(n))
    dn_grad = pl.pallas_call(
        down_grad_kernel,
        grid=(steps,),
        in_specs=[whole((D, slots)), col(slots)],
        out_specs=col(D),
        out_shape=shape((D, FF)),
        compiler_params=params(),
        name="dgrad",
        cost_estimate=cost(10),
    )(ogx_t, ghid)
    dn_sum = lax.psum_scatter(dn_grad, "rep", scatter_dimension=0, tiled=True)
    lane = core_sums(tg, tg_far, dn_grad)
    two_parts = [lane[0]] + [ring(lane[s], -s) for s in range(1, Z)]

    if square:

        def rel_col(swapped):
            def index(i, q):
                d = i // per
                d = (d % 2) * 2 + d // 2 if swapped else d
                return (0, (d ^ q[0]) * per + i % per)

            return pl.BlockSpec((slots, ft), index)

        early = pl.BlockSpec(
            (1, D, ft),
            lambda i, q: (jnp.minimum(i // per, 1), 0, jnp.where(i < 2 * per, i % per, per - 1)),
        )
        late = pl.BlockSpec(
            (1, D, ft),
            lambda i, q: (jnp.maximum(i // per - 2, 0), 0, jnp.where(i < 2 * per, 0, i % per)),
        )
        gu_in = [rel_col(True), rel_col(False)]
        gu_specs = (early, late, early, late)
        gu_shapes = [(2, D, wide_rep)] * 4
        gu_kernel = functools.partial(wgrad_kernel, per)
    else:
        gu_in = [pl.BlockSpec((slots, ft), lambda i, q: (0, ((i // per) ^ q[0]) * per + i % per))] * 2
        gu_specs = (pl.BlockSpec((1, D, ft), lambda i, q: (i // per, 0, i % per)),) * 2
        gu_shapes = [(R, D, wide_rep)] * 2
        gu_kernel = wgrad_all_kernel
    gu_out = pl.pallas_call(
        gu_kernel,
        grid_spec=pltpu.PrefetchScalarGridSpec(
            num_scalar_prefetch=1,
            grid=(steps,),
            in_specs=[at0((slots, D))] + gu_in,
            out_specs=gu_specs,
            scratch_shapes=[pltpu.VMEM((D, slots), BF)],
        ),
        out_shape=tuple(shape(dims) for dims in gu_shapes),
        compiler_params=params(),
        name="wgrad",
        cost_estimate=cost(13),
    )(r_arr, after(x_rows, *lane), degate, deup)

    def pieces(x):
        return [lax.dynamic_index_in_dim(x, r ^ s, 0, keepdims=False) for s in range(R)]

    def direct(pieces, *deps):
        total = pieces[0].astype(F32)
        for d in range(1, R):
            got = cross(pieces[d], d)
            total += (after(got, *deps) if deps else got).astype(F32)
        return total

    two_parts[1] = after(two_parts[1], gu_out[0])
    near = []
    if square:
        gate_a, up_a = cross(gu_out[1][0], 1), cross(gu_out[3][0], 2)
    mix, sgu_grad, sd_grad = pl.pallas_call(
        functools.partial(result_kernel, E, T),
        grid=(steps,),
        in_specs=[
            smem,
            block_of(D),
            whole((E, T + 8, D)),
            whole((E, T, cap)),
            block_of(fs),
            block_of(fs),
            block_of(fs),
            whole((fs, D)),
            col(slots),
            wdn,
        ],
        out_specs=(whole((E, T, D)), whole((D, 2 * fs)), whole((fs, D))),
        out_shape=(shape((E, T, D)), shape((D, 2 * fs)), shape((fs, D))),
        scratch_shapes=[
            pltpu.VMEM((slots, D), F32),
            pltpu.VMEM((E * T, D), F32),
            pltpu.VMEM((D, 2 * fs), F32),
            pltpu.VMEM((fs, D), F32),
        ],
        compiler_params=params(),
        name="result",
        cost_estimate=cost(14),
    )(ix_arr, g_rows, og_all, pick_t, shid, dsg, dsu, wsd, after(ghid, gu_out[0], two_parts[1], *near), expert_down)

    sgrad = jnp.concatenate(
        [sgu_grad[:, :fs].reshape(R, gr, fs), sgu_grad[:, fs:].reshape(R, gr, fs)]
        + [sd_grad[:, k * fs : (k + 1) * fs].reshape(R, drow, fs) for k in range(wide)],
        axis=1,
    )
    two_parts[2:] = [after(x, mix) for x in two_parts[2:]]
    if square:
        gate_a, up_a = after(gate_a, mix), after(up_a, mix)
        two_parts[0], gate_a, up_a = lax.optimization_barrier((two_parts[0], gate_a, up_a))
        gate_c, up_c = cross(after(gu_out[1][1], mix), 1), cross(after(gu_out[3][1], mix), 2)

    mix_in = after(mix, two_parts[2], *((gate_a, up_a) if square else ()))
    mix_sum = lax.psum_scatter(mix_in.reshape(E * T, D), "ep", scatter_dimension=0, tiled=True)

    mid_grad, attn_grad, att_grad, gain2_part = pl.pallas_call(
        functools.partial(mid_back_kernel, Z),
        in_specs=vmem(Z + 4),
        out_specs=tuple(vmem(4)),
        out_shape=(shape((T, D), F32), shape((T, D)), shape((2 * pairs, T, 128)), shape((8, D), F32)),
        compiler_params=params(),
        name="mid_back",
        cost_estimate=cost(4),
    )(*two_parts, mid, gain2, out_grad, wo)

    ag_own, ag_other = ordered(att_grad[:pairs], att_grad[pairs:])
    do_a, do_b = ordered(ag_own, swap(ag_other))
    do = jnp.concatenate([do_a, do_b], axis=1)
    wo_part = tn(attended, after(attn_grad, ag_other)).astype(BF)
    wo_mine, wo_other = ordered(wo_part[:, :half], wo_part[:, half:])
    wo_got = swap(wo_other)
    if square:
        gate_mid = gu_out[0][1] + after(gate_c, do)
        up_mid = gu_out[2][1] + after(up_c, do)
        gate_b, up_b = cross(gate_mid, 2), cross(up_mid, 1)
        sg_own, sg_near, sg_a, sg_c = pieces(after(sgrad, do))
        sg_send = jnp.stack([sg_a, sg_c])
        sg_got = cross(sg_send, 2)
        do, gate_mid, up_mid, wo_other, sg_send = lax.optimization_barrier(
            (do, gate_mid, up_mid, wo_other, sg_send)
        )

    cos2, sin2 = cos.reshape(kv_rows, 128), sin.reshape(kv_rows, 128)
    grads, og1, og1_far, gain1_part = pl.pallas_call(
        functools.partial(attend_back_kernel, first, count, T),
        grid=(pairs,),
        in_specs=[
            one(2 * T, 128),
            one(kv_rows, 128),
            one(kv_rows, 128),
            one(2 * T, 128),
            one(2 * T, 128),
            one(8, 2 * T),
            whole((1, 2 * T)),
            whole((kv_rows, 128)),
            whole((kv_rows, 128)),
            whole((kv_rows, 128)),
            whole((kv_rows, D)),
            pl.BlockSpec((D, 128), lambda i: (0, i)),
            pl.BlockSpec((D, 128), lambda i: (0, i)),
            pl.BlockSpec((D, 128), lambda i: (0, i)),
            whole((1, D)),
            smem,
        ],
        out_specs=(
            pl.BlockSpec((1, 3, D, 128), lambda i: (i, 0, 0, 0)),
            whole((chips, T, D)),
            whole((chips, T, D)),
            whole((8, D)),
        ),
        out_shape=(shape((pairs, 3, D, 128)), shape((chips, T, D)), shape((chips, T, D)), shape((8, D), F32)),
        scratch_shapes=[
            pltpu.VMEM((D, kv_rows), BF),
            pltpu.VMEM((128, kv_rows), BF),
            pltpu.VMEM((kv_rows, 128), F32),
            pltpu.VMEM((kv_rows, 128), F32),
            pltpu.VMEM((kv_rows, D), F32),
        ],
        compiler_params=params(),
        name="attend_back",
        cost_estimate=cost(30),
    )(quer, keys, vals, att, do, lse, seg_flat[:, -2 * T :], seg_wide, cos2, sin2, h1, wq, wk, wv, gain1, c_arr)

    wo_got = after(wo_got, og1)
    if square:
        gate_b, up_b, sg_got = after(gate_b, og1), after(up_b, og1), after(sg_got, og1)
        og1_far, grads, gate_b, up_b, wo_got, sg_got = lax.optimization_barrier(
            (og1_far, grads, gate_b, up_b, wo_got, sg_got)
        )
    far_got = swap(og1_far)
    if square:
        sg_mid = cross(sg_near + sg_got[1], 1)
        sg_mid, far_got = lax.optimization_barrier((sg_mid, far_got))
    lane = og1 + far_got
    one_moved = lane[0]
    for i in range(1, nb):
        one_moved = lane[i] + line(one_moved, -1)
    one_parts = [lane[nb], line(one_moved, -1)]

    n_chip = R * Z

    def dense_pack(groups, ext):
        rows = groups.reshape(-1, n_chip, hrow, 128).transpose(1, 0, 2, 3).reshape(n_chip, -1, 128)
        ext = ext.astype(BF)
        ext = jnp.pad(ext, ((0, 0), (0, -ext.shape[1] % 128))).reshape(n_chip, -1, 128)
        rows = jnp.concatenate([rows, ext], axis=1)
        return jnp.pad(rows, ((0, 0), (0, -rows.shape[1] % 8), (0, 0))).reshape(R, Z, -1, 128)

    wo_lane = wo_mine + wo_got
    wo_groups = wo_lane.reshape(D, pairs, 128).transpose(1, 0, 2)
    ext = jnp.concatenate(
        [
            gain1_part[0].reshape(n_chip, hrow),
            gain2_part[0].reshape(n_chip, hrow),
            rgrad[:experts].reshape(experts, n_chip, hrow).transpose(1, 0, 2).reshape(n_chip, experts * hrow),
        ],
        axis=1,
    )

    groups = 4 * pairs
    pack_d = dense_pack(jnp.concatenate([grads.reshape(-1, D, 128), wo_groups]), ext)
    send_d = pieces(pack_d)
    got_d = [after(cross(send_d[s], s), *one_parts[1:]) for s in range(1, R)]
    total_d = send_d[0].astype(F32)
    for x in got_d:
        total_d += x.astype(F32)
    total_d = total_d.astype(BF)
    if square:
        sgrad = sg_own.astype(F32) + sg_got[0].astype(F32) + sg_mid.astype(F32)
    else:
        sgrad = lax.psum_scatter(sgrad.reshape(-1, fs), "rep", scatter_dimension=0, tiled=True).astype(F32)
    sd_sum = jnp.concatenate(
        [sgrad[2 * gr + k * drow : 2 * gr + (k + 1) * drow] for k in range(wide)], axis=1
    )
    sgu = jnp.concatenate([sgrad[:gr], sgrad[gr : 2 * gr]], axis=1).astype(BF)
    sgu = sgu.reshape(Z, hrow, -1, 128).transpose(0, 2, 1, 3).reshape(Z, -1, 128)
    rows_d = total_d.shape[1]
    to_z = jnp.concatenate([total_d, sgu], axis=1)
    z_own = lax.dynamic_index_in_dim(to_z, z, 0, keepdims=False)
    z_got = [ring(lax.dynamic_index_in_dim(to_z, (z + s) % Z, 0, keepdims=False), s) for s in range(1, Z)]

    if square:
        gate_sum = gu_out[0][0].astype(F32) + (gate_a.astype(F32) + after(gate_b, lane).astype(F32))
        up_sum = gu_out[2][0].astype(F32) + (up_a.astype(F32) + after(up_b, lane).astype(F32))
    else:
        gate_sum, up_sum = (direct(x, lane) for x in gu_out)
    dn_sum = after(dn_sum, lane).T.astype(F32)
    layer_out = (mid + after(mix_sum, lane).astype(F32)).astype(BF)
    done = [gate_sum, up_sum, dn_sum, layer_out, sd_sum, to_z]
    one_parts[0], *done = lax.optimization_barrier((one_parts[0], *done))
    gate_sum, up_sum, dn_sum, layer_out, sd_sum, to_z = done
    tokens_grad = pl.pallas_call(
        functools.partial(last_kernel, 2),
        in_specs=vmem(5),
        out_specs=vmem(1)[0],
        out_shape=shape((T, D), F32),
        compiler_params=params(),
        name="last",
        cost_estimate=cost(3),
    )(*one_parts, tokens, gain1, mid_grad)

    z_got = [after(x, tokens_grad) for x in z_got]
    total = z_own[:rows_d].astype(F32)
    for x in z_got:
        total += x[:rows_d].astype(F32)
    sg_from = put(jnp.zeros((Z,) + sgu.shape[1:], BF), z_own[rows_d:], z)
    for s in range(1, Z):
        sg_from = put(sg_from, z_got[s - 1][rows_d:], (z - s) % Z)
    sg_groups = Z * (2 * fs // 128)
    mats_all, ext_all = total[: groups * hrow], total[groups * hrow :]
    rows_all = jnp.concatenate([mats_all, sg_from.reshape(-1, 128).astype(F32)])
    rows_all = rows_all.reshape(groups + sg_groups, 2, wrow, 128)
    mine, other = ordered(rows_all[:, 0], rows_all[:, 1])
    got = swap(jnp.concatenate([other.reshape(-1, 128), ext_all], axis=0).astype(BF)).astype(F32)
    count_rows = (groups + sg_groups) * wrow
    left, right = ordered(mine, got[:count_rows].reshape(-1, wrow, 128))
    ext_all = ext_all + got[count_rows:]
    ext_all = ext_all.reshape(-1)[: (2 + experts) * hrow].reshape(2 + experts, 2, wrow)
    ext_all = jnp.where(is0, ext_all[:, 0], ext_all[:, 1])

    def joined_mat(indices):
        return jnp.concatenate([left[i] for i in indices] + [right[i] for i in indices], axis=1)

    mats = [joined_mat([3 * p + m for p in range(pairs)]) for m in range(3)]
    mats.append(joined_mat([3 * pairs + p for p in range(pairs)]))

    sg = jnp.stack([left[groups:].reshape(Z, -1, wrow, 128), right[groups:].reshape(Z, -1, wrow, 128)], axis=1)
    sg = sg.reshape(E, 2, fs // 128, wrow, 128)

    def units_back(x):
        x = x.transpose(0, 2, 1, 3).reshape(E, wrow, R, drow)
        return x.transpose(1, 2, 0, 3).reshape(wrow, FF)

    sg_sum, su_sum = units_back(sg[:, 0]), units_back(sg[:, 1])

    return (
        layer_out,
        tokens_grad,
        ext_all[0],
        mats[0],
        mats[1],
        mats[2],
        mats[3],
        ext_all[1],
        ext_all[2:].T,
        sg_sum,
        su_sum,
        sd_sum,
        gate_sum[None],
        up_sum[None],
        dn_sum[None],
    )


def solution(mesh):
    rows = P(("rep", "ep"), None)
    flat = P(("rep", "ep"))
    expert = P("ep", None, None)
    expert_out = P("ep", None, "rep")
    return jax.shard_map(
        functools.partial(shards, mesh.shape["rep"], mesh.shape["ep"]),
        mesh=mesh,
        in_specs=(rows, P("rep", "ep"), rows, flat, rows, rows, rows, rows, flat)
        + (rows,) * 4
        + (expert,) * 3
        + (rows,),
        out_specs=(rows, rows, flat, rows, rows, rows, rows, flat)
        + (rows,) * 4
        + (expert_out,) * 3,
        check_vma=False,
    )
```

```python
import functools
import math

import jax
import jax.numpy as jnp
from jax import lax
from jax.experimental import pallas as pl
from jax.experimental.pallas import tpu as pltpu
from jax.sharding import PartitionSpec as P

HEADS = 12
EPSILON = 1e-06
NEG_LARGE = -1e30
BF = jnp.bfloat16
F32 = jnp.float32
VMEM_LIMIT = 58 * 1024 * 1024


def nn(a, b):
    return lax.dot_general(a, b, (((1,), (0,)), ((), ())), preferred_element_type=F32)


def nt(a, b):
    return lax.dot_general(a, b, (((1,), (1,)), ((), ())), preferred_element_type=F32)


def tn(a, b):
    return lax.dot_general(a, b, (((0,), (0,)), ((), ())), preferred_element_type=F32)


def rms_scale(values):
    return lax.rsqrt(jnp.mean(values * values, axis=1, keepdims=True) + EPSILON)


def lanes(shape):
    return lax.broadcasted_iota(jnp.int32, shape, len(shape) - 1)


def turned(x):
    front = lanes(x.shape) % 64 < 32
    return jnp.where(front, -pltpu.roll(x, 96, 1), pltpu.roll(x, 32, 1))


def vmem(n):
    return [pl.BlockSpec(memory_space=pltpu.VMEM)] * n


def params(**kw):
    return pltpu.CompilerParams(vmem_limit_bytes=VMEM_LIMIT, **kw)


def cost(micros):
    return pl.CostEstimate(flops=int(micros * 1.1e9), bytes_accessed=int(micros * 1e5), transcendentals=0)


def after(x, *deps):
    return lax.optimization_barrier((x,) + deps)[0]


def whole(shape):
    return pl.BlockSpec(shape, lambda *_: (0,) * len(shape))


def qkv_kernel(chips, rows, c_ref, *refs):
    own, par = refs[:chips], refs[chips : 2 * chips]
    wq, wk, wv, cos, sin, gain, h1, keys, vals, quer = refs[2 * chips :]
    c = c_ref[0]
    pairs = keys.shape[0]
    scale = 0.125
    for s in range(chips):
        for p, src in ((0, own[s]), (1, par[s])):
            core = c if p == 0 else 1 - c
            slot = 2 * (chips - 1 - s) + core
            x = src[0:rows, :].astype(F32)
            h = (x * rms_scale(x) * gain[...]).astype(BF)
            h1[slot] = h
            co, si = cos[slot], sin[slot]
            k = nn(h, wk[...])
            v = nn(h, wv[...])
            for i in range(pairs):
                kp = k[:, 128 * i : 128 * i + 128]
                keys[i, slot] = (kp * co + turned(kp) * si).astype(BF)
                vals[i, slot] = v[:, 128 * i : 128 * i + 128].astype(BF)
            if s == 0:
                q = nn(h, wq[...])
                for i in range(pairs):
                    qp = q[:, 128 * i : 128 * i + 128]
                    quer[i, core] = ((qp * co + turned(qp) * si) * scale).astype(BF)


def attend_kernel(first, count, rows, q_ref, k_ref, v_ref, sq_ref, sk_ref, o_ref, ol_ref, lse_ref, s_scr):
    low = lanes((rows, 128)) < 64
    for qi in range(2):
        qpair = q_ref[0, qi * rows : (qi + 1) * rows, :]
        sq = sq_ref[qi * rows : (qi + 1) * rows, 0:1]
        outs, lses = [], []
        for hh in range(2):
            keep = low if hh == 0 else jnp.logical_not(low)
            q = jnp.where(keep, qpair, jnp.zeros_like(qpair))
            m = jnp.full((rows, 128), NEG_LARGE, F32)
            for j in range(count):
                at = (first + qi + j) * rows
                s = nt(q, k_ref[0, at : at + rows, :])
                s = jnp.where(sq == sk_ref[0:1, at : at + rows], s, NEG_LARGE)
                s_scr[:, j * rows : (j + 1) * rows] = s
                for g in range(rows // 128):
                    m = jnp.maximum(m, s[:, g * 128 : (g + 1) * 128])
            m = jnp.max(m, axis=1, keepdims=True)
            total = jnp.zeros((rows, 128), F32)
            acc = jnp.zeros((rows, 128), F32)
            for j in range(count):
                at = (first + qi + j) * rows
                e = jnp.exp(s_scr[:, j * rows : (j + 1) * rows] - m)
                for g in range(rows // 128):
                    total = total + e[:, g * 128 : (g + 1) * 128]
                acc = acc + nn(e.astype(BF), v_ref[0, at : at + rows, :])
            total = jnp.sum(total, axis=1, keepdims=True)
            outs.append(acc / total)
            lses.append(m + jnp.log(total))
        o = jnp.where(low, outs[0], outs[1])
        o_ref[0, qi * rows : (qi + 1) * rows, :] = o
        ol_ref[0, qi * rows : (qi + 1) * rows, :] = o.astype(BF)
        both = jnp.where(lanes((rows, 128)) == 0, lses[0], lses[1])
        lse_ref[0, :, qi * rows : (qi + 1) * rows] = both.T[0:8, :]


def mid_kernel(a_ref, w_ref, x_ref, g_ref, mid_ref, h_ref):
    mid = x_ref[...].astype(F32) + nn(a_ref[...], w_ref[...])
    mid_ref[...] = mid
    h_ref[...] = (mid * rms_scale(mid) * g_ref[...]).astype(BF)


def pre_kernel(nblk, rows, ix, og, p_ref, wd, dehid, ogx_t, ogx):
    cap = p_ref.shape[1]

    @pl.when(pl.program_id(0) == 0)
    def _():
        for b in range(nblk):
            block = og[ix[b], 0:rows, :]
            ogx[b * cap : (b + 1) * cap, :] = nn(p_ref[ix[b]], block).astype(BF)
        ogx_t[...] = ogx[...].T

    dehid[...] = nt(ogx[...], wd[...]).astype(BF)


def act(g, u, dh):
    s = 0.5 * jnp.tanh(0.5 * g) + 0.5
    silu = g * s
    hid = (silu * u).astype(BF)
    dg = (dh * u * (s + silu * (1.0 - s))).astype(BF)
    du = (dh * silu).astype(BF)
    return hid, dg, du


def expert_kernel(nblk, rows, experts, e_ref, ix, *refs):
    g_refs = refs[:nblk]
    (p_ref, pt_ref, wr, wr_t, wsg, wsu, wsd, og, wg, wu, dehid) = refs[nblk : nblk + 11]
    (x_out, g_out, ghid, degate, deup, shid, dsg, dsu, tg, tg_far, rgrad) = refs[nblk + 11 : nblk + 22]
    x_scr, row_scr, tg_scr, pg_scr, prob_scr, g_scr = refs[nblk + 22 :]
    cap = p_ref.shape[1]
    slots = nblk * cap
    step = pl.program_id(0)
    per = nblk // pl.num_programs(0)

    @pl.when(step == 0)
    def _():
        row_scr[...] = jnp.zeros_like(row_scr)
        pg_scr[...] = jnp.zeros_like(pg_scr)
        for b in range(nblk):
            block = g_refs[b][...]
            g_scr[b * rows : (b + 1) * rows, :] = block
            x_scr[b * cap : (b + 1) * cap, :] = nn(p_ref[ix[b]], block).astype(BF)
        logits = jnp.where(lanes((slots, 128)) < experts, nn(x_scr[...], wr[...]), NEG_LARGE)
        shifted = jnp.exp(logits - jnp.max(logits, axis=1, keepdims=True))
        prob_scr[...] = shifted / jnp.sum(shifted, axis=1, keepdims=True)

    own = lanes((slots, 128)) == e_ref[0]
    gate = jnp.sum(jnp.where(own, prob_scr[...], 0.0), axis=1, keepdims=True)
    raw = dehid[...].astype(F32)
    hid, dg, du = act(nn(x_scr[...], wg[0]), nn(x_scr[...], wu[0]), raw * gate)
    hid = hid.astype(F32)
    ghid[...] = (hid * gate).astype(BF)
    degate[...] = dg
    deup[...] = du
    row_scr[...] += nt(dg, wg[0]) + nt(du, wu[0])
    pg_scr[...] += jnp.sum(hid * raw, axis=1, keepdims=True)

    for k in range(per):
        b = step * per + k
        at = pl.multiple_of(b * rows, rows)
        block = g_scr[pl.ds(at, rows), :]
        g_out[k * rows : (k + 1) * rows, :] = block
        dsh = nt(og[ix[b], 0:rows, :], wsd[...])
        sh, sg, su = act(nn(block, wsg[...]), nn(block, wsu[...]), dsh)
        here = slice(k * rows, (k + 1) * rows)
        shid[here, :] = sh
        dsg[here, :] = sg
        dsu[here, :] = su
        tg_scr[pl.ds(at, rows), :] = nt(sg, wsg[...]) + nt(su, wsu[...])

    @pl.when(step == pl.num_programs(0) - 1)
    def _():
        x_out[...] = x_scr[...]
        lgrad = (pg_scr[:, 0:1] * prob_scr[...] * (own.astype(F32) - gate)).astype(BF)
        rgrad[...] = tn(lgrad, x_scr[...])
        total = (row_scr[...] + nn(lgrad, wr_t[...])).astype(BF)
        for b in range(nblk):
            back = nn(pt_ref[ix[b]], total[b * cap : (b + 1) * cap, :])
            (tg_far if b % 2 else tg)[b // 2] = (tg_scr[b * rows : (b + 1) * rows, :] + back).astype(BF)


def wgrad_kernel(per, r_ref, x_ref, degate, deup, gate_near, gate_far, up_near, up_far, x_t):
    step = pl.program_id(0)

    @pl.when(step == 0)
    def _():
        x_t[...] = x_ref[...].T

    @pl.when(step < 2 * per)
    def _():
        gate_near[0] = nn(x_t[...], degate[...]).astype(BF)
        up_near[0] = nn(x_t[...], deup[...]).astype(BF)

    @pl.when(step >= 2 * per)
    def _():
        gate_far[0] = nn(x_t[...], degate[...]).astype(BF)
        up_far[0] = nn(x_t[...], deup[...]).astype(BF)


def wgrad_all_kernel(r_ref, x_ref, degate, deup, gate, up, x_t):
    @pl.when(pl.program_id(0) == 0)
    def _():
        x_t[...] = x_ref[...].T

    gate[0] = nn(x_t[...], degate[...]).astype(BF)
    up[0] = nn(x_t[...], deup[...]).astype(BF)


def down_grad_kernel(ogx_t, ghid, dn):
    dn[...] = nn(ogx_t[...], ghid[...]).astype(BF)


def result_kernel(nblk, rows, ix_s, g_ref, og, pt_ref, shid, dsg, dsu, wsd, ghid, wd, mix, sgu, sd, acc, part, sg_acc, sd_acc):
    cap = pt_ref.shape[2]
    step = pl.program_id(0)
    per = nblk // pl.num_programs(0)
    width = dsg.shape[1]

    @pl.when(step == 0)
    def _():
        acc[...] = jnp.zeros_like(acc)
        sg_acc[...] = jnp.zeros_like(sg_acc)
        sd_acc[...] = jnp.zeros_like(sd_acc)

    acc[...] += nn(ghid[...], wd[0])
    sg_acc[:, :width] += tn(g_ref[...], dsg[...])
    sg_acc[:, width:] += tn(g_ref[...], dsu[...])
    for k in range(per):
        b = step * per + k
        here = slice(k * rows, (k + 1) * rows)
        sd_acc[...] += tn(shid[here, :], og[ix_s[b], 0:rows, :])
        part[pl.ds(pl.multiple_of(b * rows, rows), rows), :] = nn(shid[here, :], wsd[...])

    @pl.when(step == pl.num_programs(0) - 1)
    def _():
        sgu[...] = sg_acc[...].astype(BF)
        sd[...] = sd_acc[...].astype(BF)
        res = acc[...].astype(BF)
        for b in range(nblk):
            picked = nn(pt_ref[ix_s[b]], res[b * cap : (b + 1) * cap, :])
            mix[ix_s[b]] = (picked + part[b * rows : (b + 1) * rows, :]).astype(BF)


def mid_back_kernel(count, *refs):
    pieces = refs[:count]
    mid_ref, g_ref, og_ref, w_ref, mg_ref, ag_ref, da_ref, gg_ref = refs[count:]
    two = pieces[0][...].astype(F32)
    for piece in pieces[1:]:
        two += piece[...].astype(F32)
    mid = mid_ref[...]
    scale = rms_scale(mid)
    mn = mid * scale
    gg_ref[...] = jnp.broadcast_to(jnp.sum(two * mn, axis=0, keepdims=True), gg_ref.shape)
    dn = two * g_ref[...]
    mg = og_ref[...].astype(F32) + scale * (dn - mn * jnp.mean(dn * mn, axis=1, keepdims=True))
    mg_ref[...] = mg
    ag = mg.astype(BF)
    ag_ref[...] = ag
    da = nt(ag, w_ref[...]).astype(BF)
    for i in range(da_ref.shape[0]):
        da_ref[i] = da[:, 128 * i : 128 * i + 128]


def attend_back_kernel(first, count, rows, q_ref, k_ref, v_ref, o_ref, do_ref, lse_ref, sq_ref, sk_ref, cos, sin,
                       h1_ref, wq, wk, wv, gain, c_ref, grads, og_own, og_far, gg, h1_t, k_t, dk, dv, og_scr):
    step = pl.program_id(0)
    low = lanes((rows, 128)) < 64
    kv_rows = k_ref.shape[1]
    base = kv_rows - 2 * rows

    @pl.when(step == 0)
    def _():
        h1_t[...] = h1_ref[...].T
        og_scr[...] = jnp.zeros_like(og_scr)

    k_t[...] = k_ref[0].T
    dk[...] = jnp.zeros_like(dk)
    dv[...] = jnp.zeros_like(dv)
    dqs = []
    for qi in range(2):
        at_q = qi * rows
        qpair = q_ref[0, at_q : at_q + rows, :]
        dopair = do_ref[0, at_q : at_q + rows, :]
        prod = dopair.astype(F32) * o_ref[0, at_q : at_q + rows, :]
        d0 = jnp.sum(jnp.where(low, prod, 0.0), axis=1, keepdims=True)
        d1 = jnp.sum(jnp.where(low, 0.0, prod), axis=1, keepdims=True)
        delta = jnp.where(lanes((rows, 128)) == 0, d0, d1).T
        sq = sq_ref[0:1, at_q : at_q + rows]
        def masked(x):
            zero = jnp.zeros_like(x)
            return jnp.concatenate([jnp.where(low, x, zero), jnp.where(low, zero, x)], axis=0)

        q, do = masked(qpair), masked(dopair)
        lse_row = jnp.concatenate([lse_ref[0, h : h + 1, at_q : at_q + rows] for h in range(2)], axis=1)
        delta_row = jnp.concatenate([delta[h : h + 1, :] for h in range(2)], axis=1)
        sq = jnp.concatenate([sq, sq], axis=1)
        halves = [jnp.zeros((64, rows), F32) for _ in range(2)]
        for j in range(count):
            at = (first + qi + j) * rows
            same = sk_ref[at : at + rows, 0:1] == sq
            s = nt(k_ref[0, at : at + rows, :], q)
            p = jnp.where(same, jnp.exp(s - lse_row), 0.0)
            dp = nt(v_ref[0, at : at + rows, :], do)
            ds = (p * (dp - delta_row)).astype(BF)
            dv[at : at + rows, :] += nn(p.astype(BF), do)
            dk[at : at + rows, :] += nn(ds, q)
            for h in range(2):
                halves[h] += nn(k_t[64 * h : 64 * h + 64, at : at + rows], ds[:, h * rows : (h + 1) * rows])
        dq = jnp.concatenate(halves, axis=0).T * 0.125
        at = base + at_q
        dq = dq * cos[at : at + rows, :] - turned(dq) * sin[at : at + rows, :]
        dqs.append(dq.astype(BF))
    dq = jnp.concatenate(dqs, axis=0)
    dkv = dk[...]
    dkb = (dkv * cos[...] - turned(dkv) * sin[...]).astype(BF)
    dvb = dv[...].astype(BF)
    grads[0, 0] = nn(h1_t[:, base:], dq).astype(BF)
    grads[0, 1] = nn(h1_t[...], dkb).astype(BF)
    grads[0, 2] = nn(h1_t[...], dvb).astype(BF)
    og_scr[...] += nt(dkb, wk[...]) + nt(dvb, wv[...])
    og_scr[base:, :] += nt(dq, wq[...])

    @pl.when(step == pl.num_programs(0) - 1)
    def _():
        one = og_scr[...]
        for slot in range(kv_rows // rows):
            block = one[slot * rows : (slot + 1) * rows, :].astype(BF)

            @pl.when(c_ref[0] == slot % 2)
            def _():
                og_own[slot // 2] = block

            @pl.when(c_ref[0] != slot % 2)
            def _():
                og_far[slot // 2] = block

        total = jnp.sum(one * h1_ref[...].astype(F32), axis=0, keepdims=True) / gain[...]
        gg[...] = jnp.broadcast_to(total, gg.shape)


def last_kernel(count, *refs):
    pieces = refs[:count]
    x_ref, g_ref, mg_ref, out = refs[count:]
    one = pieces[0][...].astype(F32)
    for piece in pieces[1:]:
        one += piece[...].astype(F32)
    x = x_ref[...].astype(F32)
    scale = rms_scale(x)
    xn = x * scale
    dn = one * g_ref[...]
    out[...] = mg_ref[...] + scale * (dn - xn * jnp.mean(dn * xn, axis=1, keepdims=True))


def shape(dims, dtype=BF):
    return jax.ShapeDtypeStruct(dims, dtype)


def shards(
    R,
    E,
    tokens,
    segment_ids,
    routes,
    norm1_gain,
    w_query,
    w_key,
    w_value,
    w_out,
    norm2_gain,
    w_router,
    shared_gate,
    shared_up,
    shared_down,
    expert_gate,
    expert_up,
    expert_down,
    out_grad,
):
    Z = E // 2
    T, D = tokens.shape
    FF = shared_gate.shape[1]
    topk = routes.shape[1]
    experts = w_router.shape[1]
    assert expert_gate.shape[0] == 1 and experts == E
    half = D // 2
    pairs = half // 128
    wrow = w_query.shape[0]
    hrow = 2 * wrow
    cap = 2 * T * topk // experts
    slots = E * cap
    fs = FF // E
    drow = shared_down.shape[0]
    longest = E * T // 2
    back = -(-(longest - 1) // T)
    nb = -(-back // 2)
    chips = nb + 1
    kvb = 2 * chips
    first = 2 * nb - back
    count = back + 1
    r = lax.axis_index("rep")
    e = lax.axis_index("ep")
    z, c = e // 2, e % 2
    is0 = c == 0
    c_arr = jnp.reshape(c, (1,)).astype(jnp.int32)
    e_arr = jnp.reshape(e, (1,)).astype(jnp.int32)

    def swap(x):
        return lax.ppermute(x, "ep", [(i, i ^ 1) for i in range(E)])

    def ring(x, s):
        return lax.ppermute(x, "ep", [(i, (i + 2 * s) % E) for i in range(E)])

    def line(x, s):
        return lax.ppermute(x, "ep", [(i, i + 2 * s) for i in range(E) if 0 <= i + 2 * s < E])

    def cross(x, s):
        return lax.ppermute(x, "rep", [(i, i ^ s) for i in range(R)])

    def ordered(mine, other):
        return jnp.where(is0, mine, other), jnp.where(is0, other, mine)

    def put(buf, x, i):
        return lax.dynamic_update_index_in_dim(buf, x, i, 0)

    def chip_pack(mats, extra):
        stacked = jnp.stack(mats).reshape(len(mats) * wrow, D)
        mine, other = ordered(stacked[:, :half], stacked[:, half:])
        ext = jnp.pad(extra.reshape(1, -1), ((0, 0), (0, half - extra.size)))
        got = swap(jnp.concatenate([other, ext], axis=0))
        a, b = ordered(mine, got[:-1])
        ea, eb = ordered(ext, got[-1:])
        rows = jnp.stack([a.reshape(-1, wrow, half), b.reshape(-1, wrow, half)], axis=1).reshape(-1, half)
        rows = jnp.concatenate([rows, ea, eb], axis=0)
        return jnp.pad(rows, ((0, -rows.shape[0] % 16), (0, 0)))

    def gather_z(pack):
        buf = put(jnp.zeros((Z,) + pack.shape, BF), pack, z)
        for s in range(1, Z):
            buf = put(buf, ring(pack, s), (z - s) % Z)
        return buf

    def gather_rep(part, *deps):
        got = [cross(part, s) for s in range(1, R)]
        if deps:
            got = [after(x, *deps) for x in got]
        buf = put(jnp.zeros((R,) + part.shape, BF), part, r)
        for s in range(1, R):
            buf = put(buf, got[s - 1], r ^ s)
        return buf

    def unpack(full, i):
        return full[:, :, i * hrow : (i + 1) * hrow, :].reshape(D, half)

    pack = chip_pack(
        [w_query, w_key, w_value, w_out], jnp.concatenate([norm1_gain, norm2_gain, w_router.reshape(-1)])
    )
    part = gather_z(pack)
    full = gather_rep(part)
    wq, wk, wv, wo_half = (unpack(full, i) for i in range(4))
    ext = full[:, :, 4 * hrow : 4 * hrow + 2, :].reshape(R * E, half)
    gain1 = ext[:, :wrow].reshape(1, D).astype(F32)
    gain2 = ext[:, wrow : 2 * wrow].reshape(1, D).astype(F32)
    router = ext[:, 2 * wrow : (2 + experts) * wrow].reshape(D, experts)
    router = jnp.pad(router, ((0, 0), (0, 128 - experts)))
    router_t = router.T

    seg_row = jnp.pad(segment_ids.reshape(1, T).astype(BF), ((0, 7), (0, D - T)))
    tok_pack = after(jnp.concatenate([tokens, seg_row], axis=0), pack)
    own_tok = [tok_pack]
    for s in range(1, chips):
        own_tok.append(line(own_tok[-1], 1))
    par_tok = [swap(x) for x in own_tok]

    seg_blocks = [None] * kvb
    for s in range(chips):
        valid = z - s >= 0
        a, b = ordered(own_tok[s][T, :T], par_tok[s][T, :T])
        seg_blocks[2 * (nb - s)] = jnp.where(valid, a.astype(F32), -1.0)
        seg_blocks[2 * (nb - s) + 1] = jnp.where(valid, b.astype(F32), -1.0)
    segs = jnp.stack(seg_blocks)
    kv_rows = kvb * T
    seg_flat = segs.reshape(1, kv_rows)
    seg_wide = jnp.broadcast_to(segs.reshape(kv_rows, 1), (kv_rows, 128))

    inverse = jnp.exp(jnp.arange(32).astype(F32) * (-2.0 * math.log(10000.0) / 64))
    inverse = jnp.tile(inverse, 4)
    places = after((z - nb) * (2 * T) + jnp.arange(kv_rows, dtype=jnp.int32), pack)
    angle = places.astype(F32)[:, None] * inverse[None, :]
    cos, sin = lax.optimization_barrier((jnp.cos(angle), jnp.sin(angle)))
    cos, sin = cos.reshape(kvb, T, 128), sin.reshape(kvb, T, 128)

    h1, keys, vals, quer = pl.pallas_call(
        functools.partial(qkv_kernel, chips, T),
        in_specs=[pl.BlockSpec(memory_space=pltpu.SMEM)] + vmem(2 * chips + 6),
        out_specs=tuple(vmem(4)),
        out_shape=(
            shape((kvb, T, D)),
            shape((pairs, kvb, T, 128)),
            shape((pairs, kvb, T, 128)),
            shape((pairs, 2, T, 128)),
        ),
        compiler_params=params(),
        name="qkv",
        cost_estimate=cost(8),
    )(c_arr, *own_tok, *par_tok, wq, wk, wv, cos, sin, gain1)
    h1 = h1.reshape(kv_rows, D)
    keys = keys.reshape(pairs, kv_rows, 128)
    vals = vals.reshape(pairs, kv_rows, 128)
    quer = quer.reshape(pairs, 2 * T, 128)

    og_pack = jnp.concatenate(
        [out_grad, jnp.pad(routes.reshape(1, topk * T).astype(BF), ((0, 7), (0, D - topk * T)))], axis=0
    )
    og_all = lax.all_gather(after(og_pack, own_tok[-1]), "ep", axis=0)
    ix_arr = jnp.stack([((z - b // 2) % Z) * 2 + (c ^ (b % 2)) for b in range(E)]).astype(jnp.int32)

    wo = jnp.concatenate(ordered(wo_half, swap(wo_half)), axis=1)

    def by_unit(w):
        return w.reshape(wrow, R, E, drow).transpose(2, 0, 1, 3).reshape(E, wrow, fs)

    gu = jnp.concatenate([by_unit(shared_gate), by_unit(shared_up)], axis=2)
    gu = lax.all_to_all(after(gu, part), "ep", split_axis=0, concat_axis=0, tiled=True).reshape(E * wrow, 2 * fs)
    gu = after(gu, keys)
    wide = D // fs
    shared = jnp.concatenate(
        [gu[:, :fs], gu[:, fs:]] + [shared_down[:, k * fs : (k + 1) * fs] for k in range(wide)], axis=0
    )
    one = lambda *dims: pl.BlockSpec((1,) + dims, lambda i: (i, 0, 0))
    att, att_low, lse = pl.pallas_call(
        functools.partial(attend_kernel, first, count, T),
        grid=(pairs,),
        in_specs=[
            one(2 * T, 128),
            one(kv_rows, 128),
            one(kv_rows, 128),
            whole((2 * T, 128)),
            whole((1, kv_rows)),
        ],
        out_specs=(one(2 * T, 128), one(2 * T, 128), one(8, 2 * T)),
        out_shape=(
            shape((pairs, 2 * T, 128), F32),
            shape((pairs, 2 * T, 128)),
            shape((pairs, 8, 2 * T), F32),
        ),
        scratch_shapes=[pltpu.VMEM((T, count * T), F32)],
        compiler_params=params(),
        name="attend",
        cost_estimate=cost(10),
    )(after(quer, wo, shared), keys, vals, seg_wide[-2 * T :], seg_flat)

    def joined(mine, other):
        both = jnp.where(is0, jnp.concatenate([mine, other]), jnp.concatenate([other, mine]))
        return both.transpose(1, 0, 2).reshape(T, D)

    att_own, att_other = ordered(att_low[:, :T], att_low[:, T:])
    attended = joined(att_own, swap(att_other))
    mid, h2 = pl.pallas_call(
        mid_kernel,
        in_specs=vmem(4),
        out_specs=tuple(vmem(2)),
        out_shape=(shape((T, D), F32), shape((T, D))),
        compiler_params=params(),
        name="mid",
        cost_estimate=cost(3),
    )(attended, wo, tokens, gain2)

    h2_lane = [h2] + [None] * (Z - 1)
    h2_lane[1] = ring(h2, 1)
    for s in range(Z - 1, Z // 2, -1):
        h2_lane[s] = ring(h2 if s == Z - 1 else h2_lane[s + 1], -1)

    def both_cores(lane):
        blocks = []
        for item in lane:
            blocks += [item, swap(item)]
        return blocks

    og_all = after(og_all, h2)
    table = og_all[:, T, : topk * T].reshape(E, T, topk)
    hit = jnp.any(table == e.astype(F32).astype(BF), axis=2).astype(F32)
    rank = jnp.cumsum(hit, axis=1) - hit
    rank = jnp.where(hit > 0, rank, -1.0)
    slot_ids = jnp.arange(cap).astype(F32)
    pick = (rank[:, None, :] == slot_ids[None, :, None]).astype(BF)
    pick_t = (rank[:, :, None] == slot_ids[None, None, :]).astype(BF)

    smem = pl.BlockSpec(memory_space=pltpu.SMEM)
    ft = min(512, FF // R)
    steps = FF // ft
    per = FF // R // ft
    col = lambda n: pl.BlockSpec((n, ft), lambda i: (0, i))
    wcol = pl.BlockSpec((1, D, ft), lambda i: (0, 0, i))
    block_of = lambda n: pl.BlockSpec((E // steps * T, n), lambda i: (i, 0))
    wdn = pl.BlockSpec((1, ft, D), lambda i: (0, i, 0))
    dehid, ogx_t = pl.pallas_call(
        functools.partial(pre_kernel, E, T),
        grid=(steps,),
        in_specs=[smem, whole((E, T + 8, D))]
        + [whole((E, cap, T)), pl.BlockSpec((ft, D), lambda i: (i, 0))],
        out_specs=(col(slots), whole((D, slots))),
        out_shape=(shape((slots, FF)), shape((D, slots))),
        scratch_shapes=[pltpu.VMEM((slots, D), BF)],
        compiler_params=params(),
        name="pre",
        cost_estimate=cost(12),
    )(ix_arr, og_all, pick, expert_down.reshape(FF, D))

    shared_part = after(shared, pick)
    shared_got = [cross(shared_part, s) for s in range(1, R)]
    shared = put(jnp.zeros((R,) + shared.shape, BF), after(shared_part, dehid), r)
    for i in range(1, R):
        shared = put(shared, after(shared_got[i - 1], dehid), r ^ i)
    gr = E * wrow
    wsg = shared[:, :gr].reshape(D, fs)
    wsu = shared[:, gr : 2 * gr].reshape(D, fs)
    wsd = jnp.concatenate(
        [shared[:, 2 * gr + k * drow : 2 * gr + (k + 1) * drow].reshape(fs, fs) for k in range(wide)], axis=1
    )
    h2_lane[1] = after(h2_lane[1], dehid)
    for s in range(2, Z // 2 + 1):
        h2_lane[s] = ring(h2_lane[s - 1], 1)
    h2_blocks = both_cores([h2_lane[s] if 0 < s <= Z // 2 else after(h2_lane[s], dehid) for s in range(Z)])
    (x_rows, g_rows, ghid, degate, deup, shid, dsg, dsu, tg, tg_far, rgrad) = pl.pallas_call(
        functools.partial(expert_kernel, E, T, experts),
        grid=(steps,),
        in_specs=[smem, smem]
        + [whole((T, D))] * E
        + [
            whole((E, cap, T)),
            whole((E, T, cap)),
            whole((D, 128)),
            whole((128, D)),
            whole((D, fs)),
            whole((D, fs)),
            whole((fs, D)),
            whole((E, T + 8, D)),
            wcol,
            wcol,
            col(slots),
        ],
        out_specs=(
            whole((slots, D)),
            block_of(D),
            col(slots),
            col(slots),
            col(slots),
            block_of(fs),
            block_of(fs),
            block_of(fs),
            whole((Z, T, D)),
            whole((Z, T, D)),
            whole((128, D)),
        ),
        out_shape=(
            shape((slots, D)),
            shape((E * T, D)),
            shape((slots, FF)),
            shape((slots, FF)),
            shape((slots, FF)),
            shape((E * T, fs)),
            shape((E * T, fs)),
            shape((E * T, fs)),
            shape((Z, T, D)),
            shape((Z, T, D)),
            shape((128, D), F32),
        ),
        scratch_shapes=[
            pltpu.VMEM((slots, D), BF),
            pltpu.VMEM((slots, D), F32),
            pltpu.VMEM((E * T, D), F32),
            pltpu.VMEM((slots, 128), F32),
            pltpu.VMEM((slots, 128), F32),
            pltpu.VMEM((E * T, D), BF),
        ],
        compiler_params=params(),
        name="expert",
        cost_estimate=cost(38),
    )(e_arr, ix_arr, *h2_blocks, pick, pick_t, router, router_t, wsg, wsu, wsd, og_all, expert_gate, expert_up, dehid)

    def core_sums(mine, other, *deps):
        got = swap(other)
        if deps:
            got = after(got, *deps)
        return [mine[s] + got[s] for s in range(Z)]


    r_arr = jnp.reshape(r, (1,)).astype(jnp.int32)
    wide_rep = FF // R
    square = R == 4
    at0 = lambda n: pl.BlockSpec(n, lambda i, q: (0,) * len(n))
    dn_grad = pl.pallas_call(
        down_grad_kernel,
        grid=(steps,),
        in_specs=[whole((D, slots)), col(slots)],
        out_specs=col(D),
        out_shape=shape((D, FF)),
        compiler_params=params(),
        name="dgrad",
        cost_estimate=cost(10),
    )(ogx_t, ghid)
    dn_sum = lax.psum_scatter(dn_grad, "rep", scatter_dimension=0, tiled=True)
    lane = core_sums(tg, tg_far, dn_grad)
    two_parts = [lane[0]] + [ring(lane[s], -s) for s in range(1, Z)]

    if square:

        def rel_col(swapped):
            def index(i, q):
                d = i // per
                d = (d % 2) * 2 + d // 2 if swapped else d
                return (0, (d ^ q[0]) * per + i % per)

            return pl.BlockSpec((slots, ft), index)

        early = pl.BlockSpec(
            (1, D, ft),
            lambda i, q: (jnp.minimum(i // per, 1), 0, jnp.where(i < 2 * per, i % per, per - 1)),
        )
        late = pl.BlockSpec(
            (1, D, ft),
            lambda i, q: (jnp.maximum(i // per - 2, 0), 0, jnp.where(i < 2 * per, 0, i % per)),
        )
        gu_in = [rel_col(True), rel_col(False)]
        gu_specs = (early, late, early, late)
        gu_shapes = [(2, D, wide_rep)] * 4
        gu_kernel = functools.partial(wgrad_kernel, per)
    else:
        gu_in = [pl.BlockSpec((slots, ft), lambda i, q: (0, ((i // per) ^ q[0]) * per + i % per))] * 2
        gu_specs = (pl.BlockSpec((1, D, ft), lambda i, q: (i // per, 0, i % per)),) * 2
        gu_shapes = [(R, D, wide_rep)] * 2
        gu_kernel = wgrad_all_kernel
    gu_out = pl.pallas_call(
        gu_kernel,
        grid_spec=pltpu.PrefetchScalarGridSpec(
            num_scalar_prefetch=1,
            grid=(steps,),
            in_specs=[at0((slots, D))] + gu_in,
            out_specs=gu_specs,
            scratch_shapes=[pltpu.VMEM((D, slots), BF)],
        ),
        out_shape=tuple(shape(dims) for dims in gu_shapes),
        compiler_params=params(),
        name="wgrad",
        cost_estimate=cost(13),
    )(r_arr, after(x_rows, *lane), degate, deup)

    def pieces(x):
        return [lax.dynamic_index_in_dim(x, r ^ s, 0, keepdims=False) for s in range(R)]

    def direct(pieces, *deps):
        total = pieces[0].astype(F32)
        for d in range(1, R):
            got = cross(pieces[d], d)
            total += (after(got, *deps) if deps else got).astype(F32)
        return total

    two_parts[1] = after(two_parts[1], gu_out[0])
    near = []
    if square:
        gate_a, up_a = cross(gu_out[1][0], 1), cross(gu_out[3][0], 2)
    mix, sgu_grad, sd_grad = pl.pallas_call(
        functools.partial(result_kernel, E, T),
        grid=(steps,),
        in_specs=[
            smem,
            block_of(D),
            whole((E, T + 8, D)),
            whole((E, T, cap)),
            block_of(fs),
            block_of(fs),
            block_of(fs),
            whole((fs, D)),
            col(slots),
            wdn,
        ],
        out_specs=(whole((E, T, D)), whole((D, 2 * fs)), whole((fs, D))),
        out_shape=(shape((E, T, D)), shape((D, 2 * fs)), shape((fs, D))),
        scratch_shapes=[
            pltpu.VMEM((slots, D), F32),
            pltpu.VMEM((E * T, D), F32),
            pltpu.VMEM((D, 2 * fs), F32),
            pltpu.VMEM((fs, D), F32),
        ],
        compiler_params=params(),
        name="result",
        cost_estimate=cost(14),
    )(ix_arr, g_rows, og_all, pick_t, shid, dsg, dsu, wsd, after(ghid, gu_out[0], two_parts[1], *near), expert_down)

    sgrad = jnp.concatenate(
        [sgu_grad[:, :fs].reshape(R, gr, fs), sgu_grad[:, fs:].reshape(R, gr, fs)]
        + [sd_grad[:, k * fs : (k + 1) * fs].reshape(R, drow, fs) for k in range(wide)],
        axis=1,
    )
    two_parts[2:] = [after(x, mix) for x in two_parts[2:]]
    if square:
        gate_a, up_a = after(gate_a, mix), after(up_a, mix)
        two_parts[0], gate_a, up_a = lax.optimization_barrier((two_parts[0], gate_a, up_a))
        gate_c, up_c = cross(after(gu_out[1][1], mix), 1), cross(after(gu_out[3][1], mix), 2)

    mix_in = after(mix, two_parts[2], *((gate_a, up_a) if square else ()))
    mix_sum = lax.psum_scatter(mix_in.reshape(E * T, D), "ep", scatter_dimension=0, tiled=True)

    mid_grad, attn_grad, att_grad, gain2_part = pl.pallas_call(
        functools.partial(mid_back_kernel, Z),
        in_specs=vmem(Z + 4),
        out_specs=tuple(vmem(4)),
        out_shape=(shape((T, D), F32), shape((T, D)), shape((2 * pairs, T, 128)), shape((8, D), F32)),
        compiler_params=params(),
        name="mid_back",
        cost_estimate=cost(4),
    )(*two_parts, mid, gain2, out_grad, wo)

    ag_own, ag_other = ordered(att_grad[:pairs], att_grad[pairs:])
    do_a, do_b = ordered(ag_own, swap(ag_other))
    do = jnp.concatenate([do_a, do_b], axis=1)
    wo_part = tn(attended, after(attn_grad, ag_other)).astype(BF)
    wo_mine, wo_other = ordered(wo_part[:, :half], wo_part[:, half:])
    wo_got = swap(wo_other)
    if square:
        gate_mid = gu_out[0][1] + after(gate_c, do)
        up_mid = gu_out[2][1] + after(up_c, do)
        gate_b, up_b = cross(gate_mid, 2), cross(up_mid, 1)
        sg_own, sg_near, sg_a, sg_c = pieces(after(sgrad, do))
        sg_send = jnp.stack([sg_a, sg_c])
        sg_got = cross(sg_send, 2)
        do, gate_mid, up_mid, wo_other, sg_send = lax.optimization_barrier(
            (do, gate_mid, up_mid, wo_other, sg_send)
        )

    cos2, sin2 = cos.reshape(kv_rows, 128), sin.reshape(kv_rows, 128)
    grads, og1, og1_far, gain1_part = pl.pallas_call(
        functools.partial(attend_back_kernel, first, count, T),
        grid=(pairs,),
        in_specs=[
            one(2 * T, 128),
            one(kv_rows, 128),
            one(kv_rows, 128),
            one(2 * T, 128),
            one(2 * T, 128),
            one(8, 2 * T),
            whole((1, 2 * T)),
            whole((kv_rows, 128)),
            whole((kv_rows, 128)),
            whole((kv_rows, 128)),
            whole((kv_rows, D)),
            pl.BlockSpec((D, 128), lambda i: (0, i)),
            pl.BlockSpec((D, 128), lambda i: (0, i)),
            pl.BlockSpec((D, 128), lambda i: (0, i)),
            whole((1, D)),
            smem,
        ],
        out_specs=(
            pl.BlockSpec((1, 3, D, 128), lambda i: (i, 0, 0, 0)),
            whole((chips, T, D)),
            whole((chips, T, D)),
            whole((8, D)),
        ),
        out_shape=(shape((pairs, 3, D, 128)), shape((chips, T, D)), shape((chips, T, D)), shape((8, D), F32)),
        scratch_shapes=[
            pltpu.VMEM((D, kv_rows), BF),
            pltpu.VMEM((128, kv_rows), BF),
            pltpu.VMEM((kv_rows, 128), F32),
            pltpu.VMEM((kv_rows, 128), F32),
            pltpu.VMEM((kv_rows, D), F32),
        ],
        compiler_params=params(),
        name="attend_back",
        cost_estimate=cost(30),
    )(quer, keys, vals, att, do, lse, seg_flat[:, -2 * T :], seg_wide, cos2, sin2, h1, wq, wk, wv, gain1, c_arr)

    wo_got = after(wo_got, og1)
    if square:
        gate_b, up_b, sg_got = after(gate_b, og1), after(up_b, og1), after(sg_got, og1)
        og1_far, grads, gate_b, up_b, wo_got, sg_got = lax.optimization_barrier(
            (og1_far, grads, gate_b, up_b, wo_got, sg_got)
        )
    far_got = swap(og1_far)
    if square:
        sg_mid = cross(sg_near + sg_got[1], 1)
        sg_mid, far_got = lax.optimization_barrier((sg_mid, far_got))
    lane = og1 + far_got
    one_moved = lane[0]
    for i in range(1, nb):
        one_moved = lane[i] + line(one_moved, -1)
    one_parts = [lane[nb], line(one_moved, -1)]

    n_chip = R * Z

    def dense_pack(groups, ext):
        rows = groups.reshape(-1, n_chip, hrow, 128).transpose(1, 0, 2, 3).reshape(n_chip, -1, 128)
        ext = ext.astype(BF)
        ext = jnp.pad(ext, ((0, 0), (0, -ext.shape[1] % 128))).reshape(n_chip, -1, 128)
        rows = jnp.concatenate([rows, ext], axis=1)
        return jnp.pad(rows, ((0, 0), (0, -rows.shape[1] % 8), (0, 0))).reshape(R, Z, -1, 128)

    wo_lane = wo_mine + wo_got
    wo_groups = wo_lane.reshape(D, pairs, 128).transpose(1, 0, 2)
    ext = jnp.concatenate(
        [
            gain1_part[0].reshape(n_chip, hrow),
            gain2_part[0].reshape(n_chip, hrow),
            rgrad[:experts].reshape(experts, n_chip, hrow).transpose(1, 0, 2).reshape(n_chip, experts * hrow),
        ],
        axis=1,
    )

    groups = 4 * pairs
    pack_d = dense_pack(jnp.concatenate([grads.reshape(-1, D, 128), wo_groups]), ext)
    send_d = pieces(pack_d)
    got_d = [after(cross(send_d[s], s), *one_parts[1:]) for s in range(1, R)]
    total_d = send_d[0].astype(F32)
    for x in got_d:
        total_d += x.astype(F32)
    total_d = total_d.astype(BF)
    if square:
        sgrad = sg_own.astype(F32) + sg_got[0].astype(F32) + sg_mid.astype(F32)
    else:
        sgrad = lax.psum_scatter(sgrad.reshape(-1, fs), "rep", scatter_dimension=0, tiled=True).astype(F32)
    sd_sum = jnp.concatenate(
        [sgrad[2 * gr + k * drow : 2 * gr + (k + 1) * drow] for k in range(wide)], axis=1
    )
    sgu = jnp.concatenate([sgrad[:gr], sgrad[gr : 2 * gr]], axis=1).astype(BF)
    sgu = sgu.reshape(Z, hrow, -1, 128).transpose(0, 2, 1, 3).reshape(Z, -1, 128)
    rows_d = total_d.shape[1]
    to_z = jnp.concatenate([total_d, sgu], axis=1)
    z_own = lax.dynamic_index_in_dim(to_z, z, 0, keepdims=False)
    z_got = [ring(lax.dynamic_index_in_dim(to_z, (z + s) % Z, 0, keepdims=False), s) for s in range(1, Z)]

    if square:
        gate_sum = gu_out[0][0].astype(F32) + (gate_a.astype(F32) + after(gate_b, lane).astype(F32))
        up_sum = gu_out[2][0].astype(F32) + (up_a.astype(F32) + after(up_b, lane).astype(F32))
    else:
        gate_sum, up_sum = (direct(x, lane) for x in gu_out)
    dn_sum = after(dn_sum, lane).T.astype(F32)
    layer_out = (mid + after(mix_sum, lane).astype(F32)).astype(BF)
    done = [gate_sum, up_sum, dn_sum, layer_out, sd_sum, to_z]
    one_parts[0], *done = lax.optimization_barrier((one_parts[0], *done))
    gate_sum, up_sum, dn_sum, layer_out, sd_sum, to_z = done
    tokens_grad = pl.pallas_call(
        functools.partial(last_kernel, 2),
        in_specs=vmem(5),
        out_specs=vmem(1)[0],
        out_shape=shape((T, D), F32),
        compiler_params=params(),
        name="last",
        cost_estimate=cost(3),
    )(*one_parts, tokens, gain1, mid_grad)

    z_got = [after(x, tokens_grad) for x in z_got]
    total = z_own[:rows_d].astype(F32)
    for x in z_got:
        total += x[:rows_d].astype(F32)
    sg_from = put(jnp.zeros((Z,) + sgu.shape[1:], BF), z_own[rows_d:], z)
    for s in range(1, Z):
        sg_from = put(sg_from, z_got[s - 1][rows_d:], (z - s) % Z)
    sg_groups = Z * (2 * fs // 128)
    mats_all, ext_all = total[: groups * hrow], total[groups * hrow :]
    rows_all = jnp.concatenate([mats_all, sg_from.reshape(-1, 128).astype(F32)])
    rows_all = rows_all.reshape(groups + sg_groups, 2, wrow, 128)
    mine, other = ordered(rows_all[:, 0], rows_all[:, 1])
    got = swap(jnp.concatenate([other.reshape(-1, 128), ext_all], axis=0).astype(BF)).astype(F32)
    count_rows = (groups + sg_groups) * wrow
    left, right = ordered(mine, got[:count_rows].reshape(-1, wrow, 128))
    ext_all = ext_all + got[count_rows:]
    ext_all = ext_all.reshape(-1)[: (2 + experts) * hrow].reshape(2 + experts, 2, wrow)
    ext_all = jnp.where(is0, ext_all[:, 0], ext_all[:, 1])

    def joined_mat(indices):
        return jnp.concatenate([left[i] for i in indices] + [right[i] for i in indices], axis=1)

    mats = [joined_mat([3 * p + m for p in range(pairs)]) for m in range(3)]
    mats.append(joined_mat([3 * pairs + p for p in range(pairs)]))

    sg = jnp.stack([left[groups:].reshape(Z, -1, wrow, 128), right[groups:].reshape(Z, -1, wrow, 128)], axis=1)
    sg = sg.reshape(E, 2, fs // 128, wrow, 128)

    def units_back(x):
        x = x.transpose(0, 2, 1, 3).reshape(E, wrow, R, drow)
        return x.transpose(1, 2, 0, 3).reshape(wrow, FF)

    sg_sum, su_sum = units_back(sg[:, 0]), units_back(sg[:, 1])

    return (
        layer_out,
        tokens_grad,
        ext_all[0],
        mats[0],
        mats[1],
        mats[2],
        mats[3],
        ext_all[1],
        ext_all[2:].T,
        sg_sum,
        su_sum,
        sd_sum,
        gate_sum[None],
        up_sum[None],
        dn_sum[None],
    )


def solution(mesh):
    rows = P(("rep", "ep"), None)
    flat = P(("rep", "ep"))
    expert = P("ep", None, None)
    expert_out = P("ep", None, "rep")
    return jax.shard_map(
        functools.partial(shards, mesh.shape["rep"], mesh.shape["ep"]),
        mesh=mesh,
        in_specs=(rows, P("rep", "ep"), rows, flat, rows, rows, rows, rows, flat)
        + (rows,) * 4
        + (expert,) * 3
        + (rows,),
        out_specs=(rows, rows, flat, rows, rows, rows, rows, flat)
        + (rows,) * 4
        + (expert_out,) * 3,
        check_vma=False,
    )
```
